512 devices in a mesh: gx: 16 (over z, core), gy: 32 (over y, x).
Axes of the slice: x: 4, y: 8, z: 8, core: 2. Of those that a mesh axis runs over, the one named last changes fastest.
Arguments:
- unary_score: bfloat16 [64, 256, 512], P('gx', 'gy'), may hold values from -12 to 400
- affinity: bfloat16 [64, 256, 1664], P('gx', 'gy'), may hold values from 0.099609375 to 1
- compatibility: float32 [8, 8], replicated, may hold values from -3 to 3
- kernel: float32 [26], replicated, may hold values from 0.05 to 0.4
- cotangent: bfloat16 [64, 256, 512], P('gx', 'gy'), may hold values from -8 to 8
Outputs:
- grad_unary: bfloat16 [64, 256, 512], P('gx', 'gy')
- grad_affinity: bfloat16 [64, 256, 1664], P('gx', 'gy')
- grad_compat: float32 [8, 8], replicated
- grad_kernel: float32 [26], replicated
The draws below stay inside these ranges and needn't reach their ends.
All inputs are finite; a program needn't handle non-finite values.
Results may differ from the reference program's by a relative error of at most 0.0045.
Values may be sent and summed in bfloat16 or wider, within the bound.
A program may use at most 128 MiB of HBM per device.

```python
import math
import jax
import jax.numpy as jnp
from jax import lax

LABELS = 8
DEPTH = 64
NEIGH = 26
ITERS = 3
NX = 64
NY = 256
VOXELS = 1048576


def draw_unary_score(key, part):
    key = jax.random.fold_in(key, 11)
    streams = jax.random.split(key, 1)
    grid_shape = (NX, NY, LABELS, DEPTH)
    values = jnp.clip(2.0 * jax.random.normal(streams[0], grid_shape, jnp.float32), -12.0, 12.0)
    return values.reshape(NX, NY, LABELS * DEPTH).astype(jnp.bfloat16)


def draw_cotangent(key, part):
    key = jax.random.fold_in(key, 23)
    streams = jax.random.split(key, 1)
    ramp_x = 1.0 + 2.0 * jnp.arange(NX, dtype=jnp.float32) / (NX - 1)
    ramp_y = 1.0 + 2.0 * jnp.arange(NY, dtype=jnp.float32) / (NY - 1)
    ramp = ramp_x[:, None, None] * ramp_y[None, :, None]
    grid_shape = (NX, NY, LABELS * DEPTH)
    values = jax.random.normal(streams[0], grid_shape, jnp.float32) * ramp * 0.4
    return jnp.clip(values, -8.0, 8.0).astype(jnp.bfloat16)


def block_levels(stream_key, shape, cuts, low, high):
    level, own = 1.0, jax.random.fold_in(stream_key, 6)
    for position, shards_of in cuts:
        draws = jnp.exp(jax.random.uniform(jax.random.fold_in(own, position), (shards_of,), jnp.float32, low / len(cuts), high / len(cuts)))
        level = level * jnp.repeat(draws, shape[position] // shards_of).reshape([-1 if axis == position else 1 for axis in range(len(shape))])
    return level


def centred(rng, dims, scale, limit, kind=jnp.bfloat16):
    entries = jax.random.normal(rng, dims, jnp.float32) * scale
    return jnp.minimum(jnp.maximum(entries, -limit), limit).astype(kind)


def setup_inputs(seed: int = 0) -> dict:
    keys = jax.random.split(jax.random.key(seed), 6)
    return {
        "unary_score": draw_unary_score(jax.random.fold_in(keys[5], 71), 0),
        "affinity": jnp.clip(jnp.exp(math.log(1.0) - 2.306499 * jax.random.uniform(keys[1], (NX, NY, NEIGH * DEPTH), jnp.float32) ** block_levels(keys[1], (NX, NY, NEIGH * DEPTH), ((0, 16), (1, 32)), -0.2, 0.2)), 0.099609375, 1.0).astype(jnp.bfloat16),
        "compatibility": centred(keys[2], (LABELS, LABELS), 0.5, 3.0, jnp.float32),
        "kernel": jnp.clip(jnp.exp(jax.random.uniform(keys[3], (NEIGH,), jnp.float32, math.log(0.05), math.log(0.4))), 0.05, 0.4),
        "cotangent": draw_cotangent(jax.random.fold_in(keys[5], 71), 0),
    }


OFFSETS = [(step_x, step_y, step_z) for step_x in (-1, 0, 1) for step_y in (-1, 0, 1) for step_z in (-1, 0, 1) if (step_x, step_y, step_z) != (0, 0, 0)]

def neighbour(values, step_x, step_y, step_z):
    padded = jnp.pad(values, ((1, 1), (1, 1), (0, 0), (1, 1)))
    size_x = values.shape[0]
    size_y = values.shape[1]
    size_z = values.shape[3]
    return padded[1 + step_x:1 + step_x + size_x, 1 + step_y:1 + step_y + size_y, :, 1 + step_z:1 + step_z + size_z]

def normalise(logits):
    highest = lax.optimization_barrier(jnp.max(logits, axis=2, keepdims=True))
    powers = jnp.exp(logits - highest)
    return powers / lax.optimization_barrier(jnp.sum(powers, axis=2, keepdims=True))

def softmax_back(current, grad_in):
    return current * (grad_in - lax.optimization_barrier(jnp.sum(current * grad_in, axis=2, keepdims=True)))

def message(marginal, weights, kernel):
    summed = jnp.zeros(marginal.shape, jnp.float32)
    for number, offset in enumerate(OFFSETS):
        coupling = kernel[number] * weights[:, :, number, :]
        summed = summed + coupling[:, :, None, :] * neighbour(marginal, *offset)
    return summed

def reference(unary_score, affinity, compatibility, kernel, cotangent):
    logits = unary_score.astype(jnp.float32).reshape(NX, NY, LABELS, DEPTH)
    weights = affinity.astype(jnp.float32).reshape(NX, NY, NEIGH, DEPTH)
    marginals = [normalise(logits)]
    messages = []
    for iteration in range(ITERS):
        coupled = message(marginals[-1], weights, kernel)
        pairwise = jnp.einsum('ab,xybz->xyaz', compatibility, coupled, precision=lax.Precision.HIGHEST)
        marginals.append(normalise(logits - pairwise))
        messages.append(coupled)
    grad_q = cotangent.astype(jnp.float32).reshape(NX, NY, LABELS, DEPTH)
    grad_u = jnp.zeros(logits.shape, jnp.float32)
    grad_c = jnp.zeros((LABELS, LABELS), jnp.float32)
    grad_k = [jnp.zeros((), jnp.float32) for number in range(NEIGH)]
    grad_w = [jnp.zeros((NX, NY, DEPTH), jnp.float32) for number in range(NEIGH)]
    for iteration in reversed(range(ITERS)):
        current = marginals[iteration + 1]
        prior = marginals[iteration]
        coupled = messages[iteration]
        grad_s = softmax_back(current, grad_q)
        grad_u = grad_u + grad_s
        grad_p = -grad_s
        grad_c = grad_c + jnp.einsum('xyaz,xybz->ab', grad_p, coupled, precision=lax.Precision.HIGHEST)
        grad_m = jnp.einsum('ab,xyaz->xybz', compatibility, grad_p, precision=lax.Precision.HIGHEST)
        back = jnp.zeros(grad_m.shape, jnp.float32)
        for number, (step_x, step_y, step_z) in enumerate(OFFSETS):
            joint = lax.optimization_barrier(jnp.sum(grad_m * neighbour(prior, step_x, step_y, step_z), axis=2))
            grad_w[number] = grad_w[number] + kernel[number] * joint
            grad_k[number] = grad_k[number] + jnp.sum(joint * weights[:, :, number, :])
            coupling = kernel[number] * weights[:, :, number, :]
            back = back + neighbour(coupling[:, :, None, :] * grad_m, -step_x, -step_y, -step_z)
        grad_q = back
    grad_u = grad_u + softmax_back(marginals[0], grad_q)
    scale = 1.0 / math.sqrt(VOXELS)
    grad_unary = grad_u.reshape(NX, NY, LABELS * DEPTH).astype(jnp.bfloat16)
    grad_affinity = jnp.stack(grad_w, axis=2).reshape(NX, NY, NEIGH * DEPTH).astype(jnp.bfloat16)
    return (grad_unary, grad_affinity, grad_c * scale, jnp.stack(grad_k) * scale)
```

```python
import functools
import math

import jax
import jax.numpy as jnp
from jax import lax
from jax.experimental import pallas as pl
from jax.experimental.pallas import tpu as pltpu
from jax.sharding import PartitionSpec as P

LABELS = 8
DEPTH = 64
NEIGH = 26
ITERS = 3

OFFSETS = [
    (step_x, step_y, step_z)
    for step_x in (-1, 0, 1)
    for step_y in (-1, 0, 1)
    for step_z in (-1, 0, 1)
    if (step_x, step_y, step_z) != (0, 0, 0)
]
NUMBER = {offset: number for number, offset in enumerate(OFFSETS)}

SPAN = 12
TALL = 24
BASE = 8
DIRECTIONS = [(-1, 0), (1, 0), (0, -1), (0, 1), (-1, -1), (-1, 1), (1, -1), (1, 1)]
WIDE = 32
MESH = pl.DeviceIdType.MESH


def low_half():
    return lax.broadcasted_iota(jnp.int32, (8, 128), 1) < DEPTH


def swap(values):
    return pltpu.roll(values, DEPTH, values.ndim - 1)


def inner_rows(y, p, label, width):
    return pl.ds(((y + 2) * 2 + p) * width + label, 8, stride=2 * width)


def side_rows(y, label, width):
    return pl.ds((y + 2) * width + label, 8, stride=width)


def spread(source, tiles, put):
    low = low_half()
    for tile in range(tiles):
        cols = [
            source[x, :, 128 * tile : 128 * (tile + 1)].astype(jnp.float32) for x in range(4)
        ]
        turned = [swap(col) for col in cols]
        for p in (0, 1):
            put(2 * tile, p, jnp.where(low, cols[p], turned[p + 2]))
            put(2 * tile + 1, p, jnp.where(low, turned[p], cols[p + 2]))


def gather_columns(values, tiles, put):
    low = low_half()
    for tile in range(tiles):
        for p in (0, 1):
            even, odd = values(2 * tile, p), values(2 * tile + 1, p)
            put(tile, p, jnp.where(low, even, swap(odd)))
            put(tile, p + 2, jnp.where(low, swap(even), odd))


def lay_out(inner, sides, width, label, first, second):
    low = low_half()
    inner[inner_rows(0, 0, label, width), :] = first
    inner[inner_rows(0, 1, label, width), :] = second
    sides[pl.ds(label, 8, stride=width), :] = jnp.where(low, first, swap(second))
    sides[pl.ds(8 * width + label, 8, stride=width), :] = jnp.where(low, swap(first), second)


def assemble(inner, minus, plus, width, label, y, reach):
    low = low_half()
    own = [inner[inner_rows(y, p, label, width), :] for p in (0, 1)]
    before = minus[side_rows(y, label, width), :]
    after = plus[side_rows(y, label, width), :]
    found = {0: own[0], 1: own[1]}
    found[2] = swap(jnp.where(low, after, own[0]))
    found[-1] = swap(jnp.where(low, own[1], before))
    if reach == 2:
        found[3] = jnp.where(low, swap(own[1]), after)
        found[-2] = jnp.where(low, before, swap(own[0]))
    return found


def message(weight, field, columns, y):
    sums = {p: None for p in columns}
    for step_y in (-1, 0, 1):
        for step_z in (-1, 0, 1):
            for source in range(min(columns) - 1, max(columns) + 2):
                users = [
                    (source - step_x, NUMBER[(step_x, step_y, step_z)])
                    for step_x in (-1, 0, 1)
                    if source - step_x in sums and (step_x, step_y, step_z) in NUMBER
                ]
                if not users:
                    continue
                near = field[step_z + 1, :, source + 2, pl.ds(BASE + y + step_y, 8), :]
                for p, number in users:
                    term = weight(number, p)[None] * near
                    sums[p] = term if sums[p] is None else sums[p] + term
    return sums


def mix(coef, values):
    rows = []
    for a in range(LABELS):
        total = coef(a, 0) * values[0]
        for b in range(1, LABELS):
            total = total + coef(a, b) * values[b]
        rows.append(total)
    return jnp.stack(rows)


def normalise(logits):
    powers = jnp.exp(logits - jnp.max(logits, axis=0, keepdims=True))
    return powers / jnp.sum(powers, axis=0, keepdims=True)


def softmax_back(current, grad_in):
    return current * (grad_in - jnp.sum(current * grad_in, axis=0, keepdims=True))


def put_field(field, label, p, y, value):
    axis = value.ndim - 1
    field[1, label, p + 2, pl.ds(BASE + y, 8), :] = value
    field[0, label, p + 2, pl.ds(BASE + y, 8), :] = pltpu.roll(value, 1, axis)
    field[2, label, p + 2, pl.ds(BASE + y, 8), :] = pltpu.roll(value, 127, axis)


def kernel(
    sizes,
    unary_hbm,
    affinity_hbm,
    cotangent_hbm,
    compat,
    strength,
    grad_unary_hbm,
    grad_affinity_hbm,
    grad_compat,
    grad_kernel,
    unary_in,
    affinity_in,
    cotangent_in,
    unary_out,
    affinity_out,
    inner_u,
    sides_u,
    minus_u,
    plus_u,
    inner_a,
    sides_a,
    minus_a,
    plus_a,
    inner_send,
    sides_send,
    inner_recv,
    minus_recv,
    plus_recv,
    inner_q,
    sides_q,
    minus_q,
    plus_q,
    inner_g,
    sides_g,
    minus_g,
    plus_g,
    inner_h,
    sides_h,
    minus_h,
    plus_h,
    logits,
    own_grad,
    field_0,
    field_1,
    field_2,
    field_g,
    field_h,
    field_i,
    wide_aff,
    weight_own,
    weight_rim,
    weight_back,
    message_1,
    message_2,
    rim_p,
    total_u,
    total_c,
    total_r,
    gather_a,
    gather_b,
    gather_c,
    load_sem,
    store_sem,
    halo_send,
    halo_recv,
    peer_send,
    peer_recv,
):
    size_gx, size_gy, size_far, size_near = sizes
    me_x, me_y = lax.axis_index("gx"), lax.axis_index("gy")
    me_far, me_near = me_y // size_near, lax.rem(me_y, size_near)
    low = low_half()

    def around(index, step, size):
        return lax.rem(index + (step + size), size)

    loads = [
        pltpu.make_async_copy(unary_hbm, unary_in, load_sem.at[0]),
        pltpu.make_async_copy(affinity_hbm, affinity_in, load_sem.at[1]),
        pltpu.make_async_copy(cotangent_hbm, cotangent_in, load_sem.at[2]),
    ]
    for load in loads:
        load.start()

    neighbours = [
        (around(me_x, step_x, size_gx), around(me_y, step_y, size_gy))
        for step_x, step_y in DIRECTIONS
    ]
    peers_a = [(around(me_x, step, size_gx), me_y) for step in range(1, size_gx)]
    peers_b = [
        (me_x, around(me_far, step, size_far) * size_near + me_near)
        for step in range(1, size_far)
    ]
    peers_c = [
        (me_x, me_far * size_near + around(me_near, step, size_near))
        for step in range(1, size_near)
    ]
    everyone = neighbours + peers_a + peers_b + peers_c
    barrier = pltpu.get_barrier_semaphore()
    for device in everyone:
        pl.semaphore_signal(barrier, inc=1, device_id=device, device_id_type=MESH)

    def exchange(number, width, reach, inner, sides, minus, plus):
        copies = []
        for d, (step_x, step_y) in enumerate(DIRECTIONS):
            if step_x == 0:
                first = 2 if step_y < 0 else 10 - reach
                land = 10 if step_y < 0 else 2 - reach
                source = inner.at[pl.ds(first * 2 * width, reach * 2 * width), :]
                target = inner.at[pl.ds(land * 2 * width, reach * 2 * width), :]
            else:
                base = 0 if step_x < 0 else 8 * width
                landing = plus if step_x < 0 else minus
                if step_y == 0:
                    source = sides.at[pl.ds(base, 8 * width), :]
                    target = landing.at[pl.ds(2 * width, 8 * width), :]
                else:
                    first = 0 if step_y < 0 else 8 - reach
                    land = 10 if step_y < 0 else 2 - reach
                    source = sides.at[pl.ds(base + first * width, reach * width), :]
                    target = landing.at[pl.ds(land * width, reach * width), :]
            copies.append(remote(number, d, source, target))
        for copy in copies:
            copy.start()
        return copies

    def remote(number, d, source, target):
        return pltpu.make_async_remote_copy(
            src_ref=source,
            dst_ref=target,
            send_sem=halo_send.at[number, d],
            recv_sem=halo_recv.at[number, d],
            device_id=neighbours[d],
            device_id_type=MESH,
        )

    def arrive(copies):
        for copy in copies:
            copy.wait_recv()

    lane = lax.broadcasted_iota(jnp.int32, (8, 128), 1)
    depth = lax.rem(lane, DEPTH)
    half = lane // DEPTH
    sublane = lax.broadcasted_iota(jnp.int32, (8, 128), 0)

    def inside(position, size):
        return jnp.where((position >= 0) & (position < size), 1.0, 0.0)

    mask_z = {step: inside(depth + step, DEPTH) for step in (-1, 0, 1)}
    mask_x = {at: inside(me_x * 4 + at + 2 * half, 4 * size_gx) for at in range(-2, 4)}

    def mask_y(y):
        return inside(me_y * 8 + y + sublane, 8 * size_gy)

    loads[0].wait()
    held = {}

    def keep(label, p, value):
        held[(label, p)] = value
        logits[label, p + 2, pl.ds(BASE, 8), :] = value
        if p == 1:
            lay_out(inner_u, sides_u, LABELS, label, held[(label, 0)], value)

    spread(unary_in, 4, keep)
    pl.semaphore_wait(barrier, len(everyone))
    sent_u = exchange(0, LABELS, 1, inner_u, sides_u, minus_u, plus_u)

    loads[1].wait()
    mask_own_y = {step: mask_y(step) for step in (-1, 0, 1)}

    def keep_affinity(number, p, value):
        held[(number, p)] = value
        step_x, step_y, step_z = OFFSETS[number]
        mask = mask_x[p + step_x] * mask_own_y[step_y] * mask_z[step_z]
        weight_own[number, p] = value * mask * strength[number]
        if p == 1:
            lay_out(inner_a, sides_a, WIDE, number, held[(number, 0)], value)

    spread(affinity_in, NEIGH // 2, keep_affinity)
    nothing = jnp.zeros((8, 128), jnp.float32)
    for number in range(NEIGH, WIDE):
        lay_out(inner_a, sides_a, WIDE, number, nothing, nothing)
    edge = 2 * 2 * WIDE
    inner_send[0:edge, :] = inner_a[edge : 2 * edge, :].astype(jnp.bfloat16)
    inner_send[edge : 2 * edge, :] = inner_a[4 * edge : 5 * edge, :].astype(jnp.bfloat16)
    sides_send[...] = sides_a[...].astype(jnp.bfloat16)
    copies_a = []
    for d, (step_x, step_y) in enumerate(DIRECTIONS):
        if step_x == 0:
            part = pl.ds(0 if step_y < 0 else edge, edge)
            source, target = inner_send.at[part, :], inner_recv.at[part, :]
        else:
            start = 0 if step_x < 0 else 8 * WIDE
            landing = plus_recv if step_x < 0 else minus_recv
            if step_y == 0:
                source = sides_send.at[pl.ds(start, 8 * WIDE), :]
                target = landing.at[pl.ds(2 * WIDE, 8 * WIDE), :]
            else:
                first = 0 if step_y < 0 else 6
                land = 10 if step_y < 0 else 0
                source = sides_send.at[pl.ds(start + first * WIDE, 2 * WIDE), :]
                target = landing.at[pl.ds(land * WIDE, 2 * WIDE), :]
        copies_a.append(remote(1, d, source, target))
    for copy in copies_a:
        copy.start()

    arrive(sent_u)
    for label in range(LABELS):
        for y in (-1, 1):
            found = assemble(inner_u, minus_u, plus_u, LABELS, label, y, 1)
            for p in (-1, 0, 1, 2):
                logits[label, p + 2, pl.ds(BASE + y, 8), :] = found[p]
    for y in (-1, 1):
        for p in (-1, 0, 1, 2):
            value = normalise(logits[:, p + 2, pl.ds(BASE + y, 8), :])
            put_field(field_0, slice(None), p, y, value)

    def own_logits(p):
        return logits[:, p + 2, pl.ds(BASE, 8), :]

    def own_weight(number, p):
        return weight_own[number, p]

    def forward(a, b):
        return compat[a, b]

    def backward(b, a):
        return compat[a, b]

    def send_field(number, reach, values, inner, sides, minus, plus):
        for label in range(LABELS):
            lay_out(inner, sides, LABELS, label, values[0][label], values[1][label])
        return exchange(number, LABELS, reach, inner, sides, minus, plus)

    sums = message(own_weight, field_0, (0, 1), 0)
    values = []
    for p in (0, 1):
        message_1[:, p] = sums[p]
        values.append(normalise(own_logits(p) - mix(forward, sums[p])))
    sent_q = send_field(2, 2, values, inner_q, sides_q, minus_q, plus_q)

    loads[2].wait()

    def keep_cotangent(label, p, value):
        own_grad[label, p] = value

    spread(cotangent_in, 4, keep_cotangent)
    arrive(copies_a)
    inner_a[0:edge, :] = inner_recv[edge : 2 * edge, :].astype(jnp.float32)
    inner_a[5 * edge : 6 * edge, :] = inner_recv[0:edge, :].astype(jnp.float32)
    minus_a[...] = minus_recv[...].astype(jnp.float32)
    plus_a[...] = plus_recv[...].astype(jnp.float32)
    for number in range(NEIGH):
        for y in (-2, 2):
            found = assemble(inner_a, minus_a, plus_a, WIDE, number, y, 2)
            for p in range(-2, 4):
                wide_aff[number, p + 2, pl.ds(BASE + y, 8), :] = found[p] * strength[number]
    rim_mask_y = {y: mask_y(y) for y in (-2, -1, 0, 1, 2)}

    def rim_weights(target, value):
        for y in (-1, 1):
            for p in (-1, 0, 1, 2):
                for number, (step_x, step_y, step_z) in enumerate(OFFSETS):
                    across = mask_x[p + step_x] * rim_mask_y[y + step_y]
                    if step_z != 0:
                        across = across * mask_z[step_z]
                    target[number, p + 1, pl.ds(BASE + y, 8), :] = across * value(number, p, y)

    def rim_value(number, p, y):
        return wide_aff[number, p + 2, pl.ds(BASE + y, 8), :]

    def back_value(number, p, y):
        step_x, step_y, step_z = OFFSETS[number]
        opposite = NUMBER[(-step_x, -step_y, -step_z)]
        value = wide_aff[opposite, p + step_x + 2, pl.ds(BASE + y + step_y, 8), :]
        if step_z != 0:
            value = pltpu.roll(value, (128 - step_z) % 128, 1)
        return value

    rim_weights(weight_rim, rim_value)

    arrive(sent_q)
    for label in range(LABELS):
        for y in (-2, 2):
            found = assemble(inner_q, minus_q, plus_q, LABELS, label, y, 2)
            for p in range(-2, 4):
                put_field(field_1, label, p, y, found[p])
    for y in (-1, 1):

        def rim_weight(number, p, y=y):
            return weight_rim[number, p + 1, pl.ds(BASE + y, 8), :]

        sums = message(rim_weight, field_1, (-1, 0, 1, 2), y)
        for p in (-1, 0, 1, 2):
            message_2[:, p + 1, pl.ds(BASE + y, 8), :] = sums[p]
            here = logits[:, p + 2, pl.ds(BASE + y, 8), :]
            put_field(field_2, slice(None), p, y, normalise(here - mix(forward, sums[p])))

    sums = message(own_weight, field_2, (0, 1), 0)
    grads = []
    values = []
    for p in (0, 1):
        current = normalise(own_logits(p) - mix(forward, sums[p]))
        step = softmax_back(current, own_grad[:, p])
        total_u[:, p] = step
        grads.append(-step)
        values.append(mix(backward, -step))
    sent_g = send_field(3, 2, values, inner_g, sides_g, minus_g, plus_g)

    def add_compat(grads, messages, begin):
        for b in range(LABELS):
            term = grads[0] * messages[0][b][None] + grads[1] * messages[1][b][None]
            total_c[b] = term if begin else total_c[b] + term

    def add_kernel(values, field, begin):
        for number, (step_x, step_y, step_z) in enumerate(OFFSETS):
            for p in (0, 1):
                near = field[step_z + 1, :, p + step_x + 2, pl.ds(BASE + step_y, 8), :]
                joint = jnp.sum(values[p] * near, axis=0)
                total_r[number, p] = joint if begin else total_r[number, p] + joint

    add_compat(grads, [sums[0], sums[1]], True)
    add_kernel(values, field_2, True)
    rim_weights(weight_back, back_value)

    arrive(sent_g)
    for label in range(LABELS):
        for y in (-2, 2):
            found = assemble(inner_g, minus_g, plus_g, LABELS, label, y, 2)
            for p in range(-2, 4):
                put_field(field_g, label, p, y, found[p])

    def back_weight_at(y):
        def back_weight(number, p):
            return weight_back[number, p + 1, pl.ds(BASE + y, 8), :]

        return back_weight

    for y in (-1, 1):
        sums = message(back_weight_at(y), field_g, (-1, 0, 1, 2), y)
        for p in (-1, 0, 1, 2):
            current = field_2[1, :, p + 2, pl.ds(BASE + y, 8), :]
            grad_p = -softmax_back(current, sums[p])
            rim_p[:, p + 1, pl.ds(BASE + y, 8), :] = grad_p
            put_field(field_h, slice(None), p, y, mix(backward, grad_p))

    sums = message(back_weight_at(0), field_h, (0, 1), 0)
    grads_1 = []
    values_1 = []
    for p in (0, 1):
        current = field_1[1, :, p + 2, pl.ds(BASE, 8), :]
        step = softmax_back(current, sums[p])
        total_u[:, p] = total_u[:, p] + step
        grads_1.append(-step)
        values_1.append(mix(backward, -step))
    sent_h = send_field(4, 1, values_1, inner_h, sides_h, minus_h, plus_h)

    grads_2 = [rim_p[:, p + 1, pl.ds(BASE, 8), :] for p in (0, 1)]
    for p in (0, 1):
        total_u[:, p] = total_u[:, p] - grads_2[p]
    add_compat(grads_2, [message_2[:, p + 1, pl.ds(BASE, 8), :] for p in (0, 1)], False)
    add_kernel([field_h[1, :, p + 2, pl.ds(BASE, 8), :] for p in (0, 1)], field_1, False)
    add_compat(grads_1, [message_1[:, p] for p in (0, 1)], False)
    add_kernel(values_1, field_0, False)

    local = jnp.zeros((8, 128), jnp.float32)
    for b in range(LABELS):
        total = jnp.sum(jnp.sum(total_c[b], axis=1), axis=1, keepdims=True)
        local = jnp.where(lane == b, total, local)
    joint_rows = []
    for number, (step_x, step_y, step_z) in enumerate(OFFSETS):
        row = None
        for p in (0, 1):
            mask = mask_x[p + step_x] * mask_own_y[step_y] * mask_z[step_z]
            joint = total_r[number, p] * mask
            total_r[number, p] = joint * strength[number]
            term = joint * inner_a[inner_rows(0, p, number, WIDE), :]
            row = term if row is None else row + term
        joint_rows.append(jnp.sum(row, axis=0, keepdims=True))
    for group in range(4):
        rows = joint_rows[8 * group : 8 * (group + 1)]
        rows = rows + [jnp.zeros((1, 128), jnp.float32)] * (8 - len(rows))
        total = jnp.sum(jnp.concatenate(rows, axis=0), axis=1, keepdims=True)
        local = jnp.where(lane == LABELS + group, total, local)

    def share(buffer, me, peers, base, value):
        buffer[me] = value
        copies = [
            pltpu.make_async_remote_copy(
                src_ref=buffer.at[me],
                dst_ref=buffer.at[me],
                send_sem=peer_send.at[base + place],
                recv_sem=peer_recv.at[base + place],
                device_id=device,
                device_id_type=MESH,
            )
            for place, device in enumerate(peers)
        ]
        for copy in copies:
            copy.start()
        return copies

    def collect(buffer, copies):
        arrive(copies)
        total = buffer[0]
        for place in range(1, buffer.shape[0]):
            total = total + buffer[place]
        return total

    shared_a = share(gather_a, me_x, peers_a, 0, local)

    def put_affinity(tile, x, value):
        affinity_out[x, :, 128 * tile : 128 * (tile + 1)] = value.astype(jnp.bfloat16)

    gather_columns(lambda number, p: total_r[number, p], NEIGH // 2, put_affinity)
    store_a = pltpu.make_async_copy(affinity_out, grad_affinity_hbm, store_sem.at[0])
    store_a.start()

    arrive(sent_h)
    for label in range(LABELS):
        for y in (-1, 1):
            found = assemble(inner_h, minus_h, plus_h, LABELS, label, y, 1)
            for p in (-1, 0, 1, 2):
                put_field(field_i, label, p, y, found[p])
    shared_b = share(gather_b, me_far, peers_b, len(peers_a), collect(gather_a, shared_a))
    sums = message(back_weight_at(0), field_i, (0, 1), 0)
    for p in (0, 1):
        current = field_0[1, :, p + 2, pl.ds(BASE, 8), :]
        total_u[:, p] = total_u[:, p] + softmax_back(current, sums[p])

    def put_unary(tile, x, value):
        unary_out[x, :, 128 * tile : 128 * (tile + 1)] = value.astype(jnp.bfloat16)

    gather_columns(lambda label, p: total_u[label, p], LABELS // 2, put_unary)
    store_u = pltpu.make_async_copy(unary_out, grad_unary_hbm, store_sem.at[1])
    store_u.start()

    shared_c = share(
        gather_c, me_near, peers_c, len(peers_a) + len(peers_b), collect(gather_b, shared_b)
    )
    voxels = size_gx * 4 * size_gy * 8 * DEPTH
    final = collect(gather_c, shared_c) * (1.0 / math.sqrt(voxels))
    grad_compat[...] = final[:, :LABELS]
    picked = jnp.zeros((8, 128), jnp.float32)
    for group in range(4):
        wanted = lane == 8 * group + sublane
        picked = jnp.where(wanted, final[:, LABELS + group : LABELS + group + 1], picked)
    grad_kernel[...] = jnp.sum(picked, axis=0, keepdims=True)[:, :NEIGH]

    for copy in sent_u + copies_a + sent_q + sent_g + sent_h + shared_a + shared_b + shared_c:
        copy.wait_send()
    store_a.wait()
    store_u.wait()


def shards(sizes, unary_score, affinity, compatibility, kernel_weights, cotangent):
    size_gx, size_gy, size_far, size_near = sizes
    f32, bf16 = jnp.float32, jnp.bfloat16

    def rows(count, kind=f32):
        return pltpu.VMEM((count, 128), kind)

    def exchanged(width):
        return [
            rows(SPAN * 2 * width),
            rows(2 * 8 * width),
            rows(SPAN * width),
            rows(SPAN * width),
        ]

    field = pltpu.VMEM((3, LABELS, 6, TALL, 128), f32)
    pair = pltpu.VMEM((LABELS, 2, 8, 128), f32)
    rim = pltpu.VMEM((LABELS, 4, TALL, 128), f32)
    peers = size_gx + size_far + size_near - 3
    scratch = (
        [
            pltpu.VMEM(unary_score.shape, bf16),
            pltpu.VMEM(affinity.shape, bf16),
            pltpu.VMEM(cotangent.shape, bf16),
            pltpu.VMEM(unary_score.shape, bf16),
            pltpu.VMEM(affinity.shape, bf16),
        ]
        + exchanged(LABELS)
        + exchanged(WIDE)
        + [
            rows(2 * 4 * WIDE, bf16),
            rows(2 * 8 * WIDE, bf16),
            rows(2 * 4 * WIDE, bf16),
            rows(SPAN * WIDE, bf16),
            rows(SPAN * WIDE, bf16),
        ]
        + exchanged(LABELS)
        + exchanged(LABELS)
        + exchanged(LABELS)
        + [
            pltpu.VMEM((LABELS, 6, TALL, 128), f32),
            pair,
            field,
            field,
            field,
            field,
            field,
            field,
            pltpu.VMEM((NEIGH, 6, TALL, 128), f32),
            pltpu.VMEM((NEIGH, 2, 8, 128), f32),
            pltpu.VMEM((NEIGH, 4, TALL, 128), f32),
            pltpu.VMEM((NEIGH, 4, TALL, 128), f32),
            pair,
            rim,
            rim,
            pair,
            pltpu.VMEM((LABELS, LABELS, 8, 128), f32),
            pltpu.VMEM((NEIGH, 2, 8, 128), f32),
            pltpu.VMEM((size_gx, 8, 128), f32),
            pltpu.VMEM((size_far, 8, 128), f32),
            pltpu.VMEM((size_near, 8, 128), f32),
            pltpu.SemaphoreType.DMA((3,)),
            pltpu.SemaphoreType.DMA((2,)),
            pltpu.SemaphoreType.DMA((5, 8)),
            pltpu.SemaphoreType.DMA((5, 8)),
            pltpu.SemaphoreType.DMA((peers,)),
            pltpu.SemaphoreType.DMA((peers,)),
        ]
    )
    anywhere = pl.BlockSpec(memory_space=pl.ANY)
    scalars = pl.BlockSpec(memory_space=pltpu.SMEM)
    vectors = pl.BlockSpec(memory_space=pltpu.VMEM)
    grad_unary, grad_affinity, grad_compat, grad_kernel = pl.pallas_call(
        functools.partial(kernel, sizes),
        out_shape=(
            jax.ShapeDtypeStruct(unary_score.shape, bf16),
            jax.ShapeDtypeStruct(affinity.shape, bf16),
            jax.ShapeDtypeStruct((LABELS, LABELS), f32),
            jax.ShapeDtypeStruct((1, NEIGH), f32),
        ),
        in_specs=[anywhere, anywhere, anywhere, scalars, scalars],
        out_specs=(anywhere, anywhere, vectors, vectors),
        scratch_shapes=scratch,
        compiler_params=pltpu.CompilerParams(
            collective_id=0, has_side_effects=True, vmem_limit_bytes=40 * 1024 * 1024
        ),
        name="mean_field_backward",
    )(unary_score, affinity, cotangent, compatibility, kernel_weights)
    return grad_unary, grad_affinity, grad_compat, grad_kernel.reshape(NEIGH)


def solution(mesh):
    size_gx, size_gy = mesh.shape["gx"], mesh.shape["gy"]
    size_near = 4 if size_gy % 4 == 0 else 1
    sizes = (size_gx, size_gy, size_gy // size_near, size_near)
    in_specs = (P("gx", "gy", None), P("gx", "gy", None), P(), P(), P("gx", "gy", None))
    out_specs = (P("gx", "gy", None), P("gx", "gy", None), P(), P())
    return jax.shard_map(
        functools.partial(shards, sizes),
        mesh=mesh,
        in_specs=in_specs,
        out_specs=out_specs,
        check_vma=False,
    )
```

```python
import functools
import math

import jax
import jax.numpy as jnp
from jax import lax
from jax.experimental import pallas as pl
from jax.experimental.pallas import tpu as pltpu
from jax.sharding import PartitionSpec as P

LABELS = 8
DEPTH = 64
NEIGH = 26
ITERS = 3

OFFSETS = [
    (step_x, step_y, step_z)
    for step_x in (-1, 0, 1)
    for step_y in (-1, 0, 1)
    for step_z in (-1, 0, 1)
    if (step_x, step_y, step_z) != (0, 0, 0)
]
NUMBER = {offset: number for number, offset in enumerate(OFFSETS)}

SPAN = 12
TALL = 24
BASE = 8
DIRECTIONS = [(-1, -1), (-1, 1), (1, -1), (1, 1), (0, -1), (0, 1), (-1, 0), (1, 0)]
WIDE = 32
GRANT = 64 * 1024 * 1024 - 65536
MESH = pl.DeviceIdType.MESH


def low_half():
    return lax.broadcasted_iota(jnp.int32, (8, 128), 1) < DEPTH


def swap(values):
    return pltpu.roll(values, DEPTH, values.ndim - 1)


def inner_rows(y, p, label, width):
    return pl.ds(((y + 2) * 2 + p) * width + label, 8, stride=2 * width)


def side_rows(y, label, width):
    return pl.ds((y + 2) * width + label, 8, stride=width)


def spread(source, tiles, put):
    low = low_half()
    for tile in range(tiles):
        cols = [
            source[x, :, 128 * tile : 128 * (tile + 1)].astype(jnp.float32) for x in range(4)
        ]
        turned = [swap(col) for col in cols]
        for p in (0, 1):
            put(2 * tile, p, jnp.where(low, cols[p], turned[p + 2]))
            put(2 * tile + 1, p, jnp.where(low, turned[p], cols[p + 2]))


def gather_columns(values, tiles, put):
    low = low_half()
    for tile in range(tiles):
        for p in (0, 1):
            even, odd = values(2 * tile, p), values(2 * tile + 1, p)
            put(tile, p, jnp.where(low, even, swap(odd)))
            put(tile, p + 2, jnp.where(low, swap(even), odd))


def lay_out(inner, sides, width, label, first, second):
    low = low_half()
    inner[inner_rows(0, 0, label, width), :] = first
    inner[inner_rows(0, 1, label, width), :] = second
    sides[pl.ds(label, 8, stride=width), :] = jnp.where(low, first, swap(second))
    sides[pl.ds(8 * width + label, 8, stride=width), :] = jnp.where(low, swap(first), second)


def assemble(inner, minus, plus, width, label, y, reach):
    low = low_half()
    own = [inner[inner_rows(y, p, label, width), :] for p in (0, 1)]
    before = minus[side_rows(y, label, width), :]
    after = plus[side_rows(y, label, width), :]
    found = {0: own[0], 1: own[1]}
    found[2] = swap(jnp.where(low, after, own[0]))
    found[-1] = swap(jnp.where(low, own[1], before))
    if reach == 2:
        found[3] = jnp.where(low, swap(own[1]), after)
        found[-2] = jnp.where(low, before, swap(own[0]))
    return found


def message(weight, field, columns, y):
    sums = {p: None for p in columns}
    for step_y in (-1, 0, 1):
        for step_z in (-1, 0, 1):
            for source in range(min(columns) - 1, max(columns) + 2):
                users = [
                    (source - step_x, NUMBER[(step_x, step_y, step_z)])
                    for step_x in (-1, 0, 1)
                    if source - step_x in sums and (step_x, step_y, step_z) in NUMBER
                ]
                if not users:
                    continue
                near = field[step_z + 1, :, source + 2, pl.ds(BASE + y + step_y, 8), :]
                for p, number in users:
                    term = weight(number, p)[None] * near
                    sums[p] = term if sums[p] is None else sums[p] + term
    return sums


def mix(coef, values):
    rows = []
    for a in range(LABELS):
        total = coef(a, 0) * values[0]
        for b in range(1, LABELS):
            total = total + coef(a, b) * values[b]
        rows.append(total)
    return jnp.stack(rows)


def normalise(logits):
    powers = jnp.exp(logits - jnp.max(logits, axis=0, keepdims=True))
    return powers / jnp.sum(powers, axis=0, keepdims=True)


def softmax_back(current, grad_in):
    return current * (grad_in - jnp.sum(current * grad_in, axis=0, keepdims=True))


def put_field(field, label, p, y, value):
    axis = value.ndim - 1
    field[1, label, p + 2, pl.ds(BASE + y, 8), :] = value
    field[0, label, p + 2, pl.ds(BASE + y, 8), :] = pltpu.roll(value, 1, axis)
    field[2, label, p + 2, pl.ds(BASE + y, 8), :] = pltpu.roll(value, 127, axis)


def kernel(
    sizes,
    unary_hbm,
    affinity_hbm,
    cotangent_hbm,
    compat_hbm,
    strength_hbm,
    grad_unary_hbm,
    grad_affinity_hbm,
    grad_compat,
    grad_kernel,
    unary_in,
    affinity_in,
    cotangent_in,
    unary_out,
    affinity_out,
    compat,
    strength,
    inner_u,
    sides_u,
    minus_u,
    plus_u,
    inner_a,
    sides_a,
    minus_a,
    plus_a,
    inner_send,
    sides_send,
    inner_recv,
    minus_recv,
    plus_recv,
    inner_q,
    sides_q,
    minus_q,
    plus_q,
    inner_g,
    sides_g,
    minus_g,
    plus_g,
    inner_h,
    sides_h,
    minus_h,
    plus_h,
    logits,
    own_grad,
    field_0,
    field_1,
    field_2,
    field_g,
    field_h,
    field_i,
    wide_aff,
    weight_own,
    weight_rim,
    weight_back,
    message_1,
    message_2,
    rim_p,
    total_u,
    total_c,
    total_r,
    gather_a,
    gather_b,
    last,
    load_sem,
    store_sem,
    halo_send,
    halo_recv,
    peer_send,
    peer_recv,
):
    size_gx, size_gy, size_far, size_near = sizes
    me_x, me_y = lax.axis_index("gx"), lax.axis_index("gy")
    me_far, me_near = me_y // size_near, lax.rem(me_y, size_near)
    chips = size_gx // 2
    chip, core = me_x // 2, lax.rem(me_x, 2)
    low = low_half()

    def around(index, step, size):
        return lax.rem(index + (step + size), size)

    loads = [
        pltpu.make_async_copy(unary_hbm, unary_in, load_sem.at[0]),
        pltpu.make_async_copy(affinity_hbm, affinity_in, load_sem.at[1]),
        pltpu.make_async_copy(cotangent_hbm, cotangent_in, load_sem.at[2]),
        pltpu.make_async_copy(strength_hbm, strength, load_sem.at[3]),
        pltpu.make_async_copy(compat_hbm, compat, load_sem.at[4]),
    ]
    for load in loads:
        load.start()

    neighbours = [
        (around(me_x, step_x, size_gx), around(me_y, step_y, size_gy))
        for step_x, step_y in DIRECTIONS
    ]
    partner = (me_x + 1 - 2 * core, me_y)
    odd = [(2 * around(chip, step, chips) + 1, me_y) for step in range(chips)]
    even = [(2 * around(chip, step, chips), me_y) for step in range(chips)]

    def ring(step, size):
        return min(step, size - step)

    hops = sorted(
        [(far, near) for far in range(size_far) for near in range(size_near)][1:],
        key=lambda hop: -ring(hop[0], size_far) - ring(hop[1], size_near),
    )
    peers_b = [
        (me_x, around(me_far, far, size_far) * size_near + around(me_near, near, size_near))
        for far, near in hops
    ]
    barrier = pltpu.get_barrier_semaphore()

    def greet(devices):
        for device in devices:
            pl.semaphore_signal(barrier, inc=1, device_id=device, device_id_type=MESH)

    greet(neighbours + [partner])

    @pl.when(core == 1)
    def _():
        greet(odd[1:] + even[1:] + peers_b)

    heard = len(neighbours) + jnp.where(core == 1, chips + len(peers_b), chips)

    def exchange(number, width, reach, inner, sides, minus, plus):
        copies = []
        for d, (step_x, step_y) in enumerate(DIRECTIONS):
            if step_x == 0:
                first = 2 if step_y < 0 else 10 - reach
                land = 10 if step_y < 0 else 2 - reach
                source = inner.at[pl.ds(first * 2 * width, reach * 2 * width), :]
                target = inner.at[pl.ds(land * 2 * width, reach * 2 * width), :]
            else:
                base = 0 if step_x < 0 else 8 * width
                landing = plus if step_x < 0 else minus
                if step_y == 0:
                    source = sides.at[pl.ds(base, 8 * width), :]
                    target = landing.at[pl.ds(2 * width, 8 * width), :]
                else:
                    first = 0 if step_y < 0 else 8 - reach
                    land = 10 if step_y < 0 else 2 - reach
                    source = sides.at[pl.ds(base + first * width, reach * width), :]
                    target = landing.at[pl.ds(land * width, reach * width), :]
            copies.append(remote(number, d, source, target))
        for copy in copies:
            copy.start()
        return copies

    def remote(number, d, source, target):
        return pltpu.make_async_remote_copy(
            src_ref=source,
            dst_ref=target,
            send_sem=halo_send.at[number, d],
            recv_sem=halo_recv.at[number, d],
            device_id=neighbours[d],
            device_id_type=MESH,
        )

    def arrive(copies):
        for copy in copies:
            copy.wait_recv()

    lane = lax.broadcasted_iota(jnp.int32, (8, 128), 1)
    depth = lax.rem(lane, DEPTH)
    half = lane // DEPTH
    sublane = lax.broadcasted_iota(jnp.int32, (8, 128), 0)

    def inside(position, size):
        return jnp.where((position >= 0) & (position < size), 1.0, 0.0)

    mask_z = {step: inside(depth + step, DEPTH) for step in (-1, 0, 1)}
    mask_x = {at: inside(me_x * 4 + at + 2 * half, 4 * size_gx) for at in range(-2, 4)}

    def mask_y(y):
        return inside(me_y * 8 + y + sublane, 8 * size_gy)

    loads[0].wait()
    held = {}

    def keep(label, p, value):
        held[(label, p)] = value
        logits[label, p + 2, pl.ds(BASE, 8), :] = value
        if p == 1:
            lay_out(inner_u, sides_u, LABELS, label, held[(label, 0)], value)

    spread(unary_in, 4, keep)

    loads[1].wait()
    loads[3].wait()
    loads[4].wait()
    mask_own_y = {step: mask_y(step) for step in (-1, 0, 1)}

    def keep_affinity(number, p, value):
        held[(number, p)] = value
        step_x, step_y, step_z = OFFSETS[number]
        mask = mask_x[p + step_x] * mask_own_y[step_y] * mask_z[step_z]
        weight_own[number, p] = value * mask * strength[number]
        if p == 1:
            lay_out(inner_a, sides_a, WIDE, number, held[(number, 0)], value)

    spread(affinity_in, NEIGH // 2, keep_affinity)
    nothing = jnp.zeros((8, 128), jnp.float32)
    for number in range(NEIGH, WIDE):
        lay_out(inner_a, sides_a, WIDE, number, nothing, nothing)
    edge = 2 * 2 * WIDE
    inner_send[0:edge, :] = inner_a[edge : 2 * edge, :].astype(jnp.bfloat16)
    inner_send[edge : 2 * edge, :] = inner_a[4 * edge : 5 * edge, :].astype(jnp.bfloat16)
    sides_send[...] = sides_a[...].astype(jnp.bfloat16)
    pl.semaphore_wait(barrier, heard)
    sent_u = exchange(0, LABELS, 1, inner_u, sides_u, minus_u, plus_u)
    copies_a = []
    for d, (step_x, step_y) in enumerate(DIRECTIONS):
        if step_x == 0:
            part = pl.ds(0 if step_y < 0 else edge, edge)
            source, target = inner_send.at[part, :], inner_recv.at[part, :]
        else:
            start = 0 if step_x < 0 else 8 * WIDE
            landing = plus_recv if step_x < 0 else minus_recv
            if step_y == 0:
                source = sides_send.at[pl.ds(start, 8 * WIDE), :]
                target = landing.at[pl.ds(2 * WIDE, 8 * WIDE), :]
            else:
                first = 0 if step_y < 0 else 6
                land = 10 if step_y < 0 else 0
                source = sides_send.at[pl.ds(start + first * WIDE, 2 * WIDE), :]
                target = landing.at[pl.ds(land * WIDE, 2 * WIDE), :]
        copies_a.append(remote(1, d, source, target))
    for copy in copies_a:
        copy.start()

    arrive(sent_u)
    for label in range(LABELS):
        for y in (-1, 1):
            found = assemble(inner_u, minus_u, plus_u, LABELS, label, y, 1)
            for p in (-1, 0, 1, 2):
                logits[label, p + 2, pl.ds(BASE + y, 8), :] = found[p]
    for y in (-1, 1):
        for p in (-1, 0, 1, 2):
            value = normalise(logits[:, p + 2, pl.ds(BASE + y, 8), :])
            put_field(field_0, slice(None), p, y, value)

    def own_logits(p):
        return logits[:, p + 2, pl.ds(BASE, 8), :]

    def own_weight(number, p):
        return weight_own[number, p]

    def forward(a, b):
        return compat[a, b]

    def backward(b, a):
        return compat[a, b]

    def send_field(number, reach, values, inner, sides, minus, plus):
        for label in range(LABELS):
            lay_out(inner, sides, LABELS, label, values[0][label], values[1][label])
        return exchange(number, LABELS, reach, inner, sides, minus, plus)

    sums = message(own_weight, field_0, (0, 1), 0)
    values = []
    for p in (0, 1):
        message_1[:, p] = sums[p]
        values.append(normalise(own_logits(p) - mix(forward, sums[p])))
    sent_q = send_field(2, 2, values, inner_q, sides_q, minus_q, plus_q)

    loads[2].wait()

    def keep_cotangent(label, p, value):
        own_grad[label, p] = value

    spread(cotangent_in, 4, keep_cotangent)
    arrive(copies_a)
    inner_a[0:edge, :] = inner_recv[edge : 2 * edge, :].astype(jnp.float32)
    inner_a[5 * edge : 6 * edge, :] = inner_recv[0:edge, :].astype(jnp.float32)
    minus_a[...] = minus_recv[...].astype(jnp.float32)
    plus_a[...] = plus_recv[...].astype(jnp.float32)
    for number in range(NEIGH):
        for y in (-2, 2):
            found = assemble(inner_a, minus_a, plus_a, WIDE, number, y, 2)
            for p in range(-2, 4):
                wide_aff[number, p + 2, pl.ds(BASE + y, 8), :] = found[p] * strength[number]
    rim_mask_y = {y: mask_y(y) for y in (-2, -1, 0, 1, 2)}

    def rim_weights(target, value):
        for y in (-1, 1):
            for p in (-1, 0, 1, 2):
                for number, (step_x, step_y, step_z) in enumerate(OFFSETS):
                    across = mask_x[p + step_x] * rim_mask_y[y + step_y]
                    if step_z != 0:
                        across = across * mask_z[step_z]
                    target[number, p + 1, pl.ds(BASE + y, 8), :] = across * value(number, p, y)

    def rim_value(number, p, y):
        return wide_aff[number, p + 2, pl.ds(BASE + y, 8), :]

    def back_value(number, p, y):
        step_x, step_y, step_z = OFFSETS[number]
        opposite = NUMBER[(-step_x, -step_y, -step_z)]
        value = wide_aff[opposite, p + step_x + 2, pl.ds(BASE + y + step_y, 8), :]
        if step_z != 0:
            value = pltpu.roll(value, (128 - step_z) % 128, 1)
        return value

    rim_weights(weight_rim, rim_value)

    arrive(sent_q)
    for label in range(LABELS):
        for y in (-2, 2):
            found = assemble(inner_q, minus_q, plus_q, LABELS, label, y, 2)
            for p in range(-2, 4):
                put_field(field_1, label, p, y, found[p])
    for y in (-1, 1):

        def rim_weight(number, p, y=y):
            return weight_rim[number, p + 1, pl.ds(BASE + y, 8), :]

        sums = message(rim_weight, field_1, (-1, 0, 1, 2), y)
        for p in (-1, 0, 1, 2):
            message_2[:, p + 1, pl.ds(BASE + y, 8), :] = sums[p]
            here = logits[:, p + 2, pl.ds(BASE + y, 8), :]
            put_field(field_2, slice(None), p, y, normalise(here - mix(forward, sums[p])))

    sums = message(own_weight, field_2, (0, 1), 0)
    grads = []
    values = []
    for p in (0, 1):
        current = normalise(own_logits(p) - mix(forward, sums[p]))
        step = softmax_back(current, own_grad[:, p])
        total_u[:, p] = step
        grads.append(-step)
        values.append(mix(backward, -step))
    sent_g = send_field(3, 2, values, inner_g, sides_g, minus_g, plus_g)

    def add_compat(grads, messages, begin):
        for b in range(LABELS):
            term = grads[0] * messages[0][b][None] + grads[1] * messages[1][b][None]
            total_c[b] = term if begin else total_c[b] + term

    def add_kernel(values, field, begin):
        for number, (step_x, step_y, step_z) in enumerate(OFFSETS):
            for p in (0, 1):
                near = field[step_z + 1, :, p + step_x + 2, pl.ds(BASE + step_y, 8), :]
                joint = jnp.sum(values[p] * near, axis=0)
                total_r[number, p] = joint if begin else total_r[number, p] + joint

    add_compat(grads, [sums[0], sums[1]], True)
    add_kernel(values, field_2, True)
    rim_weights(weight_back, back_value)

    arrive(sent_g)
    for label in range(LABELS):
        for y in (-2, 2):
            found = assemble(inner_g, minus_g, plus_g, LABELS, label, y, 2)
            for p in range(-2, 4):
                put_field(field_g, label, p, y, found[p])

    def back_weight_at(y):
        def back_weight(number, p):
            return weight_back[number, p + 1, pl.ds(BASE + y, 8), :]

        return back_weight

    for y in (-1, 1):
        sums = message(back_weight_at(y), field_g, (-1, 0, 1, 2), y)
        for p in (-1, 0, 1, 2):
            current = field_2[1, :, p + 2, pl.ds(BASE + y, 8), :]
            grad_p = -softmax_back(current, sums[p])
            rim_p[:, p + 1, pl.ds(BASE + y, 8), :] = grad_p
            put_field(field_h, slice(None), p, y, mix(backward, grad_p))

    sums = message(back_weight_at(0), field_h, (0, 1), 0)
    grads_1 = []
    values_1 = []
    for p in (0, 1):
        current = field_1[1, :, p + 2, pl.ds(BASE, 8), :]
        step = softmax_back(current, sums[p])
        total_u[:, p] = total_u[:, p] + step
        grads_1.append(-step)
        values_1.append(mix(backward, -step))
    sent_h = send_field(4, 1, values_1, inner_h, sides_h, minus_h, plus_h)

    grads_2 = [rim_p[:, p + 1, pl.ds(BASE, 8), :] for p in (0, 1)]
    for p in (0, 1):
        total_u[:, p] = total_u[:, p] - grads_2[p]
    add_compat(grads_2, [message_2[:, p + 1, pl.ds(BASE, 8), :] for p in (0, 1)], False)
    add_kernel([field_h[1, :, p + 2, pl.ds(BASE, 8), :] for p in (0, 1)], field_1, False)
    add_compat(grads_1, [message_1[:, p] for p in (0, 1)], False)
    add_kernel(values_1, field_0, False)

    local = jnp.zeros((8, 128), jnp.float32)
    for b in range(LABELS):
        total = jnp.sum(jnp.sum(total_c[b], axis=1), axis=1, keepdims=True)
        local = jnp.where(lane == 8 * b + sublane, total, local)
    joint_rows = []
    for number, (step_x, step_y, step_z) in enumerate(OFFSETS):
        row = None
        for p in (0, 1):
            mask = mask_x[p + step_x] * mask_own_y[step_y] * mask_z[step_z]
            joint = total_r[number, p] * mask
            total_r[number, p] = joint * strength[number]
            term = joint * inner_a[inner_rows(0, p, number, WIDE), :]
            row = term if row is None else row + term
        joint_rows.append(jnp.sum(row, axis=0, keepdims=True))
    for group in range(4):
        rows = joint_rows[8 * group : 8 * (group + 1)]
        rows = rows + [jnp.zeros((1, 128), jnp.float32)] * (8 - len(rows))
        total = jnp.sum(jnp.concatenate(rows, axis=0), axis=1, keepdims=True)
        local = jnp.where(lane == 8 * (LABELS + group) + sublane, total, local)

    gather_a[me_x] = jnp.sum(local, axis=0, keepdims=True)

    def to_peer(buffer, me, place_send, place_recv, device):
        return pltpu.make_async_remote_copy(
            src_ref=buffer.at[me],
            dst_ref=buffer.at[me],
            send_sem=peer_send.at[place_send],
            recv_sem=peer_recv.at[place_recv],
            device_id=device,
            device_id_type=MESH,
        )

    along_x = [to_peer(gather_a, me_x, step, 2 * step + core, odd[step]) for step in range(chips)]
    for step in sorted(range(1, chips), key=lambda step: -ring(step, chips)):
        along_x[step].start()

    @pl.when(core == 0)
    def _():
        along_x[0].start()

    def put_affinity(tile, x, value):
        affinity_out[x, :, 128 * tile : 128 * (tile + 1)] = value.astype(jnp.bfloat16)

    gather_columns(lambda number, p: total_r[number, p], NEIGH // 2, put_affinity)
    store_a = pltpu.make_async_copy(affinity_out, grad_affinity_hbm, store_sem.at[0])
    store_a.start()

    arrive(sent_h)
    for label in range(LABELS):
        for y in (-1, 1):
            found = assemble(inner_h, minus_h, plus_h, LABELS, label, y, 1)
            for p in (-1, 0, 1, 2):
                put_field(field_i, label, p, y, found[p])
    sums = message(back_weight_at(0), field_i, (0, 1), 0)
    for p in (0, 1):
        current = field_0[1, :, p + 2, pl.ds(BASE, 8), :]
        total_u[:, p] = total_u[:, p] + softmax_back(current, sums[p])

    def put_unary(tile, x, value):
        unary_out[x, :, 128 * tile : 128 * (tile + 1)] = value.astype(jnp.bfloat16)

    gather_columns(lambda label, p: total_u[label, p], LABELS // 2, put_unary)
    store_u = pltpu.make_async_copy(unary_out, grad_unary_hbm, store_sem.at[1])
    store_u.start()

    base = 2 * chips
    along_y = [
        to_peer(gather_b, me_y, base + place, base + place, device)
        for place, device in enumerate(peers_b)
    ]
    to_even = to_peer(last, 0, base + len(peers_b), base + len(peers_b), partner)

    @pl.when(core == 1)
    def _():
        for step in range(chips):
            for sender in (0, 1):
                if (step, sender) != (0, 1):
                    to_peer(gather_a, me_x, 0, 2 * step + sender, partner).wait_recv()
        total = gather_a[0]
        for place in range(1, size_gx):
            total = total + gather_a[place]
        gather_b[me_y] = total
        for copy in along_y:
            copy.start()
        for copy in along_y:
            copy.wait_recv()
        total = gather_b[0]
        for place in range(1, size_gy):
            total = total + gather_b[place]
        last[0] = total
        to_even.start()

    @pl.when(core == 0)
    def _():
        to_even.wait_recv()

    voxels = size_gx * 4 * size_gy * 8 * DEPTH
    final = last[0] * (1.0 / math.sqrt(voxels))
    grad_kernel[...] = pltpu.roll(final, 128 - LABELS * LABELS, 1)[:, :NEIGH]
    spaced = jnp.where(lax.rem(lane, 8) == sublane, jnp.broadcast_to(final, (8, 128)), 0.0)
    table = jnp.zeros((8, 128), jnp.float32)
    for b in range(LABELS):
        column = jnp.sum(jnp.where(lane // 8 == b, spaced, 0.0), axis=1, keepdims=True)
        table = jnp.where(lane == b, column, table)
    grad_compat[...] = table[:, :LABELS]

    for copy in sent_u + copies_a + sent_q + sent_g + sent_h + along_x[1:]:
        copy.wait_send()

    @pl.when(core == 0)
    def _():
        along_x[0].wait_send()

    @pl.when(core == 1)
    def _():
        for copy in along_y + [to_even]:
            copy.wait_send()

    store_a.wait()
    store_u.wait()


def hand_out(*refs):
    parts, results, sem = refs[:4], refs[4:8], refs[8]
    copies = [
        pltpu.make_async_copy(part, result, sem.at[number])
        for number, (part, result) in enumerate(zip(parts, results))
    ]
    for copy in copies:
        copy.start()
    for copy in copies:
        copy.wait()


def shards(sizes, unary_score, affinity, compatibility, kernel_weights, cotangent):
    size_gx, size_gy, size_far, size_near = sizes
    f32, bf16 = jnp.float32, jnp.bfloat16

    def rows(count, kind=f32):
        return pltpu.VMEM((count, 128), kind)

    def exchanged(width):
        return [
            rows(SPAN * 2 * width),
            rows(2 * 8 * width),
            rows(SPAN * width),
            rows(SPAN * width),
        ]

    field = pltpu.VMEM((3, LABELS, 6, TALL, 128), f32)
    pair = pltpu.VMEM((LABELS, 2, 8, 128), f32)
    rim = pltpu.VMEM((LABELS, 4, TALL, 128), f32)
    peers = size_gx + size_gy
    scratch = (
        [
            pltpu.VMEM(unary_score.shape, bf16),
            pltpu.VMEM(affinity.shape, bf16),
            pltpu.VMEM(cotangent.shape, bf16),
            pltpu.VMEM(unary_score.shape, bf16),
            pltpu.VMEM(affinity.shape, bf16),
            pltpu.SMEM(compatibility.shape, f32),
            pltpu.SMEM(kernel_weights.shape, f32),
        ]
        + exchanged(LABELS)
        + exchanged(WIDE)
        + [
            rows(2 * 4 * WIDE, bf16),
            rows(2 * 8 * WIDE, bf16),
            rows(2 * 4 * WIDE, bf16),
            rows(SPAN * WIDE, bf16),
            rows(SPAN * WIDE, bf16),
        ]
        + exchanged(LABELS)
        + exchanged(LABELS)
        + exchanged(LABELS)
        + [
            pltpu.VMEM((LABELS, 6, TALL, 128), f32),
            pair,
            field,
            field,
            field,
            field,
            field,
            field,
            pltpu.VMEM((NEIGH, 6, TALL, 128), f32),
            pltpu.VMEM((NEIGH, 2, 8, 128), f32),
            pltpu.VMEM((NEIGH, 4, TALL, 128), f32),
            pltpu.VMEM((NEIGH, 4, TALL, 128), f32),
            pair,
            rim,
            rim,
            pair,
            pltpu.VMEM((LABELS, LABELS, 8, 128), f32),
            pltpu.VMEM((NEIGH, 2, 8, 128), f32),
            pltpu.VMEM((size_gx, 1, 128), f32),
            pltpu.VMEM((size_gy, 1, 128), f32),
            pltpu.VMEM((1, 1, 128), f32),
            pltpu.SemaphoreType.DMA((5,)),
            pltpu.SemaphoreType.DMA((2,)),
            pltpu.SemaphoreType.DMA((5, 8)),
            pltpu.SemaphoreType.DMA((5, 8)),
            pltpu.SemaphoreType.DMA((peers,)),
            pltpu.SemaphoreType.DMA((peers,)),
        ]
    )
    anywhere = pl.BlockSpec(memory_space=pl.ANY)
    in_hbm = pl.BlockSpec(memory_space=pltpu.HBM)
    vectors = pl.BlockSpec(memory_space=pltpu.VMEM)
    grad_unary, grad_affinity, grad_compat, grad_kernel = pl.pallas_call(
        functools.partial(kernel, sizes),
        out_shape=(
            jax.ShapeDtypeStruct(unary_score.shape, bf16),
            jax.ShapeDtypeStruct(affinity.shape, bf16),
            jax.ShapeDtypeStruct((LABELS, LABELS), f32),
            jax.ShapeDtypeStruct((1, NEIGH), f32),
        ),
        in_specs=[in_hbm] * 5,
        out_specs=(anywhere, anywhere, vectors, vectors),
        scratch_shapes=scratch,
        compiler_params=pltpu.CompilerParams(
            collective_id=0, has_side_effects=True, vmem_limit_bytes=GRANT
        ),
        name="mean_field_backward",
    )(unary_score, affinity, cotangent, compatibility, kernel_weights)
    found = (grad_unary, grad_affinity, grad_compat, grad_kernel.reshape(NEIGH))
    return pl.pallas_call(
        hand_out,
        out_shape=tuple(jax.ShapeDtypeStruct(part.shape, part.dtype) for part in found),
        in_specs=[anywhere] * 4,
        out_specs=(in_hbm,) * 4,
        scratch_shapes=[pltpu.SemaphoreType.DMA((4,))],
        compiler_params=pltpu.CompilerParams(vmem_limit_bytes=GRANT),
        name="hand_out",
    )(*found)


def solution(mesh):
    size_gx, size_gy = mesh.shape["gx"], mesh.shape["gy"]
    size_near = 4 if size_gy % 4 == 0 else 1
    sizes = (size_gx, size_gy, size_gy // size_near, size_near)
    in_specs = (P("gx", "gy", None), P("gx", "gy", None), P(), P(), P("gx", "gy", None))
    out_specs = (P("gx", "gy", None), P("gx", "gy", None), P(), P())
    return jax.shard_map(
        functools.partial(shards, sizes),
        mesh=mesh,
        in_specs=in_specs,
        out_specs=out_specs,
        check_vma=False,
    )
```

```python
import functools
import math

import jax
import jax.numpy as jnp
from jax import lax
from jax.experimental import pallas as pl
from jax.experimental.pallas import tpu as pltpu
from jax.sharding import PartitionSpec as P

LABELS = 8
DEPTH = 64
NEIGH = 26
ITERS = 3

OFFSETS = [
    (step_x, step_y, step_z)
    for step_x in (-1, 0, 1)
    for step_y in (-1, 0, 1)
    for step_z in (-1, 0, 1)
    if (step_x, step_y, step_z) != (0, 0, 0)
]
NUMBER = {offset: number for number, offset in enumerate(OFFSETS)}

SPAN = 12
TALL = 24
BASE = 8
DIRECTIONS = [(-1, -1), (-1, 1), (1, -1), (1, 1), (0, -1), (0, 1), (-1, 0), (1, 0)]
WIDE = 32
GRANT = 64 * 1024 * 1024 - 65536
MESH = pl.DeviceIdType.MESH


def low_half():
    return lax.broadcasted_iota(jnp.int32, (8, 128), 1) < DEPTH


def swap(values):
    return pltpu.roll(values, DEPTH, values.ndim - 1)


def inner_rows(y, p, label, width):
    return pl.ds(((y + 2) * 2 + p) * width + label, 8, stride=2 * width)


def side_rows(y, label, width):
    return pl.ds((y + 2) * width + label, 8, stride=width)


def spread(source, tiles, put):
    low = low_half()
    for tile in range(tiles):
        cols = [
            source[x, :, 128 * tile : 128 * (tile + 1)].astype(jnp.float32) for x in range(4)
        ]
        turned = [swap(col) for col in cols]
        for p in (0, 1):
            put(2 * tile, p, jnp.where(low, cols[p], turned[p + 2]))
            put(2 * tile + 1, p, jnp.where(low, turned[p], cols[p + 2]))


def gather_columns(values, tiles, put):
    low = low_half()
    for tile in range(tiles):
        for p in (0, 1):
            even, odd = values(2 * tile, p), values(2 * tile + 1, p)
            put(tile, p, jnp.where(low, even, swap(odd)))
            put(tile, p + 2, jnp.where(low, swap(even), odd))


def lay_out(inner, sides, width, label, first, second):
    low = low_half()
    inner[inner_rows(0, 0, label, width), :] = first
    inner[inner_rows(0, 1, label, width), :] = second
    sides[pl.ds(label, 8, stride=width), :] = jnp.where(low, first, swap(second))
    sides[pl.ds(8 * width + label, 8, stride=width), :] = jnp.where(low, swap(first), second)


def assemble(inner, minus, plus, width, label, y, reach):
    low = low_half()
    own = [inner[inner_rows(y, p, label, width), :] for p in (0, 1)]
    before = minus[side_rows(y, label, width), :]
    after = plus[side_rows(y, label, width), :]
    found = {0: own[0], 1: own[1]}
    found[2] = swap(jnp.where(low, after, own[0]))
    found[-1] = swap(jnp.where(low, own[1], before))
    if reach == 2:
        found[3] = jnp.where(low, swap(own[1]), after)
        found[-2] = jnp.where(low, before, swap(own[0]))
    return found


def message(weight, field, columns, y):
    sums = {p: None for p in columns}
    for step_y in (-1, 0, 1):
        for step_z in (-1, 0, 1):
            for source in range(min(columns) - 1, max(columns) + 2):
                users = [
                    (source - step_x, NUMBER[(step_x, step_y, step_z)])
                    for step_x in (-1, 0, 1)
                    if source - step_x in sums and (step_x, step_y, step_z) in NUMBER
                ]
                if not users:
                    continue
                near = field[step_z + 1, :, source + 2, pl.ds(BASE + y + step_y, 8), :]
                for p, number in users:
                    term = weight(number, p)[None] * near
                    sums[p] = term if sums[p] is None else sums[p] + term
    return sums


def mix(coef, values):
    rows = []
    for a in range(LABELS):
        total = coef(a, 0) * values[0]
        for b in range(1, LABELS):
            total = total + coef(a, b) * values[b]
        rows.append(total)
    return jnp.stack(rows)


def normalise(logits):
    powers = jnp.exp(logits - jnp.max(logits, axis=0, keepdims=True))
    return powers / jnp.sum(powers, axis=0, keepdims=True)


def softmax_back(current, grad_in):
    return current * (grad_in - jnp.sum(current * grad_in, axis=0, keepdims=True))


def put_shifts(field, p, y, values):
    field[0, :, p + 2, pl.ds(BASE + y, 8), :] = pltpu.roll(values, 1, 2)
    field[2, :, p + 2, pl.ds(BASE + y, 8), :] = pltpu.roll(values, 127, 2)


def put_field(field, p, y, values):
    field[1, :, p + 2, pl.ds(BASE + y, 8), :] = values
    put_shifts(field, p, y, values)


def rim_tiles(reach):
    return range(-reach, 2 + reach), (-2, 2) if reach == 2 else (-1, 1)


def gather_field(field, inner, minus, plus, reach):
    columns, starts = rim_tiles(reach)
    for label in range(LABELS):
        for y in starts:
            found = assemble(inner, minus, plus, LABELS, label, y, reach)
            for p in columns:
                field[1, label, p + 2, pl.ds(BASE + y, 8), :] = found[p]
    for y in starts:
        for p in columns:
            put_shifts(field, p, y, field[1, :, p + 2, pl.ds(BASE + y, 8), :])


def kernel(
    sizes,
    unary_hbm,
    affinity_hbm,
    cotangent_hbm,
    compat_hbm,
    strength_hbm,
    grad_unary_hbm,
    grad_affinity_hbm,
    grad_compat,
    grad_kernel,
    unary_in,
    affinity_in,
    cotangent_in,
    unary_out,
    affinity_out,
    compat,
    strength,
    inner_u,
    sides_u,
    minus_u,
    plus_u,
    inner_a,
    sides_a,
    minus_a,
    plus_a,
    *rest,
):
    boxes, rest = rest[:15], rest[15:]
    box_u, box_a, box_g = boxes[:5], boxes[5:10], boxes[10:]
    (
        inner_q,
        sides_q,
        minus_q,
        plus_q,
        inner_g,
        sides_g,
        minus_g,
        plus_g,
        inner_h,
        sides_h,
        minus_h,
        plus_h,
        logits,
        own_grad,
        field_0,
        field_1,
        field_2,
        field_g,
        field_h,
        field_i,
        wide_aff,
        weight_own,
        weight_rim,
        weight_back,
        message_1,
        message_2,
        rim_p,
        total_u,
        total_c,
        total_r,
        gather_a,
        gather_b,
        last,
        load_sem,
        store_sem,
        halo_send,
        halo_recv,
        peer_send,
        peer_recv,
    ) = rest
    size_gx, size_gy, size_far, size_near = sizes
    me_x, me_y = lax.axis_index("gx"), lax.axis_index("gy")
    me_far, me_near = me_y // size_near, lax.rem(me_y, size_near)
    chips = size_gx // 2
    chip, core = me_x // 2, lax.rem(me_x, 2)
    low = low_half()

    def around(index, step, size):
        return lax.rem(index + (step + size), size)

    loads = [
        pltpu.make_async_copy(unary_hbm, unary_in, load_sem.at[0]),
        pltpu.make_async_copy(affinity_hbm, affinity_in, load_sem.at[1]),
        pltpu.make_async_copy(cotangent_hbm, cotangent_in, load_sem.at[2]),
        pltpu.make_async_copy(strength_hbm, strength, load_sem.at[3]),
        pltpu.make_async_copy(compat_hbm, compat, load_sem.at[4]),
    ]
    for load in loads:
        load.start()

    neighbours = [
        (around(me_x, step_x, size_gx), around(me_y, step_y, size_gy))
        for step_x, step_y in DIRECTIONS
    ]
    partner = (me_x + 1 - 2 * core, me_y)
    odd = [(2 * around(chip, step, chips) + 1, me_y) for step in range(chips)]
    even = [(2 * around(chip, step, chips), me_y) for step in range(chips)]

    def ring(step, size):
        return min(step, size - step)

    hops = sorted(
        [(far, near) for far in range(size_far) for near in range(size_near)][1:],
        key=lambda hop: -ring(hop[0], size_far) - ring(hop[1], size_near),
    )
    peers_b = [
        (me_x, around(me_far, far, size_far) * size_near + around(me_near, near, size_near))
        for far, near in hops
    ]
    barrier = pltpu.get_barrier_semaphore()

    def greet(devices):
        for device in devices:
            pl.semaphore_signal(barrier, inc=1, device_id=device, device_id_type=MESH)

    greet(neighbours + [partner])

    @pl.when(core == 1)
    def _():
        greet(odd[1:] + even[1:] + peers_b)

    heard = len(neighbours) + jnp.where(core == 1, chips + len(peers_b), chips)

    def exchange(number, width, reach, inner, sides, minus, plus):
        copies = []
        for d, (step_x, step_y) in enumerate(DIRECTIONS):
            if step_x == 0:
                first = 2 if step_y < 0 else 10 - reach
                land = 10 if step_y < 0 else 2 - reach
                source = inner.at[pl.ds(first * 2 * width, reach * 2 * width), :]
                target = inner.at[pl.ds(land * 2 * width, reach * 2 * width), :]
            else:
                base = 0 if step_x < 0 else 8 * width
                landing = plus if step_x < 0 else minus
                if step_y == 0:
                    source = sides.at[pl.ds(base, 8 * width), :]
                    target = landing.at[pl.ds(2 * width, 8 * width), :]
                else:
                    first = 0 if step_y < 0 else 8 - reach
                    land = 10 if step_y < 0 else 2 - reach
                    source = sides.at[pl.ds(base + first * width, reach * width), :]
                    target = landing.at[pl.ds(land * width, reach * width), :]
            copies.append(remote(number, d, source, target))
        for copy in copies:
            copy.start()
        return copies

    def remote(number, d, source, target):
        return pltpu.make_async_remote_copy(
            src_ref=source,
            dst_ref=target,
            send_sem=halo_send.at[number, d],
            recv_sem=halo_recv.at[number, d],
            device_id=neighbours[d],
            device_id_type=MESH,
        )

    def arrive(copies):
        for copy in copies:
            copy.wait_recv()

    def narrow(width, reach, inner, sides, box):
        inner_send, sides_send = box[:2]
        part = reach * 2 * width
        for place, first in enumerate((2, 10 - reach)):
            rows = inner[pl.ds(first * 2 * width, part), :]
            inner_send[pl.ds(place * part, part), :] = rows.astype(jnp.bfloat16)
        sides_send[...] = sides[...].astype(jnp.bfloat16)

    def start_narrow(number, reach, box):
        inner_send, sides_send, inner_recv, minus_recv, plus_recv = box
        width = sides_send.shape[0] // 16
        part = reach * 2 * width
        copies = []
        for d, (step_x, step_y) in enumerate(DIRECTIONS):
            if step_x == 0:
                rows = pl.ds(0 if step_y < 0 else part, part)
                source, target = inner_send.at[rows, :], inner_recv.at[rows, :]
            else:
                start = 0 if step_x < 0 else 8 * width
                landing = plus_recv if step_x < 0 else minus_recv
                if step_y == 0:
                    source = sides_send.at[pl.ds(start, 8 * width), :]
                    target = landing.at[pl.ds(2 * width, 8 * width), :]
                else:
                    first = 0 if step_y < 0 else 6
                    land = 10 if step_y < 0 else 0
                    source = sides_send.at[pl.ds(start + first * width, 2 * width), :]
                    target = landing.at[pl.ds(land * width, 2 * width), :]
            copies.append(remote(number, d, source, target))
        for copy in copies:
            copy.start()
        return copies

    def arrive_narrow(copies, width, reach, inner, minus, plus, box):
        inner_recv, minus_recv, plus_recv = box[2:]
        part = reach * 2 * width
        arrive(copies)
        for place, land in enumerate((10, 2 - reach)):
            rows = inner_recv[pl.ds(place * part, part), :]
            inner[pl.ds(land * 2 * width, part), :] = rows.astype(jnp.float32)
        minus[...] = minus_recv[...].astype(jnp.float32)
        plus[...] = plus_recv[...].astype(jnp.float32)

    lane = lax.broadcasted_iota(jnp.int32, (8, 128), 1)
    depth = lax.rem(lane, DEPTH)
    half = lane // DEPTH
    sublane = lax.broadcasted_iota(jnp.int32, (8, 128), 0)

    def inside(position, size):
        return jnp.where((position >= 0) & (position < size), 1.0, 0.0)

    mask_z = {step: inside(depth + step, DEPTH) for step in (-1, 0, 1)}
    mask_x = {at: inside(me_x * 4 + at + 2 * half, 4 * size_gx) for at in range(-2, 4)}

    def mask_y(y):
        return inside(me_y * 8 + y + sublane, 8 * size_gy)

    loads[0].wait()
    held = {}

    def keep(label, p, value):
        held[(label, p)] = value
        logits[label, p + 2, pl.ds(BASE, 8), :] = value
        if p == 1:
            lay_out(inner_u, sides_u, LABELS, label, held[(label, 0)], value)

    spread(unary_in, 4, keep)

    loads[1].wait()
    loads[3].wait()
    loads[4].wait()
    mask_own_y = {step: mask_y(step) for step in (-1, 0, 1)}

    def keep_affinity(number, p, value):
        held[(number, p)] = value
        step_x, step_y, step_z = OFFSETS[number]
        mask = mask_x[p + step_x] * mask_own_y[step_y] * mask_z[step_z]
        weight_own[number, p] = value * mask * strength[number]
        if p == 1:
            lay_out(inner_a, sides_a, WIDE, number, held[(number, 0)], value)

    spread(affinity_in, NEIGH // 2, keep_affinity)
    nothing = jnp.zeros((8, 128), jnp.float32)
    for number in range(NEIGH, WIDE):
        lay_out(inner_a, sides_a, WIDE, number, nothing, nothing)
    narrow(LABELS, 1, inner_u, sides_u, box_u)
    narrow(WIDE, 2, inner_a, sides_a, box_a)
    pl.semaphore_wait(barrier, heard)
    sent_u = start_narrow(0, 1, box_u)
    sent_a = start_narrow(1, 2, box_a)

    arrive_narrow(sent_u, LABELS, 1, inner_u, minus_u, plus_u, box_u)
    for label in range(LABELS):
        for y in (-1, 1):
            found = assemble(inner_u, minus_u, plus_u, LABELS, label, y, 1)
            for p in (-1, 0, 1, 2):
                logits[label, p + 2, pl.ds(BASE + y, 8), :] = found[p]
    for y in (-1, 1):
        for p in (-1, 0, 1, 2):
            value = normalise(logits[:, p + 2, pl.ds(BASE + y, 8), :])
            put_field(field_0, p, y, value)

    def own_logits(p):
        return logits[:, p + 2, pl.ds(BASE, 8), :]

    def own_weight(number, p):
        return weight_own[number, p]

    def forward(a, b):
        return compat[a, b]

    def backward(b, a):
        return compat[a, b]

    def lay_field(values, inner, sides):
        for label in range(LABELS):
            lay_out(inner, sides, LABELS, label, values[0][label], values[1][label])

    def send_field(number, reach, values, inner, sides, minus, plus):
        lay_field(values, inner, sides)
        return exchange(number, LABELS, reach, inner, sides, minus, plus)

    sums = message(own_weight, field_0, (0, 1), 0)
    values = []
    for p in (0, 1):
        message_1[:, p] = sums[p]
        values.append(normalise(own_logits(p) - mix(forward, sums[p])))
    sent_q = send_field(2, 2, values, inner_q, sides_q, minus_q, plus_q)

    loads[2].wait()

    def keep_cotangent(label, p, value):
        own_grad[label, p] = value

    spread(cotangent_in, 4, keep_cotangent)
    arrive_narrow(sent_a, WIDE, 2, inner_a, minus_a, plus_a, box_a)
    for number in range(NEIGH):
        for y in (-2, 2):
            found = assemble(inner_a, minus_a, plus_a, WIDE, number, y, 2)
            for p in range(-2, 4):
                wide_aff[number, p + 2, pl.ds(BASE + y, 8), :] = found[p] * strength[number]
    rim_mask_y = {y: mask_y(y) for y in (-2, -1, 0, 1, 2)}

    def rim_weights(target, value):
        for y in (-1, 1):
            for p in (-1, 0, 1, 2):
                for number, (step_x, step_y, step_z) in enumerate(OFFSETS):
                    across = mask_x[p + step_x] * rim_mask_y[y + step_y]
                    if step_z != 0:
                        across = across * mask_z[step_z]
                    target[number, p + 1, pl.ds(BASE + y, 8), :] = across * value(number, p, y)

    def rim_value(number, p, y):
        return wide_aff[number, p + 2, pl.ds(BASE + y, 8), :]

    def back_value(number, p, y):
        step_x, step_y, step_z = OFFSETS[number]
        opposite = NUMBER[(-step_x, -step_y, -step_z)]
        value = wide_aff[opposite, p + step_x + 2, pl.ds(BASE + y + step_y, 8), :]
        if step_z != 0:
            value = pltpu.roll(value, (128 - step_z) % 128, 1)
        return value

    rim_weights(weight_rim, rim_value)

    arrive(sent_q)
    gather_field(field_1, inner_q, minus_q, plus_q, 2)
    for y in (-1, 1):

        def rim_weight(number, p, y=y):
            return weight_rim[number, p + 1, pl.ds(BASE + y, 8), :]

        sums = message(rim_weight, field_1, (-1, 0, 1, 2), y)
        for p in (-1, 0, 1, 2):
            message_2[:, p + 1, pl.ds(BASE + y, 8), :] = sums[p]
            here = logits[:, p + 2, pl.ds(BASE + y, 8), :]
            put_field(field_2, p, y, normalise(here - mix(forward, sums[p])))

    sums = message(own_weight, field_2, (0, 1), 0)
    grads = []
    values = []
    for p in (0, 1):
        current = normalise(own_logits(p) - mix(forward, sums[p]))
        step = softmax_back(current, own_grad[:, p])
        total_u[:, p] = step
        grads.append(-step)
        values.append(mix(backward, -step))
    lay_field(values, inner_g, sides_g)
    narrow(LABELS, 2, inner_g, sides_g, box_g)
    sent_g = start_narrow(3, 2, box_g)

    def add_compat(grads, messages, begin):
        for b in range(LABELS):
            term = grads[0] * messages[0][b][None] + grads[1] * messages[1][b][None]
            total_c[b] = term if begin else total_c[b] + term

    def add_kernel(values, field, begin):
        for number, (step_x, step_y, step_z) in enumerate(OFFSETS):
            for p in (0, 1):
                near = field[step_z + 1, :, p + step_x + 2, pl.ds(BASE + step_y, 8), :]
                joint = jnp.sum(values[p] * near, axis=0)
                total_r[number, p] = joint if begin else total_r[number, p] + joint

    add_compat(grads, [sums[0], sums[1]], True)
    add_kernel(values, field_2, True)
    rim_weights(weight_back, back_value)

    arrive_narrow(sent_g, LABELS, 2, inner_g, minus_g, plus_g, box_g)
    gather_field(field_g, inner_g, minus_g, plus_g, 2)

    def back_weight_at(y):
        def back_weight(number, p):
            return weight_back[number, p + 1, pl.ds(BASE + y, 8), :]

        return back_weight

    for y in (-1, 1):
        sums = message(back_weight_at(y), field_g, (-1, 0, 1, 2), y)
        for p in (-1, 0, 1, 2):
            current = field_2[1, :, p + 2, pl.ds(BASE + y, 8), :]
            grad_p = -softmax_back(current, sums[p])
            rim_p[:, p + 1, pl.ds(BASE + y, 8), :] = grad_p
            put_field(field_h, p, y, mix(backward, grad_p))

    sums = message(back_weight_at(0), field_h, (0, 1), 0)
    grads_1 = []
    values_1 = []
    for p in (0, 1):
        current = field_1[1, :, p + 2, pl.ds(BASE, 8), :]
        step = softmax_back(current, sums[p])
        total_u[:, p] = total_u[:, p] + step
        grads_1.append(-step)
        values_1.append(mix(backward, -step))
    sent_h = send_field(4, 1, values_1, inner_h, sides_h, minus_h, plus_h)

    grads_2 = [rim_p[:, p + 1, pl.ds(BASE, 8), :] for p in (0, 1)]
    for p in (0, 1):
        total_u[:, p] = total_u[:, p] - grads_2[p]
    add_compat(grads_2, [message_2[:, p + 1, pl.ds(BASE, 8), :] for p in (0, 1)], False)
    add_kernel([field_h[1, :, p + 2, pl.ds(BASE, 8), :] for p in (0, 1)], field_1, False)
    add_compat(grads_1, [message_1[:, p] for p in (0, 1)], False)
    add_kernel(values_1, field_0, False)

    local = jnp.zeros((8, 128), jnp.float32)
    for b in range(LABELS):
        total = jnp.sum(jnp.sum(total_c[b], axis=1), axis=1, keepdims=True)
        local = jnp.where(lane == 8 * b + sublane, total, local)
    joint_rows = []
    for number, (step_x, step_y, step_z) in enumerate(OFFSETS):
        row = None
        for p in (0, 1):
            mask = mask_x[p + step_x] * mask_own_y[step_y] * mask_z[step_z]
            joint = total_r[number, p] * mask
            total_r[number, p] = joint * strength[number]
            term = joint * inner_a[inner_rows(0, p, number, WIDE), :]
            row = term if row is None else row + term
        joint_rows.append(jnp.sum(row, axis=0, keepdims=True))
    for group in range(4):
        rows = joint_rows[8 * group : 8 * (group + 1)]
        rows = rows + [jnp.zeros((1, 128), jnp.float32)] * (8 - len(rows))
        total = jnp.sum(jnp.concatenate(rows, axis=0), axis=1, keepdims=True)
        local = jnp.where(lane == 8 * (LABELS + group) + sublane, total, local)

    gather_a[me_x] = jnp.sum(local, axis=0, keepdims=True)

    def to_peer(buffer, me, place_send, place_recv, device):
        return pltpu.make_async_remote_copy(
            src_ref=buffer.at[me],
            dst_ref=buffer.at[me],
            send_sem=peer_send.at[place_send],
            recv_sem=peer_recv.at[place_recv],
            device_id=device,
            device_id_type=MESH,
        )

    along_x = [to_peer(gather_a, me_x, step, 2 * step + core, odd[step]) for step in range(chips)]
    for step in sorted(range(1, chips), key=lambda step: -ring(step, chips)):
        along_x[step].start()

    @pl.when(core == 0)
    def _():
        along_x[0].start()

    def put_affinity(tile, x, value):
        affinity_out[x, :, 128 * tile : 128 * (tile + 1)] = value.astype(jnp.bfloat16)

    gather_columns(lambda number, p: total_r[number, p], NEIGH // 2, put_affinity)
    store_a = pltpu.make_async_copy(affinity_out, grad_affinity_hbm, store_sem.at[0])
    store_a.start()

    arrive(sent_h)
    gather_field(field_i, inner_h, minus_h, plus_h, 1)
    sums = message(back_weight_at(0), field_i, (0, 1), 0)
    for p in (0, 1):
        current = field_0[1, :, p + 2, pl.ds(BASE, 8), :]
        total_u[:, p] = total_u[:, p] + softmax_back(current, sums[p])

    def put_unary(tile, x, value):
        unary_out[x, :, 128 * tile : 128 * (tile + 1)] = value.astype(jnp.bfloat16)

    gather_columns(lambda label, p: total_u[label, p], LABELS // 2, put_unary)
    store_u = pltpu.make_async_copy(unary_out, grad_unary_hbm, store_sem.at[1])
    store_u.start()

    base = 2 * chips
    along_y = [
        to_peer(gather_b, me_y, base + place, base + place, device)
        for place, device in enumerate(peers_b)
    ]
    to_even = to_peer(last, 0, base + len(peers_b), base + len(peers_b), partner)

    @pl.when(core == 1)
    def _():
        for step in range(chips):
            for sender in (0, 1):
                if (step, sender) != (0, 1):
                    to_peer(gather_a, me_x, 0, 2 * step + sender, partner).wait_recv()
        total = gather_a[0]
        for place in range(1, size_gx):
            total = total + gather_a[place]
        gather_b[me_y] = total
        for copy in along_y:
            copy.start()
        for copy in along_y:
            copy.wait_recv()
        total = gather_b[0]
        for place in range(1, size_gy):
            total = total + gather_b[place]
        last[0] = total
        to_even.start()

    @pl.when(core == 0)
    def _():
        to_even.wait_recv()

    voxels = size_gx * 4 * size_gy * 8 * DEPTH
    final = last[0] * (1.0 / math.sqrt(voxels))
    grad_kernel[...] = pltpu.roll(final, 128 - LABELS * LABELS, 1)[:, :NEIGH]
    spaced = jnp.where(lax.rem(lane, 8) == sublane, jnp.broadcast_to(final, (8, 128)), 0.0)
    table = jnp.zeros((8, 128), jnp.float32)
    for b in range(LABELS):
        column = jnp.sum(jnp.where(lane // 8 == b, spaced, 0.0), axis=1, keepdims=True)
        table = jnp.where(lane == b, column, table)
    grad_compat[...] = table[:, :LABELS]

    for copy in sent_u + sent_a + sent_q + sent_g + sent_h + along_x[1:]:
        copy.wait_send()

    @pl.when(core == 0)
    def _():
        along_x[0].wait_send()

    @pl.when(core == 1)
    def _():
        for copy in along_y + [to_even]:
            copy.wait_send()

    store_a.wait()
    store_u.wait()


def hand_out(*refs):
    parts, results, held, sem = refs[:4], refs[4:8], refs[8:12], refs[12]
    inward = [
        pltpu.make_async_copy(part, hold, sem.at[0, number])
        for number, (part, hold) in enumerate(zip(parts, held))
    ]
    outward = [
        pltpu.make_async_copy(hold, result, sem.at[1, number])
        for number, (hold, result) in enumerate(zip(held, results))
    ]
    for copy in inward:
        copy.start()
    for came, copy in zip(inward, outward):
        came.wait()
        copy.start()
    for copy in outward:
        copy.wait()


def shards(sizes, unary_score, affinity, compatibility, kernel_weights, cotangent):
    size_gx, size_gy, size_far, size_near = sizes
    f32, bf16 = jnp.float32, jnp.bfloat16

    def rows(count, kind=f32):
        return pltpu.VMEM((count, 128), kind)

    def exchanged(width):
        return [
            rows(SPAN * 2 * width),
            rows(2 * 8 * width),
            rows(SPAN * width),
            rows(SPAN * width),
        ]

    def boxed(width, reach):
        return [
            rows(2 * reach * 2 * width, bf16),
            rows(2 * 8 * width, bf16),
            rows(2 * reach * 2 * width, bf16),
            rows(SPAN * width, bf16),
            rows(SPAN * width, bf16),
        ]

    field = pltpu.VMEM((3, LABELS, 6, TALL, 128), f32)
    pair = pltpu.VMEM((LABELS, 2, 8, 128), f32)
    rim = pltpu.VMEM((LABELS, 4, TALL, 128), f32)
    peers = size_gx + size_gy
    scratch = (
        [
            pltpu.VMEM(unary_score.shape, bf16),
            pltpu.VMEM(affinity.shape, bf16),
            pltpu.VMEM(cotangent.shape, bf16),
            pltpu.VMEM(unary_score.shape, bf16),
            pltpu.VMEM(affinity.shape, bf16),
            pltpu.SMEM(compatibility.shape, f32),
            pltpu.SMEM(kernel_weights.shape, f32),
        ]
        + exchanged(LABELS)
        + exchanged(WIDE)
        + boxed(LABELS, 1)
        + boxed(WIDE, 2)
        + boxed(LABELS, 2)
        + exchanged(LABELS)
        + exchanged(LABELS)
        + exchanged(LABELS)
        + [
            pltpu.VMEM((LABELS, 6, TALL, 128), f32),
            pair,
            field,
            field,
            field,
            field,
            field,
            field,
            pltpu.VMEM((NEIGH, 6, TALL, 128), f32),
            pltpu.VMEM((NEIGH, 2, 8, 128), f32),
            pltpu.VMEM((NEIGH, 4, TALL, 128), f32),
            pltpu.VMEM((NEIGH, 4, TALL, 128), f32),
            pair,
            rim,
            rim,
            pair,
            pltpu.VMEM((LABELS, LABELS, 8, 128), f32),
            pltpu.VMEM((NEIGH, 2, 8, 128), f32),
            pltpu.VMEM((size_gx, 1, 128), f32),
            pltpu.VMEM((size_gy, 1, 128), f32),
            pltpu.VMEM((1, 1, 128), f32),
            pltpu.SemaphoreType.DMA((5,)),
            pltpu.SemaphoreType.DMA((2,)),
            pltpu.SemaphoreType.DMA((5, 8)),
            pltpu.SemaphoreType.DMA((5, 8)),
            pltpu.SemaphoreType.DMA((peers,)),
            pltpu.SemaphoreType.DMA((peers,)),
        ]
    )
    anywhere = pl.BlockSpec(memory_space=pl.ANY)
    in_hbm = pl.BlockSpec(memory_space=pltpu.HBM)
    vectors = pl.BlockSpec(memory_space=pltpu.VMEM)
    grad_unary, grad_affinity, grad_compat, grad_kernel = pl.pallas_call(
        functools.partial(kernel, sizes),
        out_shape=(
            jax.ShapeDtypeStruct(unary_score.shape, bf16),
            jax.ShapeDtypeStruct(affinity.shape, bf16),
            jax.ShapeDtypeStruct((LABELS, LABELS), f32),
            jax.ShapeDtypeStruct((1, NEIGH), f32),
        ),
        in_specs=[in_hbm] * 5,
        out_specs=(anywhere, anywhere, vectors, vectors),
        scratch_shapes=scratch,
        compiler_params=pltpu.CompilerParams(
            collective_id=0, has_side_effects=True, vmem_limit_bytes=GRANT
        ),
        name="mean_field_backward",
    )(unary_score, affinity, cotangent, compatibility, kernel_weights)
    found = (grad_unary, grad_affinity, grad_compat, grad_kernel.reshape(NEIGH))
    return pl.pallas_call(
        hand_out,
        out_shape=tuple(jax.ShapeDtypeStruct(part.shape, part.dtype) for part in found),
        in_specs=[anywhere] * 4,
        out_specs=(in_hbm,) * 4,
        scratch_shapes=[pltpu.VMEM(part.shape, part.dtype) for part in found]
        + [pltpu.SemaphoreType.DMA((2, 4))],
        compiler_params=pltpu.CompilerParams(vmem_limit_bytes=GRANT),
        name="hand_out",
    )(*found)


def solution(mesh):
    size_gx, size_gy = mesh.shape["gx"], mesh.shape["gy"]
    size_near = 4 if size_gy % 4 == 0 else 1
    sizes = (size_gx, size_gy, size_gy // size_near, size_near)
    in_specs = (P("gx", "gy", None), P("gx", "gy", None), P(), P(), P("gx", "gy", None))
    out_specs = (P("gx", "gy", None), P("gx", "gy", None), P(), P())
    return jax.shard_map(
        functools.partial(shards, sizes),
        mesh=mesh,
        in_specs=in_specs,
        out_specs=out_specs,
        check_vma=False,
    )
```

```python
import functools
import math

import jax
import jax.numpy as jnp
from jax import lax
from jax.experimental import pallas as pl
from jax.experimental.pallas import tpu as pltpu
from jax.sharding import PartitionSpec as P

LABELS = 8
DEPTH = 64
NEIGH = 26
ITERS = 3

OFFSETS = [
    (step_x, step_y, step_z)
    for step_x in (-1, 0, 1)
    for step_y in (-1, 0, 1)
    for step_z in (-1, 0, 1)
    if (step_x, step_y, step_z) != (0, 0, 0)
]
NUMBER = {offset: number for number, offset in enumerate(OFFSETS)}

SPAN = 12
TALL = 24
BASE = 8
DIRECTIONS = [(-1, -1), (-1, 1), (1, -1), (1, 1), (0, -1), (0, 1), (-1, 0), (1, 0)]
WIDE = 32
GRANT = 64 * 1024 * 1024 - 65536
MESH = pl.DeviceIdType.MESH


def low_half():
    return lax.broadcasted_iota(jnp.int32, (8, 128), 1) < DEPTH


def swap(values):
    return pltpu.roll(values, DEPTH, values.ndim - 1)


def inner_rows(y, p, label, width):
    return pl.ds(((y + 2) * 2 + p) * width + label, 8, stride=2 * width)


def side_rows(y, label, width):
    return pl.ds((y + 2) * width + label, 8, stride=width)


def spread(source, tiles, put):
    low = low_half()
    for tile in range(tiles):
        cols = [
            source[x, :, 128 * tile : 128 * (tile + 1)].astype(jnp.float32) for x in range(4)
        ]
        turned = [swap(col) for col in cols]
        for p in (0, 1):
            put(2 * tile, p, jnp.where(low, cols[p], turned[p + 2]))
            put(2 * tile + 1, p, jnp.where(low, turned[p], cols[p + 2]))


def gather_columns(values, tiles, put):
    low = low_half()
    for tile in range(tiles):
        for p in (0, 1):
            even, odd = values(2 * tile, p), values(2 * tile + 1, p)
            put(tile, p, jnp.where(low, even, swap(odd)))
            put(tile, p + 2, jnp.where(low, swap(even), odd))


def lay_out(inner, sides, width, label, first, second):
    low = low_half()
    inner[inner_rows(0, 0, label, width), :] = first
    inner[inner_rows(0, 1, label, width), :] = second
    sides[pl.ds(label, 8, stride=width), :] = jnp.where(low, first, swap(second))
    sides[pl.ds(8 * width + label, 8, stride=width), :] = jnp.where(low, swap(first), second)


def assemble(inner, minus, plus, width, label, y, reach):
    low = low_half()
    own = [inner[inner_rows(y, p, label, width), :] for p in (0, 1)]
    before = minus[side_rows(y, label, width), :]
    after = plus[side_rows(y, label, width), :]
    found = {0: own[0], 1: own[1]}
    found[2] = swap(jnp.where(low, after, own[0]))
    found[-1] = swap(jnp.where(low, own[1], before))
    if reach == 2:
        found[3] = jnp.where(low, swap(own[1]), after)
        found[-2] = jnp.where(low, before, swap(own[0]))
    return found


def message(weight, field, columns, y):
    sums = {p: None for p in columns}
    for step_y in (-1, 0, 1):
        for step_z in (-1, 0, 1):
            for source in range(min(columns) - 1, max(columns) + 2):
                users = [
                    (source - step_x, NUMBER[(step_x, step_y, step_z)])
                    for step_x in (-1, 0, 1)
                    if source - step_x in sums and (step_x, step_y, step_z) in NUMBER
                ]
                if not users:
                    continue
                near = field[step_z + 1, :, source + 2, pl.ds(BASE + y + step_y, 8), :]
                for p, number in users:
                    term = weight(number, p)[None] * near
                    sums[p] = term if sums[p] is None else sums[p] + term
    return sums


def mix(coef, values):
    rows = []
    for a in range(LABELS):
        total = coef(a, 0) * values[0]
        for b in range(1, LABELS):
            total = total + coef(a, b) * values[b]
        rows.append(total)
    return jnp.stack(rows)


def normalise(logits):
    powers = jnp.exp(logits - jnp.max(logits, axis=0, keepdims=True))
    return powers / jnp.sum(powers, axis=0, keepdims=True)


def softmax_back(current, grad_in):
    return current * (grad_in - jnp.sum(current * grad_in, axis=0, keepdims=True))


def put_shifts(field, p, y, values):
    field[0, :, p + 2, pl.ds(BASE + y, 8), :] = pltpu.roll(values, 1, 2)
    field[2, :, p + 2, pl.ds(BASE + y, 8), :] = pltpu.roll(values, 127, 2)


def put_field(field, p, y, values):
    field[1, :, p + 2, pl.ds(BASE + y, 8), :] = values
    put_shifts(field, p, y, values)


def rim_tiles(reach):
    return range(-reach, 2 + reach), (-2, 2) if reach == 2 else (-1, 1)


def gather_field(field, inner, minus, plus, reach):
    columns, starts = rim_tiles(reach)
    for label in range(LABELS):
        for y in starts:
            found = assemble(inner, minus, plus, LABELS, label, y, reach)
            for p in columns:
                field[1, label, p + 2, pl.ds(BASE + y, 8), :] = found[p]
    for y in starts:
        for p in columns:
            put_shifts(field, p, y, field[1, :, p + 2, pl.ds(BASE + y, 8), :])


def kernel(
    sizes,
    unary_hbm,
    affinity_hbm,
    cotangent_hbm,
    compat_hbm,
    strength_hbm,
    grad_unary_hbm,
    grad_affinity_hbm,
    grad_compat,
    grad_kernel,
    unary_in,
    affinity_in,
    cotangent_in,
    unary_out,
    affinity_out,
    compat,
    strength,
    inner_u,
    sides_u,
    minus_u,
    plus_u,
    inner_a,
    sides_a,
    minus_a,
    plus_a,
    *rest,
):
    boxes, rest = rest[:15], rest[15:]
    box_u, box_a, box_g = boxes[:5], boxes[5:10], boxes[10:]
    (
        inner_q,
        sides_q,
        minus_q,
        plus_q,
        inner_g,
        sides_g,
        minus_g,
        plus_g,
        inner_h,
        sides_h,
        minus_h,
        plus_h,
        logits,
        own_grad,
        field_0,
        field_1,
        field_2,
        field_g,
        field_h,
        field_i,
        wide_aff,
        weight_own,
        weight_rim,
        weight_back,
        message_1,
        message_2,
        rim_p,
        total_u,
        total_c,
        total_r,
        gather_a,
        gather_b,
        last,
        load_sem,
        store_sem,
        halo_send,
        halo_recv,
        peer_send,
        peer_recv,
        meet_sem,
    ) = rest
    size_gx, size_gy, size_far, size_near = sizes
    me_x, me_y = lax.axis_index("gx"), lax.axis_index("gy")
    me_far, me_near = me_y // size_near, lax.rem(me_y, size_near)
    chips = size_gx // 2
    chip, core = me_x // 2, lax.rem(me_x, 2)
    low = low_half()

    def around(index, step, size):
        return lax.rem(index + (step + size), size)

    loads = [
        pltpu.make_async_copy(unary_hbm, unary_in, load_sem.at[0]),
        pltpu.make_async_copy(affinity_hbm, affinity_in, load_sem.at[1]),
        pltpu.make_async_copy(cotangent_hbm, cotangent_in, load_sem.at[2]),
        pltpu.make_async_copy(strength_hbm, strength, load_sem.at[3]),
        pltpu.make_async_copy(compat_hbm, compat, load_sem.at[4]),
    ]
    for load in loads:
        load.start()

    neighbours = [
        (around(me_x, step_x, size_gx), around(me_y, step_y, size_gy))
        for step_x, step_y in DIRECTIONS
    ]
    partner = (me_x + 1 - 2 * core, me_y)
    odd = [(2 * around(chip, step, chips) + 1, me_y) for step in range(chips)]
    even = [(2 * around(chip, step, chips), me_y) for step in range(chips)]

    def ring(step, size):
        return min(step, size - step)

    hops = sorted(
        [(far, near) for far in range(size_far) for near in range(size_near)][1:],
        key=lambda hop: -ring(hop[0], size_far) - ring(hop[1], size_near),
    )
    peers_b = [
        (me_x, around(me_far, far, size_far) * size_near + around(me_near, near, size_near))
        for far, near in hops
    ]
    barrier = pltpu.get_barrier_semaphore()

    def greet(devices):
        for device in devices:
            pl.semaphore_signal(barrier, inc=1, device_id=device, device_id_type=MESH)

    greet(neighbours)

    rounds = [doubling(size_gx), doubling(size_gy)]

    def meet(stage):
        for axis in (0, 1):
            if 0 < stage <= len(rounds[axis]):
                pl.semaphore_wait(meet_sem.at[axis, stage - 1], 2)
        for axis in (0, 1):
            if stage < len(rounds[axis]):
                step = rounds[axis][stage]
                for by in (-step, step):
                    device = (
                        (around(me_x, by, size_gx), me_y)
                        if axis == 0
                        else (me_x, around(me_y, by, size_gy))
                    )
                    pl.semaphore_signal(
                        meet_sem.at[axis, stage], inc=1, device_id=device, device_id_type=MESH
                    )

    def exchange(number, width, reach, inner, sides, minus, plus):
        copies = []
        for d, (step_x, step_y) in enumerate(DIRECTIONS):
            if step_x == 0:
                first = 2 if step_y < 0 else 10 - reach
                land = 10 if step_y < 0 else 2 - reach
                source = inner.at[pl.ds(first * 2 * width, reach * 2 * width), :]
                target = inner.at[pl.ds(land * 2 * width, reach * 2 * width), :]
            else:
                base = 0 if step_x < 0 else 8 * width
                landing = plus if step_x < 0 else minus
                if step_y == 0:
                    source = sides.at[pl.ds(base, 8 * width), :]
                    target = landing.at[pl.ds(2 * width, 8 * width), :]
                else:
                    first = 0 if step_y < 0 else 8 - reach
                    land = 10 if step_y < 0 else 2 - reach
                    source = sides.at[pl.ds(base + first * width, reach * width), :]
                    target = landing.at[pl.ds(land * width, reach * width), :]
            copies.append(remote(number, d, source, target))
        for copy in copies:
            copy.start()
        return copies

    def remote(number, d, source, target):
        return pltpu.make_async_remote_copy(
            src_ref=source,
            dst_ref=target,
            send_sem=halo_send.at[number, d],
            recv_sem=halo_recv.at[number, d],
            device_id=neighbours[d],
            device_id_type=MESH,
        )

    def arrive(copies):
        for copy in copies:
            copy.wait_recv()

    def narrow(width, reach, inner, sides, box):
        inner_send, sides_send = box[:2]
        part = reach * 2 * width
        for place, first in enumerate((2, 10 - reach)):
            rows = inner[pl.ds(first * 2 * width, part), :]
            inner_send[pl.ds(place * part, part), :] = rows.astype(jnp.bfloat16)
        sides_send[...] = sides[...].astype(jnp.bfloat16)

    def start_narrow(number, reach, box):
        inner_send, sides_send, inner_recv, minus_recv, plus_recv = box
        width = sides_send.shape[0] // 16
        part = reach * 2 * width
        copies = []
        for d, (step_x, step_y) in enumerate(DIRECTIONS):
            if step_x == 0:
                rows = pl.ds(0 if step_y < 0 else part, part)
                source, target = inner_send.at[rows, :], inner_recv.at[rows, :]
            else:
                start = 0 if step_x < 0 else 8 * width
                landing = plus_recv if step_x < 0 else minus_recv
                if step_y == 0:
                    source = sides_send.at[pl.ds(start, 8 * width), :]
                    target = landing.at[pl.ds(2 * width, 8 * width), :]
                else:
                    first = 0 if step_y < 0 else 6
                    land = 10 if step_y < 0 else 0
                    source = sides_send.at[pl.ds(start + first * width, 2 * width), :]
                    target = landing.at[pl.ds(land * width, 2 * width), :]
            copies.append(remote(number, d, source, target))
        for copy in copies:
            copy.start()
        return copies

    def arrive_narrow(copies, width, reach, inner, minus, plus, box):
        inner_recv, minus_recv, plus_recv = box[2:]
        part = reach * 2 * width
        arrive(copies)
        for place, land in enumerate((10, 2 - reach)):
            rows = inner_recv[pl.ds(place * part, part), :]
            inner[pl.ds(land * 2 * width, part), :] = rows.astype(jnp.float32)
        minus[...] = minus_recv[...].astype(jnp.float32)
        plus[...] = plus_recv[...].astype(jnp.float32)

    lane = lax.broadcasted_iota(jnp.int32, (8, 128), 1)
    depth = lax.rem(lane, DEPTH)
    half = lane // DEPTH
    sublane = lax.broadcasted_iota(jnp.int32, (8, 128), 0)

    def inside(position, size):
        return jnp.where((position >= 0) & (position < size), 1.0, 0.0)

    mask_z = {step: inside(depth + step, DEPTH) for step in (-1, 0, 1)}
    mask_x = {at: inside(me_x * 4 + at + 2 * half, 4 * size_gx) for at in range(-2, 4)}

    def mask_y(y):
        return inside(me_y * 8 + y + sublane, 8 * size_gy)

    loads[0].wait()
    held = {}

    def keep(label, p, value):
        held[(label, p)] = value
        logits[label, p + 2, pl.ds(BASE, 8), :] = value
        if p == 1:
            lay_out(inner_u, sides_u, LABELS, label, held[(label, 0)], value)

    spread(unary_in, 4, keep)

    loads[1].wait()
    loads[3].wait()
    loads[4].wait()
    mask_own_y = {step: mask_y(step) for step in (-1, 0, 1)}

    def keep_affinity(number, p, value):
        held[(number, p)] = value
        step_x, step_y, step_z = OFFSETS[number]
        mask = mask_x[p + step_x] * mask_own_y[step_y] * mask_z[step_z]
        weight_own[number, p] = value * mask * strength[number]
        if p == 1:
            lay_out(inner_a, sides_a, WIDE, number, held[(number, 0)], value)

    spread(affinity_in, NEIGH // 2, keep_affinity)
    nothing = jnp.zeros((8, 128), jnp.float32)
    for number in range(NEIGH, WIDE):
        lay_out(inner_a, sides_a, WIDE, number, nothing, nothing)
    narrow(LABELS, 1, inner_u, sides_u, box_u)
    narrow(WIDE, 2, inner_a, sides_a, box_a)
    pl.semaphore_wait(barrier, len(neighbours))
    meet(0)
    sent_u = start_narrow(0, 1, box_u)
    sent_a = start_narrow(1, 2, box_a)

    arrive_narrow(sent_u, LABELS, 1, inner_u, minus_u, plus_u, box_u)
    meet(1)
    for label in range(LABELS):
        for y in (-1, 1):
            found = assemble(inner_u, minus_u, plus_u, LABELS, label, y, 1)
            for p in (-1, 0, 1, 2):
                logits[label, p + 2, pl.ds(BASE + y, 8), :] = found[p]
    for y in (-1, 1):
        for p in (-1, 0, 1, 2):
            value = normalise(logits[:, p + 2, pl.ds(BASE + y, 8), :])
            put_field(field_0, p, y, value)

    def own_logits(p):
        return logits[:, p + 2, pl.ds(BASE, 8), :]

    def own_weight(number, p):
        return weight_own[number, p]

    def forward(a, b):
        return compat[a, b]

    def backward(b, a):
        return compat[a, b]

    def lay_field(values, inner, sides):
        for label in range(LABELS):
            lay_out(inner, sides, LABELS, label, values[0][label], values[1][label])

    def send_field(number, reach, values, inner, sides, minus, plus):
        lay_field(values, inner, sides)
        return exchange(number, LABELS, reach, inner, sides, minus, plus)

    sums = message(own_weight, field_0, (0, 1), 0)
    values = []
    for p in (0, 1):
        message_1[:, p] = sums[p]
        values.append(normalise(own_logits(p) - mix(forward, sums[p])))
    sent_q = send_field(2, 2, values, inner_q, sides_q, minus_q, plus_q)

    loads[2].wait()

    def keep_cotangent(label, p, value):
        own_grad[label, p] = value

    spread(cotangent_in, 4, keep_cotangent)
    arrive_narrow(sent_a, WIDE, 2, inner_a, minus_a, plus_a, box_a)
    for number in range(NEIGH):
        for y in (-2, 2):
            found = assemble(inner_a, minus_a, plus_a, WIDE, number, y, 2)
            for p in range(-2, 4):
                wide_aff[number, p + 2, pl.ds(BASE + y, 8), :] = found[p] * strength[number]
    rim_mask_y = {y: mask_y(y) for y in (-2, -1, 0, 1, 2)}

    def rim_weights(target, value):
        for y in (-1, 1):
            for p in (-1, 0, 1, 2):
                for number, (step_x, step_y, step_z) in enumerate(OFFSETS):
                    across = mask_x[p + step_x] * rim_mask_y[y + step_y]
                    if step_z != 0:
                        across = across * mask_z[step_z]
                    target[number, p + 1, pl.ds(BASE + y, 8), :] = across * value(number, p, y)

    def rim_value(number, p, y):
        return wide_aff[number, p + 2, pl.ds(BASE + y, 8), :]

    def back_value(number, p, y):
        step_x, step_y, step_z = OFFSETS[number]
        opposite = NUMBER[(-step_x, -step_y, -step_z)]
        value = wide_aff[opposite, p + step_x + 2, pl.ds(BASE + y + step_y, 8), :]
        if step_z != 0:
            value = pltpu.roll(value, (128 - step_z) % 128, 1)
        return value

    rim_weights(weight_rim, rim_value)

    arrive(sent_q)
    meet(2)
    gather_field(field_1, inner_q, minus_q, plus_q, 2)
    for y in (-1, 1):

        def rim_weight(number, p, y=y):
            return weight_rim[number, p + 1, pl.ds(BASE + y, 8), :]

        sums = message(rim_weight, field_1, (-1, 0, 1, 2), y)
        for p in (-1, 0, 1, 2):
            message_2[:, p + 1, pl.ds(BASE + y, 8), :] = sums[p]
            here = logits[:, p + 2, pl.ds(BASE + y, 8), :]
            put_field(field_2, p, y, normalise(here - mix(forward, sums[p])))

    sums = message(own_weight, field_2, (0, 1), 0)
    grads = []
    values = []
    for p in (0, 1):
        current = normalise(own_logits(p) - mix(forward, sums[p]))
        step = softmax_back(current, own_grad[:, p])
        total_u[:, p] = step
        grads.append(-step)
        values.append(mix(backward, -step))
    lay_field(values, inner_g, sides_g)
    narrow(LABELS, 2, inner_g, sides_g, box_g)
    sent_g = start_narrow(3, 2, box_g)

    def add_compat(grads, messages, begin):
        for b in range(LABELS):
            term = grads[0] * messages[0][b][None] + grads[1] * messages[1][b][None]
            total_c[b] = term if begin else total_c[b] + term

    def add_kernel(values, field, begin):
        for number, (step_x, step_y, step_z) in enumerate(OFFSETS):
            for p in (0, 1):
                near = field[step_z + 1, :, p + step_x + 2, pl.ds(BASE + step_y, 8), :]
                joint = jnp.sum(values[p] * near, axis=0)
                total_r[number, p] = joint if begin else total_r[number, p] + joint

    add_compat(grads, [sums[0], sums[1]], True)
    add_kernel(values, field_2, True)
    rim_weights(weight_back, back_value)

    arrive_narrow(sent_g, LABELS, 2, inner_g, minus_g, plus_g, box_g)
    meet(3)
    gather_field(field_g, inner_g, minus_g, plus_g, 2)

    def back_weight_at(y):
        def back_weight(number, p):
            return weight_back[number, p + 1, pl.ds(BASE + y, 8), :]

        return back_weight

    for y in (-1, 1):
        sums = message(back_weight_at(y), field_g, (-1, 0, 1, 2), y)
        for p in (-1, 0, 1, 2):
            current = field_2[1, :, p + 2, pl.ds(BASE + y, 8), :]
            grad_p = -softmax_back(current, sums[p])
            rim_p[:, p + 1, pl.ds(BASE + y, 8), :] = grad_p
            put_field(field_h, p, y, mix(backward, grad_p))

    sums = message(back_weight_at(0), field_h, (0, 1), 0)
    grads_1 = []
    values_1 = []
    for p in (0, 1):
        current = field_1[1, :, p + 2, pl.ds(BASE, 8), :]
        step = softmax_back(current, sums[p])
        total_u[:, p] = total_u[:, p] + step
        grads_1.append(-step)
        values_1.append(mix(backward, -step))
    sent_h = send_field(4, 1, values_1, inner_h, sides_h, minus_h, plus_h)

    grads_2 = [rim_p[:, p + 1, pl.ds(BASE, 8), :] for p in (0, 1)]
    for p in (0, 1):
        total_u[:, p] = total_u[:, p] - grads_2[p]
    add_compat(grads_2, [message_2[:, p + 1, pl.ds(BASE, 8), :] for p in (0, 1)], False)
    add_kernel([field_h[1, :, p + 2, pl.ds(BASE, 8), :] for p in (0, 1)], field_1, False)
    add_compat(grads_1, [message_1[:, p] for p in (0, 1)], False)
    add_kernel(values_1, field_0, False)

    local = jnp.zeros((8, 128), jnp.float32)
    for b in range(LABELS):
        total = jnp.sum(jnp.sum(total_c[b], axis=1), axis=1, keepdims=True)
        local = jnp.where(lane == 8 * b + sublane, total, local)
    joint_rows = []
    for number, (step_x, step_y, step_z) in enumerate(OFFSETS):
        row = None
        for p in (0, 1):
            mask = mask_x[p + step_x] * mask_own_y[step_y] * mask_z[step_z]
            joint = total_r[number, p] * mask
            total_r[number, p] = joint * strength[number]
            term = joint * inner_a[inner_rows(0, p, number, WIDE), :]
            row = term if row is None else row + term
        joint_rows.append(jnp.sum(row, axis=0, keepdims=True))
    for group in range(4):
        rows = joint_rows[8 * group : 8 * (group + 1)]
        rows = rows + [jnp.zeros((1, 128), jnp.float32)] * (8 - len(rows))
        total = jnp.sum(jnp.concatenate(rows, axis=0), axis=1, keepdims=True)
        local = jnp.where(lane == 8 * (LABELS + group) + sublane, total, local)

    gather_a[me_x] = jnp.sum(local, axis=0, keepdims=True)

    def to_peer(buffer, me, place_send, place_recv, device):
        return pltpu.make_async_remote_copy(
            src_ref=buffer.at[me],
            dst_ref=buffer.at[me],
            send_sem=peer_send.at[place_send],
            recv_sem=peer_recv.at[place_recv],
            device_id=device,
            device_id_type=MESH,
        )

    along_x = [to_peer(gather_a, me_x, step, 2 * step + core, odd[step]) for step in range(chips)]
    for step in sorted(range(1, chips), key=lambda step: -ring(step, chips)):
        along_x[step].start()

    @pl.when(core == 0)
    def _():
        along_x[0].start()

    def put_affinity(tile, x, value):
        affinity_out[x, :, 128 * tile : 128 * (tile + 1)] = value.astype(jnp.bfloat16)

    gather_columns(lambda number, p: total_r[number, p], NEIGH // 2, put_affinity)
    store_a = pltpu.make_async_copy(affinity_out, grad_affinity_hbm, store_sem.at[0])
    store_a.start()

    arrive(sent_h)
    meet(4)
    gather_field(field_i, inner_h, minus_h, plus_h, 1)
    sums = message(back_weight_at(0), field_i, (0, 1), 0)
    for p in (0, 1):
        current = field_0[1, :, p + 2, pl.ds(BASE, 8), :]
        total_u[:, p] = total_u[:, p] + softmax_back(current, sums[p])

    def put_unary(tile, x, value):
        unary_out[x, :, 128 * tile : 128 * (tile + 1)] = value.astype(jnp.bfloat16)

    gather_columns(lambda label, p: total_u[label, p], LABELS // 2, put_unary)
    store_u = pltpu.make_async_copy(unary_out, grad_unary_hbm, store_sem.at[1])
    store_u.start()

    base = 2 * chips
    along_y = [
        to_peer(gather_b, me_y, base + place, base + place, device)
        for place, device in enumerate(peers_b)
    ]
    to_even = to_peer(last, 0, base + len(peers_b), base + len(peers_b), partner)

    @pl.when(core == 1)
    def _():
        for step in range(chips):
            for sender in (0, 1):
                if (step, sender) != (0, 1):
                    to_peer(gather_a, me_x, 0, 2 * step + sender, partner).wait_recv()
        total = gather_a[0]
        for place in range(1, size_gx):
            total = total + gather_a[place]
        gather_b[me_y] = total
        for copy in along_y:
            copy.start()
        for copy in along_y:
            copy.wait_recv()
        total = gather_b[0]
        for place in range(1, size_gy):
            total = total + gather_b[place]
        last[0] = total
        to_even.start()

    @pl.when(core == 0)
    def _():
        to_even.wait_recv()

    voxels = size_gx * 4 * size_gy * 8 * DEPTH
    final = last[0] * (1.0 / math.sqrt(voxels))
    grad_kernel[...] = pltpu.roll(final, 128 - LABELS * LABELS, 1)[:, :NEIGH]
    spaced = jnp.where(lax.rem(lane, 8) == sublane, jnp.broadcast_to(final, (8, 128)), 0.0)
    table = jnp.zeros((8, 128), jnp.float32)
    for b in range(LABELS):
        column = jnp.sum(jnp.where(lane // 8 == b, spaced, 0.0), axis=1, keepdims=True)
        table = jnp.where(lane == b, column, table)
    grad_compat[...] = table[:, :LABELS]

    for copy in sent_u + sent_a + sent_q + sent_g + sent_h + along_x[1:]:
        copy.wait_send()

    @pl.when(core == 0)
    def _():
        along_x[0].wait_send()

    @pl.when(core == 1)
    def _():
        for copy in along_y + [to_even]:
            copy.wait_send()

    store_a.wait()
    store_u.wait()


def doubling(size):
    steps, reach = [], 1
    while reach < size // 2:
        steps.append(reach)
        reach *= 2
    return steps


def hand_out(*refs):
    parts, results, held, sem = refs[:4], refs[4:8], refs[8:12], refs[12]
    inward = [
        pltpu.make_async_copy(part, hold, sem.at[0, number])
        for number, (part, hold) in enumerate(zip(parts, held))
    ]
    outward = [
        pltpu.make_async_copy(hold, result, sem.at[1, number])
        for number, (hold, result) in enumerate(zip(held, results))
    ]
    for copy in inward:
        copy.start()
    for came, copy in zip(inward, outward):
        came.wait()
        copy.start()
    for copy in outward:
        copy.wait()


def shards(sizes, unary_score, affinity, compatibility, kernel_weights, cotangent):
    size_gx, size_gy, size_far, size_near = sizes
    f32, bf16 = jnp.float32, jnp.bfloat16

    def rows(count, kind=f32):
        return pltpu.VMEM((count, 128), kind)

    def exchanged(width):
        return [
            rows(SPAN * 2 * width),
            rows(2 * 8 * width),
            rows(SPAN * width),
            rows(SPAN * width),
        ]

    def boxed(width, reach):
        return [
            rows(2 * reach * 2 * width, bf16),
            rows(2 * 8 * width, bf16),
            rows(2 * reach * 2 * width, bf16),
            rows(SPAN * width, bf16),
            rows(SPAN * width, bf16),
        ]

    field = pltpu.VMEM((3, LABELS, 6, TALL, 128), f32)
    pair = pltpu.VMEM((LABELS, 2, 8, 128), f32)
    rim = pltpu.VMEM((LABELS, 4, TALL, 128), f32)
    peers = size_gx + size_gy
    scratch = (
        [
            pltpu.VMEM(unary_score.shape, bf16),
            pltpu.VMEM(affinity.shape, bf16),
            pltpu.VMEM(cotangent.shape, bf16),
            pltpu.VMEM(unary_score.shape, bf16),
            pltpu.VMEM(affinity.shape, bf16),
            pltpu.SMEM(compatibility.shape, f32),
            pltpu.SMEM(kernel_weights.shape, f32),
        ]
        + exchanged(LABELS)
        + exchanged(WIDE)
        + boxed(LABELS, 1)
        + boxed(WIDE, 2)
        + boxed(LABELS, 2)
        + exchanged(LABELS)
        + exchanged(LABELS)
        + exchanged(LABELS)
        + [
            pltpu.VMEM((LABELS, 6, TALL, 128), f32),
            pair,
            field,
            field,
            field,
            field,
            field,
            field,
            pltpu.VMEM((NEIGH, 6, TALL, 128), f32),
            pltpu.VMEM((NEIGH, 2, 8, 128), f32),
            pltpu.VMEM((NEIGH, 4, TALL, 128), f32),
            pltpu.VMEM((NEIGH, 4, TALL, 128), f32),
            pair,
            rim,
            rim,
            pair,
            pltpu.VMEM((LABELS, LABELS, 8, 128), f32),
            pltpu.VMEM((NEIGH, 2, 8, 128), f32),
            pltpu.VMEM((size_gx, 1, 128), f32),
            pltpu.VMEM((size_gy, 1, 128), f32),
            pltpu.VMEM((1, 1, 128), f32),
            pltpu.SemaphoreType.DMA((5,)),
            pltpu.SemaphoreType.DMA((2,)),
            pltpu.SemaphoreType.DMA((5, 8)),
            pltpu.SemaphoreType.DMA((5, 8)),
            pltpu.SemaphoreType.DMA((peers,)),
            pltpu.SemaphoreType.DMA((peers,)),
            pltpu.SemaphoreType.REGULAR((2, 4)),
        ]
    )
    anywhere = pl.BlockSpec(memory_space=pl.ANY)
    in_hbm = pl.BlockSpec(memory_space=pltpu.HBM)
    vectors = pl.BlockSpec(memory_space=pltpu.VMEM)
    grad_unary, grad_affinity, grad_compat, grad_kernel = pl.pallas_call(
        functools.partial(kernel, sizes),
        out_shape=(
            jax.ShapeDtypeStruct(unary_score.shape, bf16),
            jax.ShapeDtypeStruct(affinity.shape, bf16),
            jax.ShapeDtypeStruct((LABELS, LABELS), f32),
            jax.ShapeDtypeStruct((1, NEIGH), f32),
        ),
        in_specs=[in_hbm] * 5,
        out_specs=(anywhere, anywhere, vectors, vectors),
        scratch_shapes=scratch,
        compiler_params=pltpu.CompilerParams(
            collective_id=0, has_side_effects=True, vmem_limit_bytes=GRANT
        ),
        name="mean_field_backward",
    )(unary_score, affinity, cotangent, compatibility, kernel_weights)
    found = (grad_unary, grad_affinity, grad_compat, grad_kernel.reshape(NEIGH))
    return pl.pallas_call(
        hand_out,
        out_shape=tuple(jax.ShapeDtypeStruct(part.shape, part.dtype) for part in found),
        in_specs=[anywhere] * 4,
        out_specs=(in_hbm,) * 4,
        scratch_shapes=[pltpu.VMEM(part.shape, part.dtype) for part in found]
        + [pltpu.SemaphoreType.DMA((2, 4))],
        compiler_params=pltpu.CompilerParams(vmem_limit_bytes=GRANT),
        name="hand_out",
    )(*found)


def solution(mesh):
    size_gx, size_gy = mesh.shape["gx"], mesh.shape["gy"]
    size_near = 4 if size_gy % 4 == 0 else 1
    sizes = (size_gx, size_gy, size_gy // size_near, size_near)
    in_specs = (P("gx", "gy", None), P("gx", "gy", None), P(), P(), P("gx", "gy", None))
    out_specs = (P("gx", "gy", None), P("gx", "gy", None), P(), P())
    return jax.shard_map(
        functools.partial(shards, sizes),
        mesh=mesh,
        in_specs=in_specs,
        out_specs=out_specs,
        check_vma=False,
    )
```

```python
import functools
import math

import jax
import jax.numpy as jnp
from jax import lax
from jax.experimental import pallas as pl
from jax.experimental.pallas import tpu as pltpu
from jax.sharding import PartitionSpec as P

LABELS = 8
DEPTH = 64
NEIGH = 26
ITERS = 3

OFFSETS = [
    (step_x, step_y, step_z)
    for step_x in (-1, 0, 1)
    for step_y in (-1, 0, 1)
    for step_z in (-1, 0, 1)
    if (step_x, step_y, step_z) != (0, 0, 0)
]
NUMBER = {offset: number for number, offset in enumerate(OFFSETS)}

SPAN = 12
TALL = 24
BASE = 8
DIRECTIONS = [(-1, -1), (-1, 1), (1, -1), (1, 1), (0, -1), (0, 1), (-1, 0), (1, 0)]
WIDE = 32
GRANT = 64 * 1024 * 1024 - 65536
MESH = pl.DeviceIdType.MESH


def low_half():
    return lax.broadcasted_iota(jnp.int32, (8, 128), 1) < DEPTH


def swap(values):
    return pltpu.roll(values, DEPTH, values.ndim - 1)


def inner_rows(y, p, label, width):
    return pl.ds(((y + 2) * 2 + p) * width + label, 8, stride=2 * width)


def side_rows(y, label, width):
    return pl.ds((y + 2) * width + label, 8, stride=width)


def spread(source, tiles, put):
    low = low_half()
    for tile in range(tiles):
        cols = [
            source[x, :, 128 * tile : 128 * (tile + 1)].astype(jnp.float32) for x in range(4)
        ]
        turned = [swap(col) for col in cols]
        for p in (0, 1):
            put(2 * tile, p, jnp.where(low, cols[p], turned[p + 2]))
            put(2 * tile + 1, p, jnp.where(low, turned[p], cols[p + 2]))


def gather_columns(values, tiles, put):
    low = low_half()
    for tile in range(tiles):
        for p in (0, 1):
            even, odd = values(2 * tile, p), values(2 * tile + 1, p)
            put(tile, p, jnp.where(low, even, swap(odd)))
            put(tile, p + 2, jnp.where(low, swap(even), odd))


def lay_out(inner, sides, width, label, first, second):
    low = low_half()
    inner[inner_rows(0, 0, label, width), :] = first
    inner[inner_rows(0, 1, label, width), :] = second
    sides[pl.ds(label, 8, stride=width), :] = jnp.where(low, first, swap(second))
    sides[pl.ds(8 * width + label, 8, stride=width), :] = jnp.where(low, swap(first), second)


def assemble(inner, minus, plus, width, label, y, reach):
    low = low_half()
    own = [inner[inner_rows(y, p, label, width), :] for p in (0, 1)]
    before = minus[side_rows(y, label, width), :]
    after = plus[side_rows(y, label, width), :]
    found = {0: own[0], 1: own[1]}
    found[2] = swap(jnp.where(low, after, own[0]))
    found[-1] = swap(jnp.where(low, own[1], before))
    if reach == 2:
        found[3] = jnp.where(low, swap(own[1]), after)
        found[-2] = jnp.where(low, before, swap(own[0]))
    return found


def message(weight, field, columns, y):
    sums = {p: None for p in columns}
    for step_y in (-1, 0, 1):
        for step_z in (-1, 0, 1):
            for source in range(min(columns) - 1, max(columns) + 2):
                users = [
                    (source - step_x, NUMBER[(step_x, step_y, step_z)])
                    for step_x in (-1, 0, 1)
                    if source - step_x in sums and (step_x, step_y, step_z) in NUMBER
                ]
                if not users:
                    continue
                near = field[step_z + 1, :, source + 2, pl.ds(BASE + y + step_y, 8), :]
                for p, number in users:
                    term = weight(number, p)[None] * near
                    sums[p] = term if sums[p] is None else sums[p] + term
    return sums


def mix(coef, values):
    rows = []
    for a in range(LABELS):
        total = coef(a, 0) * values[0]
        for b in range(1, LABELS):
            total = total + coef(a, b) * values[b]
        rows.append(total)
    return jnp.stack(rows)


def normalise(logits):
    powers = jnp.exp(logits - jnp.max(logits, axis=0, keepdims=True))
    return powers / jnp.sum(powers, axis=0, keepdims=True)


def softmax_back(current, grad_in):
    return current * (grad_in - jnp.sum(current * grad_in, axis=0, keepdims=True))


def put_shifts(field, p, y, values):
    field[0, :, p + 2, pl.ds(BASE + y, 8), :] = pltpu.roll(values, 1, 2)
    field[2, :, p + 2, pl.ds(BASE + y, 8), :] = pltpu.roll(values, 127, 2)


def put_field(field, p, y, values):
    field[1, :, p + 2, pl.ds(BASE + y, 8), :] = values
    put_shifts(field, p, y, values)


def rim_tiles(reach):
    return range(-reach, 2 + reach), (-2, 2) if reach == 2 else (-1, 1)


def gather_field(field, inner, minus, plus, reach):
    columns, starts = rim_tiles(reach)
    for label in range(LABELS):
        for y in starts:
            found = assemble(inner, minus, plus, LABELS, label, y, reach)
            for p in columns:
                field[1, label, p + 2, pl.ds(BASE + y, 8), :] = found[p]
    for y in starts:
        for p in columns:
            put_shifts(field, p, y, field[1, :, p + 2, pl.ds(BASE + y, 8), :])


def kernel(
    sizes,
    unary_hbm,
    affinity_hbm,
    cotangent_hbm,
    compat_hbm,
    strength_hbm,
    grad_unary_hbm,
    grad_affinity_hbm,
    grad_compat,
    grad_kernel,
    unary_in,
    affinity_in,
    cotangent_in,
    unary_out,
    affinity_out,
    compat,
    strength,
    inner_u,
    sides_u,
    minus_u,
    plus_u,
    inner_a,
    sides_a,
    minus_a,
    plus_a,
    *rest,
):
    boxes, rest = rest[:15], rest[15:]
    box_u, box_a, box_g = boxes[:5], boxes[5:10], boxes[10:]
    (
        inner_q,
        sides_q,
        minus_q,
        plus_q,
        inner_g,
        sides_g,
        minus_g,
        plus_g,
        inner_h,
        sides_h,
        minus_h,
        plus_h,
        logits,
        own_grad,
        field_0,
        field_1,
        field_2,
        field_g,
        field_h,
        field_i,
        wide_aff,
        weight_own,
        weight_rim,
        weight_back,
        message_1,
        message_2,
        rim_p,
        total_u,
        total_c,
        total_r,
        gather_a,
        gather_b,
        last,
        load_sem,
        store_sem,
        halo_send,
        halo_recv,
        peer_send,
        peer_recv,
        meet_sem,
    ) = rest
    size_gx, size_gy, size_far, size_near = sizes
    me_x, me_y = lax.axis_index("gx"), lax.axis_index("gy")
    me_far, me_near = me_y // size_near, lax.rem(me_y, size_near)
    chips = size_gx // 2
    chip, core = me_x // 2, lax.rem(me_x, 2)
    low = low_half()

    def around(index, step, size):
        return lax.rem(index + (step + size), size)

    loads = [
        pltpu.make_async_copy(unary_hbm, unary_in, load_sem.at[0]),
        pltpu.make_async_copy(affinity_hbm, affinity_in, load_sem.at[1]),
        pltpu.make_async_copy(cotangent_hbm, cotangent_in, load_sem.at[2]),
        pltpu.make_async_copy(strength_hbm, strength, load_sem.at[3]),
        pltpu.make_async_copy(compat_hbm, compat, load_sem.at[4]),
    ]
    for load in loads:
        load.start()

    neighbours = [
        (around(me_x, step_x, size_gx), around(me_y, step_y, size_gy))
        for step_x, step_y in DIRECTIONS
    ]
    partner = (me_x + 1 - 2 * core, me_y)
    odd = [(2 * around(chip, step, chips) + 1, me_y) for step in range(chips)]
    even = [(2 * around(chip, step, chips), me_y) for step in range(chips)]

    def ring(step, size):
        return min(step, size - step)

    hops = sorted(
        [(far, near) for far in range(size_far) for near in range(size_near)][1:],
        key=lambda hop: -ring(hop[0], size_far) - ring(hop[1], size_near),
    )
    peers_b = [
        (me_x, around(me_far, far, size_far) * size_near + around(me_near, near, size_near))
        for far, near in hops
    ]
    barrier = pltpu.get_barrier_semaphore()

    def greet(devices):
        for device in devices:
            pl.semaphore_signal(barrier, inc=1, device_id=device, device_id_type=MESH)

    greet(neighbours)

    rounds = [doubling(size_gx), doubling(size_gy)]

    def meet(stage):
        for axis in (0, 1):
            if 0 < stage <= len(rounds[axis]):
                pl.semaphore_wait(meet_sem.at[axis, stage - 1], 2)
        for axis in (0, 1):
            if stage < len(rounds[axis]):
                step = rounds[axis][stage]
                for by in (-step, step):
                    device = (
                        (around(me_x, by, size_gx), me_y)
                        if axis == 0
                        else (me_x, around(me_y, by, size_gy))
                    )
                    pl.semaphore_signal(
                        meet_sem.at[axis, stage], inc=1, device_id=device, device_id_type=MESH
                    )

    def exchange(number, width, reach, inner, sides, minus, plus):
        copies = []
        for d, (step_x, step_y) in enumerate(DIRECTIONS):
            if step_x == 0:
                first = 2 if step_y < 0 else 10 - reach
                land = 10 if step_y < 0 else 2 - reach
                source = inner.at[pl.ds(first * 2 * width, reach * 2 * width), :]
                target = inner.at[pl.ds(land * 2 * width, reach * 2 * width), :]
            else:
                base = 0 if step_x < 0 else 8 * width
                landing = plus if step_x < 0 else minus
                if step_y == 0:
                    source = sides.at[pl.ds(base, 8 * width), :]
                    target = landing.at[pl.ds(2 * width, 8 * width), :]
                else:
                    first = 0 if step_y < 0 else 8 - reach
                    land = 10 if step_y < 0 else 2 - reach
                    source = sides.at[pl.ds(base + first * width, reach * width), :]
                    target = landing.at[pl.ds(land * width, reach * width), :]
            copies.append(remote(number, d, source, target))
        for copy in copies:
            copy.start()
        return copies

    def remote(number, d, source, target):
        return pltpu.make_async_remote_copy(
            src_ref=source,
            dst_ref=target,
            send_sem=halo_send.at[number, d],
            recv_sem=halo_recv.at[number, d],
            device_id=neighbours[d],
            device_id_type=MESH,
        )

    def arrive(copies):
        for copy in copies:
            copy.wait_recv()

    def narrow(width, reach, inner, sides, box):
        inner_send, sides_send = box[:2]
        part = reach * 2 * width
        for place, first in enumerate((2, 10 - reach)):
            rows = inner[pl.ds(first * 2 * width, part), :]
            inner_send[pl.ds(place * part, part), :] = rows.astype(jnp.bfloat16)
        sides_send[...] = sides[...].astype(jnp.bfloat16)

    def start_narrow(number, reach, box):
        inner_send, sides_send, inner_recv, minus_recv, plus_recv = box
        width = sides_send.shape[0] // 16
        part = reach * 2 * width
        copies = []
        for d, (step_x, step_y) in enumerate(DIRECTIONS):
            if step_x == 0:
                rows = pl.ds(0 if step_y < 0 else part, part)
                source, target = inner_send.at[rows, :], inner_recv.at[rows, :]
            else:
                start = 0 if step_x < 0 else 8 * width
                landing = plus_recv if step_x < 0 else minus_recv
                if step_y == 0:
                    source = sides_send.at[pl.ds(start, 8 * width), :]
                    target = landing.at[pl.ds(2 * width, 8 * width), :]
                else:
                    first = 0 if step_y < 0 else 6
                    land = 10 if step_y < 0 else 0
                    source = sides_send.at[pl.ds(start + first * width, 2 * width), :]
                    target = landing.at[pl.ds(land * width, 2 * width), :]
            copies.append(remote(number, d, source, target))
        for copy in copies:
            copy.start()
        return copies

    def arrive_narrow(copies, width, reach, inner, minus, plus, box):
        inner_recv, minus_recv, plus_recv = box[2:]
        part = reach * 2 * width
        arrive(copies)
        for place, land in enumerate((10, 2 - reach)):
            rows = inner_recv[pl.ds(place * part, part), :]
            inner[pl.ds(land * 2 * width, part), :] = rows.astype(jnp.float32)
        minus[...] = minus_recv[...].astype(jnp.float32)
        plus[...] = plus_recv[...].astype(jnp.float32)

    lane = lax.broadcasted_iota(jnp.int32, (8, 128), 1)
    depth = lax.rem(lane, DEPTH)
    half = lane // DEPTH
    sublane = lax.broadcasted_iota(jnp.int32, (8, 128), 0)

    def inside(position, size):
        return jnp.where((position >= 0) & (position < size), 1.0, 0.0)

    mask_z = {step: inside(depth + step, DEPTH) for step in (-1, 0, 1)}
    mask_x = {at: inside(me_x * 4 + at + 2 * half, 4 * size_gx) for at in range(-2, 4)}

    def mask_y(y):
        return inside(me_y * 8 + y + sublane, 8 * size_gy)

    loads[0].wait()
    held = {}

    def keep(label, p, value):
        held[(label, p)] = value
        logits[label, p + 2, pl.ds(BASE, 8), :] = value
        if p == 1:
            lay_out(inner_u, sides_u, LABELS, label, held[(label, 0)], value)

    spread(unary_in, 4, keep)

    loads[1].wait()
    loads[3].wait()
    loads[4].wait()
    mask_own_y = {step: mask_y(step) for step in (-1, 0, 1)}

    def keep_affinity(number, p, value):
        held[(number, p)] = value
        step_x, step_y, step_z = OFFSETS[number]
        mask = mask_x[p + step_x] * mask_own_y[step_y] * mask_z[step_z]
        weight_own[number, p] = value * mask * strength[number]
        if p == 1:
            lay_out(inner_a, sides_a, WIDE, number, held[(number, 0)], value)

    spread(affinity_in, NEIGH // 2, keep_affinity)
    nothing = jnp.zeros((8, 128), jnp.float32)
    for number in range(NEIGH, WIDE):
        lay_out(inner_a, sides_a, WIDE, number, nothing, nothing)
    narrow(LABELS, 1, inner_u, sides_u, box_u)
    narrow(WIDE, 2, inner_a, sides_a, box_a)
    pl.semaphore_wait(barrier, len(neighbours))
    meet(0)
    sent_u = start_narrow(0, 1, box_u)
    sent_a = start_narrow(1, 2, box_a)

    arrive_narrow(sent_u, LABELS, 1, inner_u, minus_u, plus_u, box_u)
    meet(1)
    for label in range(LABELS):
        for y in (-1, 1):
            found = assemble(inner_u, minus_u, plus_u, LABELS, label, y, 1)
            for p in (-1, 0, 1, 2):
                logits[label, p + 2, pl.ds(BASE + y, 8), :] = found[p]
    for y in (-1, 1):
        for p in (-1, 0, 1, 2):
            value = normalise(logits[:, p + 2, pl.ds(BASE + y, 8), :])
            put_field(field_0, p, y, value)

    def own_logits(p):
        return logits[:, p + 2, pl.ds(BASE, 8), :]

    def own_weight(number, p):
        return weight_own[number, p]

    def forward(a, b):
        return compat[a, b]

    def backward(b, a):
        return compat[a, b]

    def lay_field(values, inner, sides):
        for label in range(LABELS):
            lay_out(inner, sides, LABELS, label, values[0][label], values[1][label])

    def send_field(number, reach, values, inner, sides, minus, plus):
        lay_field(values, inner, sides)
        return exchange(number, LABELS, reach, inner, sides, minus, plus)

    sums = message(own_weight, field_0, (0, 1), 0)
    values = []
    for p in (0, 1):
        message_1[:, p] = sums[p]
        values.append(normalise(own_logits(p) - mix(forward, sums[p])))
    sent_q = send_field(2, 2, values, inner_q, sides_q, minus_q, plus_q)

    loads[2].wait()

    def keep_cotangent(label, p, value):
        own_grad[label, p] = value

    spread(cotangent_in, 4, keep_cotangent)
    arrive_narrow(sent_a, WIDE, 2, inner_a, minus_a, plus_a, box_a)
    for number in range(NEIGH):
        for y in (-2, 2):
            found = assemble(inner_a, minus_a, plus_a, WIDE, number, y, 2)
            for p in range(-2, 4):
                wide_aff[number, p + 2, pl.ds(BASE + y, 8), :] = found[p] * strength[number]
    rim_mask_y = {y: mask_y(y) for y in (-2, -1, 0, 1, 2)}

    def rim_weights(target, value):
        for y in (-1, 1):
            for p in (-1, 0, 1, 2):
                for number, (step_x, step_y, step_z) in enumerate(OFFSETS):
                    across = mask_x[p + step_x] * rim_mask_y[y + step_y]
                    if step_z != 0:
                        across = across * mask_z[step_z]
                    target[number, p + 1, pl.ds(BASE + y, 8), :] = across * value(number, p, y)

    def rim_value(number, p, y):
        return wide_aff[number, p + 2, pl.ds(BASE + y, 8), :]

    def back_value(number, p, y):
        step_x, step_y, step_z = OFFSETS[number]
        opposite = NUMBER[(-step_x, -step_y, -step_z)]
        value = wide_aff[opposite, p + step_x + 2, pl.ds(BASE + y + step_y, 8), :]
        if step_z != 0:
            value = pltpu.roll(value, (128 - step_z) % 128, 1)
        return value

    rim_weights(weight_rim, rim_value)

    arrive(sent_q)
    meet(2)
    gather_field(field_1, inner_q, minus_q, plus_q, 2)
    for y in (-1, 1):

        def rim_weight(number, p, y=y):
            return weight_rim[number, p + 1, pl.ds(BASE + y, 8), :]

        sums = message(rim_weight, field_1, (-1, 0, 1, 2), y)
        for p in (-1, 0, 1, 2):
            message_2[:, p + 1, pl.ds(BASE + y, 8), :] = sums[p]
            here = logits[:, p + 2, pl.ds(BASE + y, 8), :]
            put_field(field_2, p, y, normalise(here - mix(forward, sums[p])))

    sums = message(own_weight, field_2, (0, 1), 0)
    grads = []
    values = []
    for p in (0, 1):
        current = normalise(own_logits(p) - mix(forward, sums[p]))
        step = softmax_back(current, own_grad[:, p])
        total_u[:, p] = step
        grads.append(-step)
        values.append(mix(backward, -step))
    lay_field(values, inner_g, sides_g)
    narrow(LABELS, 2, inner_g, sides_g, box_g)
    sent_g = start_narrow(3, 2, box_g)

    def add_compat(grads, messages, begin):
        for b in range(LABELS):
            term = grads[0] * messages[0][b][None] + grads[1] * messages[1][b][None]
            total_c[b] = term if begin else total_c[b] + term

    def add_kernel(values, field, begin):
        for number, (step_x, step_y, step_z) in enumerate(OFFSETS):
            for p in (0, 1):
                near = field[step_z + 1, :, p + step_x + 2, pl.ds(BASE + step_y, 8), :]
                joint = jnp.sum(values[p] * near, axis=0)
                total_r[number, p] = joint if begin else total_r[number, p] + joint

    add_compat(grads, [sums[0], sums[1]], True)
    add_kernel(values, field_2, True)
    rim_weights(weight_back, back_value)

    arrive_narrow(sent_g, LABELS, 2, inner_g, minus_g, plus_g, box_g)
    meet(3)
    gather_field(field_g, inner_g, minus_g, plus_g, 2)

    def back_weight_at(y):
        def back_weight(number, p):
            return weight_back[number, p + 1, pl.ds(BASE + y, 8), :]

        return back_weight

    for y in (-1, 1):
        sums = message(back_weight_at(y), field_g, (-1, 0, 1, 2), y)
        for p in (-1, 0, 1, 2):
            current = field_2[1, :, p + 2, pl.ds(BASE + y, 8), :]
            grad_p = -softmax_back(current, sums[p])
            rim_p[:, p + 1, pl.ds(BASE + y, 8), :] = grad_p
            put_field(field_h, p, y, mix(backward, grad_p))

    sums = message(back_weight_at(0), field_h, (0, 1), 0)
    grads_1 = []
    values_1 = []
    for p in (0, 1):
        current = field_1[1, :, p + 2, pl.ds(BASE, 8), :]
        step = softmax_back(current, sums[p])
        total_u[:, p] = total_u[:, p] + step
        grads_1.append(-step)
        values_1.append(mix(backward, -step))
    grads_2 = [rim_p[:, p + 1, pl.ds(BASE, 8), :] for p in (0, 1)]
    for p in (0, 1):
        total_u[:, p] = total_u[:, p] - grads_2[p]
    add_compat(grads_2, [message_2[:, p + 1, pl.ds(BASE, 8), :] for p in (0, 1)], False)
    add_kernel([field_h[1, :, p + 2, pl.ds(BASE, 8), :] for p in (0, 1)], field_1, False)
    add_compat(grads_1, [message_1[:, p] for p in (0, 1)], False)
    add_kernel(values_1, field_0, False)

    local = jnp.zeros((8, 128), jnp.float32)
    for b in range(LABELS):
        total = jnp.sum(jnp.sum(total_c[b], axis=1), axis=1, keepdims=True)
        local = jnp.where(lane == 8 * b + sublane, total, local)
    joint_rows = []
    for number, (step_x, step_y, step_z) in enumerate(OFFSETS):
        row = None
        for p in (0, 1):
            mask = mask_x[p + step_x] * mask_own_y[step_y] * mask_z[step_z]
            joint = total_r[number, p] * mask
            total_r[number, p] = joint * strength[number]
            term = joint * inner_a[inner_rows(0, p, number, WIDE), :]
            row = term if row is None else row + term
        joint_rows.append(jnp.sum(row, axis=0, keepdims=True))
    for group in range(4):
        rows = joint_rows[8 * group : 8 * (group + 1)]
        rows = rows + [jnp.zeros((1, 128), jnp.float32)] * (8 - len(rows))
        total = jnp.sum(jnp.concatenate(rows, axis=0), axis=1, keepdims=True)
        local = jnp.where(lane == 8 * (LABELS + group) + sublane, total, local)

    gather_a[me_x] = jnp.sum(local, axis=0, keepdims=True)

    def to_peer(buffer, me, place_send, place_recv, device):
        return pltpu.make_async_remote_copy(
            src_ref=buffer.at[me],
            dst_ref=buffer.at[me],
            send_sem=peer_send.at[place_send],
            recv_sem=peer_recv.at[place_recv],
            device_id=device,
            device_id_type=MESH,
        )

    along_x = [to_peer(gather_a, me_x, step, 2 * step + core, odd[step]) for step in range(chips)]
    for step in sorted(range(1, chips), key=lambda step: -ring(step, chips)):
        along_x[step].start()

    @pl.when(core == 0)
    def _():
        along_x[0].start()

    sent_h = send_field(4, 1, values_1, inner_h, sides_h, minus_h, plus_h)

    def put_affinity(tile, x, value):
        affinity_out[x, :, 128 * tile : 128 * (tile + 1)] = value.astype(jnp.bfloat16)

    gather_columns(lambda number, p: total_r[number, p], NEIGH // 2, put_affinity)
    store_a = pltpu.make_async_copy(affinity_out, grad_affinity_hbm, store_sem.at[0])
    store_a.start()

    meet(4)
    base = 2 * chips
    along_y = [
        to_peer(gather_b, me_y, base + place, base + place, device)
        for place, device in enumerate(peers_b)
    ]
    to_even = to_peer(last, 0, base + len(peers_b), base + len(peers_b), partner)

    @pl.when(core == 1)
    def _():
        for step in range(chips):
            for sender in (0, 1):
                if (step, sender) != (0, 1):
                    to_peer(gather_a, me_x, 0, 2 * step + sender, partner).wait_recv()
        total = gather_a[0]
        for place in range(1, size_gx):
            total = total + gather_a[place]
        gather_b[me_y] = total
        for copy in along_y:
            copy.start()

    arrive(sent_h)
    gather_field(field_i, inner_h, minus_h, plus_h, 1)
    sums = message(back_weight_at(0), field_i, (0, 1), 0)
    for p in (0, 1):
        current = field_0[1, :, p + 2, pl.ds(BASE, 8), :]
        total_u[:, p] = total_u[:, p] + softmax_back(current, sums[p])

    def put_unary(tile, x, value):
        unary_out[x, :, 128 * tile : 128 * (tile + 1)] = value.astype(jnp.bfloat16)

    gather_columns(lambda label, p: total_u[label, p], LABELS // 2, put_unary)
    store_u = pltpu.make_async_copy(unary_out, grad_unary_hbm, store_sem.at[1])
    store_u.start()

    @pl.when(core == 1)
    def _():
        for copy in along_y:
            copy.wait_recv()
        total = gather_b[0]
        for place in range(1, size_gy):
            total = total + gather_b[place]
        last[0] = total
        to_even.start()

    @pl.when(core == 0)
    def _():
        to_even.wait_recv()

    voxels = size_gx * 4 * size_gy * 8 * DEPTH
    final = last[0] * (1.0 / math.sqrt(voxels))
    grad_kernel[...] = pltpu.roll(final, 128 - LABELS * LABELS, 1)[:, :NEIGH]
    spaced = jnp.where(lax.rem(lane, 8) == sublane, jnp.broadcast_to(final, (8, 128)), 0.0)
    table = jnp.zeros((8, 128), jnp.float32)
    for b in range(LABELS):
        column = jnp.sum(jnp.where(lane // 8 == b, spaced, 0.0), axis=1, keepdims=True)
        table = jnp.where(lane == b, column, table)
    grad_compat[...] = table[:, :LABELS]

    for copy in sent_u + sent_a + sent_q + sent_g + sent_h + along_x[1:]:
        copy.wait_send()

    @pl.when(core == 0)
    def _():
        along_x[0].wait_send()

    @pl.when(core == 1)
    def _():
        for copy in along_y + [to_even]:
            copy.wait_send()

    store_a.wait()
    store_u.wait()


def doubling(size):
    steps, reach = [], 1
    while reach < size // 2:
        steps.append(reach)
        reach *= 2
    return steps


def hand_out(*refs):
    parts, results, held, sem = refs[:4], refs[4:8], refs[8:12], refs[12]
    inward = [
        pltpu.make_async_copy(part, hold, sem.at[0, number])
        for number, (part, hold) in enumerate(zip(parts, held))
    ]
    outward = [
        pltpu.make_async_copy(hold, result, sem.at[1, number])
        for number, (hold, result) in enumerate(zip(held, results))
    ]
    for copy in inward:
        copy.start()
    for came, copy in zip(inward, outward):
        came.wait()
        copy.start()
    for copy in outward:
        copy.wait()


def shards(sizes, unary_score, affinity, compatibility, kernel_weights, cotangent):
    size_gx, size_gy, size_far, size_near = sizes
    f32, bf16 = jnp.float32, jnp.bfloat16

    def rows(count, kind=f32):
        return pltpu.VMEM((count, 128), kind)

    def exchanged(width):
        return [
            rows(SPAN * 2 * width),
            rows(2 * 8 * width),
            rows(SPAN * width),
            rows(SPAN * width),
        ]

    def boxed(width, reach):
        return [
            rows(2 * reach * 2 * width, bf16),
            rows(2 * 8 * width, bf16),
            rows(2 * reach * 2 * width, bf16),
            rows(SPAN * width, bf16),
            rows(SPAN * width, bf16),
        ]

    field = pltpu.VMEM((3, LABELS, 6, TALL, 128), f32)
    pair = pltpu.VMEM((LABELS, 2, 8, 128), f32)
    rim = pltpu.VMEM((LABELS, 4, TALL, 128), f32)
    peers = size_gx + size_gy
    scratch = (
        [
            pltpu.VMEM(unary_score.shape, bf16),
            pltpu.VMEM(affinity.shape, bf16),
            pltpu.VMEM(cotangent.shape, bf16),
            pltpu.VMEM(unary_score.shape, bf16),
            pltpu.VMEM(affinity.shape, bf16),
            pltpu.SMEM(compatibility.shape, f32),
            pltpu.SMEM(kernel_weights.shape, f32),
        ]
        + exchanged(LABELS)
        + exchanged(WIDE)
        + boxed(LABELS, 1)
        + boxed(WIDE, 2)
        + boxed(LABELS, 2)
        + exchanged(LABELS)
        + exchanged(LABELS)
        + exchanged(LABELS)
        + [
            pltpu.VMEM((LABELS, 6, TALL, 128), f32),
            pair,
            field,
            field,
            field,
            field,
            field,
            field,
            pltpu.VMEM((NEIGH, 6, TALL, 128), f32),
            pltpu.VMEM((NEIGH, 2, 8, 128), f32),
            pltpu.VMEM((NEIGH, 4, TALL, 128), f32),
            pltpu.VMEM((NEIGH, 4, TALL, 128), f32),
            pair,
            rim,
            rim,
            pair,
            pltpu.VMEM((LABELS, LABELS, 8, 128), f32),
            pltpu.VMEM((NEIGH, 2, 8, 128), f32),
            pltpu.VMEM((size_gx, 1, 128), f32),
            pltpu.VMEM((size_gy, 1, 128), f32),
            pltpu.VMEM((1, 1, 128), f32),
            pltpu.SemaphoreType.DMA((5,)),
            pltpu.SemaphoreType.DMA((2,)),
            pltpu.SemaphoreType.DMA((5, 8)),
            pltpu.SemaphoreType.DMA((5, 8)),
            pltpu.SemaphoreType.DMA((peers,)),
            pltpu.SemaphoreType.DMA((peers,)),
            pltpu.SemaphoreType.REGULAR((2, 4)),
        ]
    )
    anywhere = pl.BlockSpec(memory_space=pl.ANY)
    in_hbm = pl.BlockSpec(memory_space=pltpu.HBM)
    vectors = pl.BlockSpec(memory_space=pltpu.VMEM)
    grad_unary, grad_affinity, grad_compat, grad_kernel = pl.pallas_call(
        functools.partial(kernel, sizes),
        out_shape=(
            jax.ShapeDtypeStruct(unary_score.shape, bf16),
            jax.ShapeDtypeStruct(affinity.shape, bf16),
            jax.ShapeDtypeStruct((LABELS, LABELS), f32),
            jax.ShapeDtypeStruct((1, NEIGH), f32),
        ),
        in_specs=[in_hbm] * 5,
        out_specs=(anywhere, anywhere, vectors, vectors),
        scratch_shapes=scratch,
        compiler_params=pltpu.CompilerParams(
            collective_id=0, has_side_effects=True, vmem_limit_bytes=GRANT
        ),
        name="mean_field_backward",
    )(unary_score, affinity, cotangent, compatibility, kernel_weights)
    found = (grad_unary, grad_affinity, grad_compat, grad_kernel.reshape(NEIGH))
    return pl.pallas_call(
        hand_out,
        out_shape=tuple(jax.ShapeDtypeStruct(part.shape, part.dtype) for part in found),
        in_specs=[anywhere] * 4,
        out_specs=(in_hbm,) * 4,
        scratch_shapes=[pltpu.VMEM(part.shape, part.dtype) for part in found]
        + [pltpu.SemaphoreType.DMA((2, 4))],
        compiler_params=pltpu.CompilerParams(vmem_limit_bytes=GRANT),
        name="hand_out",
    )(*found)


def solution(mesh):
    size_gx, size_gy = mesh.shape["gx"], mesh.shape["gy"]
    size_near = 4 if size_gy % 4 == 0 else 1
    sizes = (size_gx, size_gy, size_gy // size_near, size_near)
    in_specs = (P("gx", "gy", None), P("gx", "gy", None), P(), P(), P("gx", "gy", None))
    out_specs = (P("gx", "gy", None), P("gx", "gy", None), P(), P())
    return jax.shard_map(
        functools.partial(shards, sizes),
        mesh=mesh,
        in_specs=in_specs,
        out_specs=out_specs,
        check_vma=False,
    )
```

```python
import functools
import math

import jax
import jax.numpy as jnp
from jax import lax
from jax.experimental import pallas as pl
from jax.experimental.pallas import tpu as pltpu
from jax.sharding import PartitionSpec as P

LABELS = 8
DEPTH = 64
NEIGH = 26
ITERS = 3

OFFSETS = [
    (step_x, step_y, step_z)
    for step_x in (-1, 0, 1)
    for step_y in (-1, 0, 1)
    for step_z in (-1, 0, 1)
    if (step_x, step_y, step_z) != (0, 0, 0)
]
NUMBER = {offset: number for number, offset in enumerate(OFFSETS)}

SPAN = 12
TALL = 24
BASE = 8
DIRECTIONS = [(-1, -1), (-1, 1), (1, -1), (1, 1), (0, -1), (0, 1), (-1, 0), (1, 0)]
WIDE = 32
GRANT = 64 * 1024 * 1024 - 65536
MESH = pl.DeviceIdType.MESH


def low_half():
    return lax.broadcasted_iota(jnp.int32, (8, 128), 1) < DEPTH


def swap(values):
    return pltpu.roll(values, DEPTH, values.ndim - 1)


def inner_rows(y, p, label, width):
    return pl.ds(((y + 2) * 2 + p) * width + label, 8, stride=2 * width)


def side_rows(y, label, width):
    return pl.ds((y + 2) * width + label, 8, stride=width)


def spread(source, tiles, put):
    low = low_half()
    for tile in range(tiles):
        cols = [
            source[x, :, 128 * tile : 128 * (tile + 1)].astype(jnp.float32) for x in range(4)
        ]
        turned = [swap(col) for col in cols]
        for p in (0, 1):
            put(2 * tile, p, jnp.where(low, cols[p], turned[p + 2]))
            put(2 * tile + 1, p, jnp.where(low, turned[p], cols[p + 2]))


def gather_columns(values, tiles, put):
    low = low_half()
    for tile in range(tiles):
        for p in (0, 1):
            even, odd = values(2 * tile, p), values(2 * tile + 1, p)
            put(tile, p, jnp.where(low, even, swap(odd)))
            put(tile, p + 2, jnp.where(low, swap(even), odd))


def lay_out(inner, sides, width, label, first, second):
    low = low_half()
    inner[inner_rows(0, 0, label, width), :] = first
    inner[inner_rows(0, 1, label, width), :] = second
    sides[pl.ds(label, 8, stride=width), :] = jnp.where(low, first, swap(second))
    sides[pl.ds(8 * width + label, 8, stride=width), :] = jnp.where(low, swap(first), second)


def assemble(inner, minus, plus, width, label, y, reach):
    low = low_half()
    own = [inner[inner_rows(y, p, label, width), :] for p in (0, 1)]
    before = minus[side_rows(y, label, width), :]
    after = plus[side_rows(y, label, width), :]
    found = {0: own[0], 1: own[1]}
    found[2] = swap(jnp.where(low, after, own[0]))
    found[-1] = swap(jnp.where(low, own[1], before))
    if reach == 2:
        found[3] = jnp.where(low, swap(own[1]), after)
        found[-2] = jnp.where(low, before, swap(own[0]))
    return found


def message(weight, field, columns, y):
    sums = {p: None for p in columns}
    for step_y in (-1, 0, 1):
        for step_z in (-1, 0, 1):
            for source in range(min(columns) - 1, max(columns) + 2):
                users = [
                    (source - step_x, NUMBER[(step_x, step_y, step_z)])
                    for step_x in (-1, 0, 1)
                    if source - step_x in sums and (step_x, step_y, step_z) in NUMBER
                ]
                if not users:
                    continue
                near = field[step_z + 1, :, source + 2, pl.ds(BASE + y + step_y, 8), :]
                for p, number in users:
                    term = weight(number, p)[None] * near
                    sums[p] = term if sums[p] is None else sums[p] + term
    return sums


def mix(coef, values):
    rows = []
    for a in range(LABELS):
        total = coef(a, 0) * values[0]
        for b in range(1, LABELS):
            total = total + coef(a, b) * values[b]
        rows.append(total)
    return jnp.stack(rows)


def normalise(logits):
    powers = jnp.exp(logits - jnp.max(logits, axis=0, keepdims=True))
    return powers / jnp.sum(powers, axis=0, keepdims=True)


def softmax_back(current, grad_in):
    return current * (grad_in - jnp.sum(current * grad_in, axis=0, keepdims=True))


def put_shifts(field, p, y, values):
    field[0, :, p + 2, pl.ds(BASE + y, 8), :] = pltpu.roll(values, 1, 2)
    field[2, :, p + 2, pl.ds(BASE + y, 8), :] = pltpu.roll(values, 127, 2)


def put_field(field, p, y, values):
    field[1, :, p + 2, pl.ds(BASE + y, 8), :] = values
    put_shifts(field, p, y, values)


def rim_tiles(reach):
    return range(-reach, 2 + reach), (-2, 2) if reach == 2 else (-1, 1)


def gather_field(field, inner, minus, plus, reach):
    columns, starts = rim_tiles(reach)
    for label in range(LABELS):
        for y in starts:
            found = assemble(inner, minus, plus, LABELS, label, y, reach)
            for p in columns:
                field[1, label, p + 2, pl.ds(BASE + y, 8), :] = found[p]
    for y in starts:
        for p in columns:
            put_shifts(field, p, y, field[1, :, p + 2, pl.ds(BASE + y, 8), :])


def kernel(
    sizes,
    unary_hbm,
    affinity_hbm,
    cotangent_hbm,
    compat_hbm,
    strength_hbm,
    grad_unary_hbm,
    grad_affinity_hbm,
    grad_compat,
    grad_kernel,
    unary_in,
    affinity_in,
    cotangent_in,
    unary_out,
    affinity_out,
    compat,
    strength,
    inner_u,
    sides_u,
    minus_u,
    plus_u,
    inner_a,
    sides_a,
    minus_a,
    plus_a,
    *rest,
):
    boxes, rest = rest[:15], rest[15:]
    box_u, box_a, box_g = boxes[:5], boxes[5:10], boxes[10:]
    (
        inner_q,
        sides_q,
        minus_q,
        plus_q,
        inner_g,
        sides_g,
        minus_g,
        plus_g,
        inner_h,
        sides_h,
        minus_h,
        plus_h,
        logits,
        own_grad,
        field_0,
        field_1,
        field_2,
        field_g,
        field_h,
        field_i,
        wide_aff,
        masked_own,
        weight_own,
        weight_rim,
        weight_back,
        message_1,
        message_2,
        rim_p,
        total_u,
        total_c,
        total_r,
        gather_a,
        gather_b,
        last,
        load_sem,
        store_sem,
        halo_send,
        halo_recv,
        peer_send,
        peer_recv,
        meet_sem,
    ) = rest
    size_gx, size_gy, size_far, size_near = sizes
    me_x, me_y = lax.axis_index("gx"), lax.axis_index("gy")
    me_far, me_near = me_y // size_near, lax.rem(me_y, size_near)
    chips = size_gx // 2
    chip, core = me_x // 2, lax.rem(me_x, 2)
    low = low_half()

    def around(index, step, size):
        return lax.rem(index + (step + size), size)

    loads = [
        pltpu.make_async_copy(unary_hbm, unary_in, load_sem.at[0]),
        pltpu.make_async_copy(affinity_hbm, affinity_in, load_sem.at[1]),
        pltpu.make_async_copy(cotangent_hbm, cotangent_in, load_sem.at[2]),
        pltpu.make_async_copy(strength_hbm, strength, load_sem.at[3]),
        pltpu.make_async_copy(compat_hbm, compat, load_sem.at[4]),
    ]
    for load in loads:
        load.start()

    neighbours = [
        (around(me_x, step_x, size_gx), around(me_y, step_y, size_gy))
        for step_x, step_y in DIRECTIONS
    ]
    partner = (me_x + 1 - 2 * core, me_y)
    odd = [(2 * around(chip, step, chips) + 1, me_y) for step in range(chips)]
    even = [(2 * around(chip, step, chips), me_y) for step in range(chips)]

    def ring(step, size):
        return min(step, size - step)

    hops = sorted(
        [(far, near) for far in range(size_far) for near in range(size_near)][1:],
        key=lambda hop: -ring(hop[0], size_far) - ring(hop[1], size_near),
    )
    peers_b = [
        (me_x, around(me_far, far, size_far) * size_near + around(me_near, near, size_near))
        for far, near in hops
    ]
    barrier = pltpu.get_barrier_semaphore()

    def greet(devices):
        for device in devices:
            pl.semaphore_signal(barrier, inc=1, device_id=device, device_id_type=MESH)

    greet(neighbours)

    rounds = [doubling(size_gx), doubling(size_gy)]

    def meet(stage):
        for axis in (0, 1):
            if 0 < stage <= len(rounds[axis]):
                pl.semaphore_wait(meet_sem.at[axis, stage - 1], 2)
        for axis in (0, 1):
            if stage < len(rounds[axis]):
                step = rounds[axis][stage]
                for by in (-step, step):
                    device = (
                        (around(me_x, by, size_gx), me_y)
                        if axis == 0
                        else (me_x, around(me_y, by, size_gy))
                    )
                    pl.semaphore_signal(
                        meet_sem.at[axis, stage], inc=1, device_id=device, device_id_type=MESH
                    )

    def exchange(number, width, reach, inner, sides, minus, plus):
        copies = []
        for d, (step_x, step_y) in enumerate(DIRECTIONS):
            if step_x == 0:
                first = 2 if step_y < 0 else 10 - reach
                land = 10 if step_y < 0 else 2 - reach
                source = inner.at[pl.ds(first * 2 * width, reach * 2 * width), :]
                target = inner.at[pl.ds(land * 2 * width, reach * 2 * width), :]
            else:
                base = 0 if step_x < 0 else 8 * width
                landing = plus if step_x < 0 else minus
                if step_y == 0:
                    source = sides.at[pl.ds(base, 8 * width), :]
                    target = landing.at[pl.ds(2 * width, 8 * width), :]
                else:
                    first = 0 if step_y < 0 else 8 - reach
                    land = 10 if step_y < 0 else 2 - reach
                    source = sides.at[pl.ds(base + first * width, reach * width), :]
                    target = landing.at[pl.ds(land * width, reach * width), :]
            copies.append(remote(number, d, source, target))
        for copy in copies:
            copy.start()
        return copies

    def remote(number, d, source, target):
        return pltpu.make_async_remote_copy(
            src_ref=source,
            dst_ref=target,
            send_sem=halo_send.at[number, d],
            recv_sem=halo_recv.at[number, d],
            device_id=neighbours[d],
            device_id_type=MESH,
        )

    def arrive(copies):
        for copy in reversed(copies):
            copy.wait_recv()

    def narrow(width, reach, inner, sides, box):
        inner_send, sides_send = box[:2]
        part = reach * 2 * width
        for place, first in enumerate((2, 10 - reach)):
            rows = inner[pl.ds(first * 2 * width, part), :]
            inner_send[pl.ds(place * part, part), :] = rows.astype(jnp.bfloat16)
        sides_send[...] = sides[...].astype(jnp.bfloat16)

    def start_narrow(number, reach, box):
        inner_send, sides_send, inner_recv, minus_recv, plus_recv = box
        width = sides_send.shape[0] // 16
        part = reach * 2 * width
        copies = []
        for d, (step_x, step_y) in enumerate(DIRECTIONS):
            if step_x == 0:
                rows = pl.ds(0 if step_y < 0 else part, part)
                source, target = inner_send.at[rows, :], inner_recv.at[rows, :]
            else:
                start = 0 if step_x < 0 else 8 * width
                landing = plus_recv if step_x < 0 else minus_recv
                if step_y == 0:
                    source = sides_send.at[pl.ds(start, 8 * width), :]
                    target = landing.at[pl.ds(2 * width, 8 * width), :]
                else:
                    first = 0 if step_y < 0 else 6
                    land = 10 if step_y < 0 else 0
                    source = sides_send.at[pl.ds(start + first * width, 2 * width), :]
                    target = landing.at[pl.ds(land * width, 2 * width), :]
            copies.append(remote(number, d, source, target))
        for copy in copies:
            copy.start()
        return copies

    def arrive_narrow(copies, width, reach, inner, minus, plus, box):
        inner_recv, minus_recv, plus_recv = box[2:]
        part = reach * 2 * width
        arrive(copies)
        for place, land in enumerate((10, 2 - reach)):
            rows = inner_recv[pl.ds(place * part, part), :]
            inner[pl.ds(land * 2 * width, part), :] = rows.astype(jnp.float32)
        minus[...] = minus_recv[...].astype(jnp.float32)
        plus[...] = plus_recv[...].astype(jnp.float32)

    lane = lax.broadcasted_iota(jnp.int32, (8, 128), 1)
    depth = lax.rem(lane, DEPTH)
    half = lane // DEPTH
    sublane = lax.broadcasted_iota(jnp.int32, (8, 128), 0)

    def inside(position, size):
        return jnp.where((position >= 0) & (position < size), 1.0, 0.0)

    mask_z = {step: inside(depth + step, DEPTH) for step in (-1, 0, 1)}
    mask_x = {at: inside(me_x * 4 + at + 2 * half, 4 * size_gx) for at in range(-2, 4)}

    def mask_y(y):
        return inside(me_y * 8 + y + sublane, 8 * size_gy)

    loads[0].wait()
    held = {}

    def keep(label, p, value):
        held[(label, p)] = value
        logits[label, p + 2, pl.ds(BASE, 8), :] = value
        if p == 1:
            lay_out(inner_u, sides_u, LABELS, label, held[(label, 0)], value)

    spread(unary_in, 4, keep)

    loads[1].wait()
    loads[3].wait()
    loads[4].wait()
    mask_own_y = {step: mask_y(step) for step in (-1, 0, 1)}

    def keep_affinity(number, p, value):
        held[(number, p)] = value
        step_x, step_y, step_z = OFFSETS[number]
        mask = mask_x[p + step_x] * mask_own_y[step_y] * mask_z[step_z]
        masked_own[number, p] = value * mask
        weight_own[number, p] = value * mask * strength[number]
        if p == 1:
            lay_out(inner_a, sides_a, WIDE, number, held[(number, 0)], value)

    spread(affinity_in, NEIGH // 2, keep_affinity)
    nothing = jnp.zeros((8, 128), jnp.float32)
    for number in range(NEIGH, WIDE):
        lay_out(inner_a, sides_a, WIDE, number, nothing, nothing)
    narrow(LABELS, 1, inner_u, sides_u, box_u)
    narrow(WIDE, 2, inner_a, sides_a, box_a)
    pl.semaphore_wait(barrier, len(neighbours))
    meet(0)
    sent_u = start_narrow(0, 1, box_u)
    sent_a = start_narrow(1, 2, box_a)

    arrive_narrow(sent_u, LABELS, 1, inner_u, minus_u, plus_u, box_u)
    meet(1)
    for label in range(LABELS):
        for y in (-1, 1):
            found = assemble(inner_u, minus_u, plus_u, LABELS, label, y, 1)
            for p in (-1, 0, 1, 2):
                logits[label, p + 2, pl.ds(BASE + y, 8), :] = found[p]
    for y in (-1, 1):
        for p in (-1, 0, 1, 2):
            value = normalise(logits[:, p + 2, pl.ds(BASE + y, 8), :])
            put_field(field_0, p, y, value)

    def own_logits(p):
        return logits[:, p + 2, pl.ds(BASE, 8), :]

    def own_weight(number, p):
        return weight_own[number, p]

    def forward(a, b):
        return compat[a, b]

    def backward(b, a):
        return compat[a, b]

    def lay_field(values, inner, sides):
        for label in range(LABELS):
            lay_out(inner, sides, LABELS, label, values[0][label], values[1][label])

    def send_field(number, reach, values, inner, sides, minus, plus):
        lay_field(values, inner, sides)
        return exchange(number, LABELS, reach, inner, sides, minus, plus)

    sums = message(own_weight, field_0, (0, 1), 0)
    values = []
    for p in (0, 1):
        message_1[:, p] = sums[p]
        values.append(normalise(own_logits(p) - mix(forward, sums[p])))
    sent_q = send_field(2, 2, values, inner_q, sides_q, minus_q, plus_q)

    loads[2].wait()

    def keep_cotangent(label, p, value):
        own_grad[label, p] = value

    spread(cotangent_in, 4, keep_cotangent)
    arrive_narrow(sent_a, WIDE, 2, inner_a, minus_a, plus_a, box_a)
    for number in range(NEIGH):
        for y in (-2, 2):
            found = assemble(inner_a, minus_a, plus_a, WIDE, number, y, 2)
            for p in range(-2, 4):
                wide_aff[number, p + 2, pl.ds(BASE + y, 8), :] = found[p] * strength[number]
    rim_mask_y = {y: mask_y(y) for y in (-2, -1, 0, 1, 2)}

    def rim_weights(target, value):
        for y in (-1, 1):
            for p in (-1, 0, 1, 2):
                for number, (step_x, step_y, step_z) in enumerate(OFFSETS):
                    across = mask_x[p + step_x] * rim_mask_y[y + step_y]
                    if step_z != 0:
                        across = across * mask_z[step_z]
                    target[number, p + 1, pl.ds(BASE + y, 8), :] = across * value(number, p, y)

    def rim_value(number, p, y):
        return wide_aff[number, p + 2, pl.ds(BASE + y, 8), :]

    def back_value(number, p, y):
        step_x, step_y, step_z = OFFSETS[number]
        opposite = NUMBER[(-step_x, -step_y, -step_z)]
        value = wide_aff[opposite, p + step_x + 2, pl.ds(BASE + y + step_y, 8), :]
        if step_z != 0:
            value = pltpu.roll(value, (128 - step_z) % 128, 1)
        return value

    rim_weights(weight_rim, rim_value)

    arrive(sent_q)
    meet(2)
    gather_field(field_1, inner_q, minus_q, plus_q, 2)
    for y in (-1, 1):

        def rim_weight(number, p, y=y):
            return weight_rim[number, p + 1, pl.ds(BASE + y, 8), :]

        sums = message(rim_weight, field_1, (-1, 0, 1, 2), y)
        for p in (-1, 0, 1, 2):
            message_2[:, p + 1, pl.ds(BASE + y, 8), :] = sums[p]
            here = logits[:, p + 2, pl.ds(BASE + y, 8), :]
            put_field(field_2, p, y, normalise(here - mix(forward, sums[p])))

    sums = message(own_weight, field_2, (0, 1), 0)
    grads = []
    values = []
    for p in (0, 1):
        current = normalise(own_logits(p) - mix(forward, sums[p]))
        step = softmax_back(current, own_grad[:, p])
        total_u[:, p] = step
        grads.append(-step)
        values.append(mix(backward, -step))
    lay_field(values, inner_g, sides_g)
    narrow(LABELS, 2, inner_g, sides_g, box_g)
    sent_g = start_narrow(3, 2, box_g)

    def add_compat(grads, messages, begin):
        for b in range(LABELS):
            term = grads[0] * messages[0][b][None] + grads[1] * messages[1][b][None]
            total_c[b] = term if begin else total_c[b] + term

    def add_kernel(values, field, begin):
        for number, (step_x, step_y, step_z) in enumerate(OFFSETS):
            for p in (0, 1):
                near = field[step_z + 1, :, p + step_x + 2, pl.ds(BASE + step_y, 8), :]
                joint = jnp.sum(values[p] * near, axis=0)
                total_r[number, p] = joint if begin else total_r[number, p] + joint

    add_compat(grads, [sums[0], sums[1]], True)
    add_kernel(values, field_2, True)
    rim_weights(weight_back, back_value)

    arrive_narrow(sent_g, LABELS, 2, inner_g, minus_g, plus_g, box_g)
    meet(3)
    gather_field(field_g, inner_g, minus_g, plus_g, 2)

    def back_weight_at(y):
        def back_weight(number, p):
            return weight_back[number, p + 1, pl.ds(BASE + y, 8), :]

        return back_weight

    for y in (-1, 1):
        sums = message(back_weight_at(y), field_g, (-1, 0, 1, 2), y)
        for p in (-1, 0, 1, 2):
            current = field_2[1, :, p + 2, pl.ds(BASE + y, 8), :]
            grad_p = -softmax_back(current, sums[p])
            rim_p[:, p + 1, pl.ds(BASE + y, 8), :] = grad_p
            put_field(field_h, p, y, mix(backward, grad_p))

    sums = message(back_weight_at(0), field_h, (0, 1), 0)
    grads_1 = []
    values_1 = []
    for p in (0, 1):
        current = field_1[1, :, p + 2, pl.ds(BASE, 8), :]
        step = softmax_back(current, sums[p])
        total_u[:, p] = total_u[:, p] + step
        grads_1.append(-step)
        values_1.append(mix(backward, -step))
    grads_2 = [rim_p[:, p + 1, pl.ds(BASE, 8), :] for p in (0, 1)]
    for p in (0, 1):
        total_u[:, p] = total_u[:, p] - grads_2[p]
    add_compat(grads_2, [message_2[:, p + 1, pl.ds(BASE, 8), :] for p in (0, 1)], False)
    add_kernel([field_h[1, :, p + 2, pl.ds(BASE, 8), :] for p in (0, 1)], field_1, False)
    add_compat(grads_1, [message_1[:, p] for p in (0, 1)], False)
    add_kernel(values_1, field_0, False)

    local = jnp.zeros((8, 128), jnp.float32)
    for b in range(LABELS):
        total = jnp.sum(jnp.sum(total_c[b], axis=1), axis=1, keepdims=True)
        local = jnp.where(lane == 8 * b + sublane, total, local)
    joint_rows = []
    for number in range(NEIGH):
        row = None
        for p in (0, 1):
            term = total_r[number, p] * masked_own[number, p]
            row = term if row is None else row + term
        joint_rows.append(jnp.sum(row, axis=0, keepdims=True))
    for group in range(4):
        rows = joint_rows[8 * group : 8 * (group + 1)]
        rows = rows + [jnp.zeros((1, 128), jnp.float32)] * (8 - len(rows))
        total = jnp.sum(jnp.concatenate(rows, axis=0), axis=1, keepdims=True)
        local = jnp.where(lane == 8 * (LABELS + group) + sublane, total, local)

    gather_a[me_x] = jnp.sum(local, axis=0, keepdims=True)

    def to_peer(buffer, me, place_send, place_recv, device):
        return pltpu.make_async_remote_copy(
            src_ref=buffer.at[me],
            dst_ref=buffer.at[me],
            send_sem=peer_send.at[place_send],
            recv_sem=peer_recv.at[place_recv],
            device_id=device,
            device_id_type=MESH,
        )

    along_x = [to_peer(gather_a, me_x, step, 2 * step + core, odd[step]) for step in range(chips)]
    for step in sorted(range(1, chips), key=lambda step: -ring(step, chips)):
        along_x[step].start()

    @pl.when(core == 0)
    def _():
        along_x[0].start()

    sent_h = send_field(4, 1, values_1, inner_h, sides_h, minus_h, plus_h)

    def put_affinity(tile, x, value):
        affinity_out[x, :, 128 * tile : 128 * (tile + 1)] = value.astype(jnp.bfloat16)

    def own_affinity(number, p):
        step_x, step_y, step_z = OFFSETS[number]
        mask = mask_x[p + step_x] * mask_own_y[step_y] * mask_z[step_z]
        return total_r[number, p] * mask * strength[number]

    gather_columns(own_affinity, NEIGH // 2, put_affinity)
    store_a = pltpu.make_async_copy(affinity_out, grad_affinity_hbm, store_sem.at[0])
    store_a.start()

    meet(4)
    base = 2 * chips
    along_y = [
        to_peer(gather_b, me_y, base + place, base + place, device)
        for place, device in enumerate(peers_b)
    ]
    to_even = to_peer(last, 0, base + len(peers_b), base + len(peers_b), partner)

    @pl.when(core == 1)
    def _():
        for step in sorted(range(chips), key=lambda step: ring(step, chips)):
            for sender in (0, 1):
                if (step, sender) != (0, 1):
                    to_peer(gather_a, me_x, 0, 2 * step + sender, partner).wait_recv()
        total = gather_a[0]
        for place in range(1, size_gx):
            total = total + gather_a[place]
        gather_b[me_y] = total
        for copy in along_y:
            copy.start()

    arrive(sent_h)
    gather_field(field_i, inner_h, minus_h, plus_h, 1)
    sums = message(back_weight_at(0), field_i, (0, 1), 0)
    for p in (0, 1):
        current = field_0[1, :, p + 2, pl.ds(BASE, 8), :]
        total_u[:, p] = total_u[:, p] + softmax_back(current, sums[p])

    def put_unary(tile, x, value):
        unary_out[x, :, 128 * tile : 128 * (tile + 1)] = value.astype(jnp.bfloat16)

    gather_columns(lambda label, p: total_u[label, p], LABELS // 2, put_unary)
    store_u = pltpu.make_async_copy(unary_out, grad_unary_hbm, store_sem.at[1])
    store_u.start()

    for copy in sent_u + sent_a + sent_q + sent_g + sent_h + along_x[1:]:
        copy.wait_send()

    @pl.when(core == 0)
    def _():
        along_x[0].wait_send()

    @pl.when(core == 1)
    def _():
        for copy in along_y:
            copy.wait_send()
        arrive(along_y)
        total = gather_b[0]
        for place in range(1, size_gy):
            total = total + gather_b[place]
        last[0] = total
        to_even.start()

    @pl.when(core == 0)
    def _():
        to_even.wait_recv()

    voxels = size_gx * 4 * size_gy * 8 * DEPTH
    final = last[0] * (1.0 / math.sqrt(voxels))
    grad_kernel[...] = pltpu.roll(final, 128 - LABELS * LABELS, 1)[:, :NEIGH]
    spaced = jnp.where(lax.rem(lane, 8) == sublane, jnp.broadcast_to(final, (8, 128)), 0.0)
    table = jnp.zeros((8, 128), jnp.float32)
    for b in range(LABELS):
        column = jnp.sum(jnp.where(lane // 8 == b, spaced, 0.0), axis=1, keepdims=True)
        table = jnp.where(lane == b, column, table)
    grad_compat[...] = table[:, :LABELS]

    @pl.when(core == 1)
    def _():
        to_even.wait_send()

    store_a.wait()
    store_u.wait()


def doubling(size):
    steps, reach = [], 1
    while reach < size // 2:
        steps.append(reach)
        reach *= 2
    return steps


def hand_out(*refs):
    parts, results, held, sem = refs[:4], refs[4:8], refs[8:12], refs[12]
    inward = [
        pltpu.make_async_copy(part, hold, sem.at[0, number])
        for number, (part, hold) in enumerate(zip(parts, held))
    ]
    outward = [
        pltpu.make_async_copy(hold, result, sem.at[1, number])
        for number, (hold, result) in enumerate(zip(held, results))
    ]
    for copy in inward:
        copy.start()
    for came, copy in zip(inward, outward):
        came.wait()
        copy.start()
    for copy in outward:
        copy.wait()


def shards(sizes, unary_score, affinity, compatibility, kernel_weights, cotangent):
    size_gx, size_gy, size_far, size_near = sizes
    f32, bf16 = jnp.float32, jnp.bfloat16

    def rows(count, kind=f32):
        return pltpu.VMEM((count, 128), kind)

    def exchanged(width):
        return [
            rows(SPAN * 2 * width),
            rows(2 * 8 * width),
            rows(SPAN * width),
            rows(SPAN * width),
        ]

    def boxed(width, reach):
        return [
            rows(2 * reach * 2 * width, bf16),
            rows(2 * 8 * width, bf16),
            rows(2 * reach * 2 * width, bf16),
            rows(SPAN * width, bf16),
            rows(SPAN * width, bf16),
        ]

    field = pltpu.VMEM((3, LABELS, 6, TALL, 128), f32)
    pair = pltpu.VMEM((LABELS, 2, 8, 128), f32)
    rim = pltpu.VMEM((LABELS, 4, TALL, 128), f32)
    peers = size_gx + size_gy
    scratch = (
        [
            pltpu.VMEM(unary_score.shape, bf16),
            pltpu.VMEM(affinity.shape, bf16),
            pltpu.VMEM(cotangent.shape, bf16),
            pltpu.VMEM(unary_score.shape, bf16),
            pltpu.VMEM(affinity.shape, bf16),
            pltpu.SMEM(compatibility.shape, f32),
            pltpu.SMEM(kernel_weights.shape, f32),
        ]
        + exchanged(LABELS)
        + exchanged(WIDE)
        + boxed(LABELS, 1)
        + boxed(WIDE, 2)
        + boxed(LABELS, 2)
        + exchanged(LABELS)
        + exchanged(LABELS)
        + exchanged(LABELS)
        + [
            pltpu.VMEM((LABELS, 6, TALL, 128), f32),
            pair,
            field,
            field,
            field,
            field,
            field,
            field,
            pltpu.VMEM((NEIGH, 6, TALL, 128), f32),
            pltpu.VMEM((NEIGH, 2, 8, 128), f32),
            pltpu.VMEM((NEIGH, 2, 8, 128), f32),
            pltpu.VMEM((NEIGH, 4, TALL, 128), f32),
            pltpu.VMEM((NEIGH, 4, TALL, 128), f32),
            pair,
            rim,
            rim,
            pair,
            pltpu.VMEM((LABELS, LABELS, 8, 128), f32),
            pltpu.VMEM((NEIGH, 2, 8, 128), f32),
            pltpu.VMEM((size_gx, 1, 128), f32),
            pltpu.VMEM((size_gy, 1, 128), f32),
            pltpu.VMEM((1, 1, 128), f32),
            pltpu.SemaphoreType.DMA((5,)),
            pltpu.SemaphoreType.DMA((2,)),
            pltpu.SemaphoreType.DMA((5, 8)),
            pltpu.SemaphoreType.DMA((5, 8)),
            pltpu.SemaphoreType.DMA((peers,)),
            pltpu.SemaphoreType.DMA((peers,)),
            pltpu.SemaphoreType.REGULAR((2, 4)),
        ]
    )
    anywhere = pl.BlockSpec(memory_space=pl.ANY)
    in_hbm = pl.BlockSpec(memory_space=pltpu.HBM)
    vectors = pl.BlockSpec(memory_space=pltpu.VMEM)
    grad_unary, grad_affinity, grad_compat, grad_kernel = pl.pallas_call(
        functools.partial(kernel, sizes),
        out_shape=(
            jax.ShapeDtypeStruct(unary_score.shape, bf16),
            jax.ShapeDtypeStruct(affinity.shape, bf16),
            jax.ShapeDtypeStruct((LABELS, LABELS), f32),
            jax.ShapeDtypeStruct((1, NEIGH), f32),
        ),
        in_specs=[in_hbm] * 5,
        out_specs=(anywhere, anywhere, vectors, vectors),
        scratch_shapes=scratch,
        compiler_params=pltpu.CompilerParams(
            collective_id=0, has_side_effects=True, vmem_limit_bytes=GRANT
        ),
        name="mean_field_backward",
    )(unary_score, affinity, cotangent, compatibility, kernel_weights)
    found = (grad_unary, grad_affinity, grad_compat, grad_kernel.reshape(NEIGH))
    return pl.pallas_call(
        hand_out,
        out_shape=tuple(jax.ShapeDtypeStruct(part.shape, part.dtype) for part in found),
        in_specs=[anywhere] * 4,
        out_specs=(in_hbm,) * 4,
        scratch_shapes=[pltpu.VMEM(part.shape, part.dtype) for part in found]
        + [pltpu.SemaphoreType.DMA((2, 4))],
        compiler_params=pltpu.CompilerParams(vmem_limit_bytes=GRANT),
        name="hand_out",
    )(*found)


def solution(mesh):
    size_gx, size_gy = mesh.shape["gx"], mesh.shape["gy"]
    size_near = 4 if size_gy % 4 == 0 else 1
    sizes = (size_gx, size_gy, size_gy // size_near, size_near)
    in_specs = (P("gx", "gy", None), P("gx", "gy", None), P(), P(), P("gx", "gy", None))
    out_specs = (P("gx", "gy", None), P("gx", "gy", None), P(), P())
    return jax.shard_map(
        functools.partial(shards, sizes),
        mesh=mesh,
        in_specs=in_specs,
        out_specs=out_specs,
        check_vma=False,
    )
```

```python
import functools
import math

import jax
import jax.numpy as jnp
from jax import lax
from jax.experimental import pallas as pl
from jax.experimental.pallas import tpu as pltpu
from jax.sharding import PartitionSpec as P

LABELS = 8
DEPTH = 64
NEIGH = 26
ITERS = 3

OFFSETS = [
    (step_x, step_y, step_z)
    for step_x in (-1, 0, 1)
    for step_y in (-1, 0, 1)
    for step_z in (-1, 0, 1)
    if (step_x, step_y, step_z) != (0, 0, 0)
]
NUMBER = {offset: number for number, offset in enumerate(OFFSETS)}

SPAN = 12
TALL = 24
BASE = 8
DIRECTIONS = [(-1, -1), (-1, 1), (1, -1), (1, 1), (0, -1), (0, 1), (-1, 0), (1, 0)]
WIDE = 32
GRANT = 64 * 1024 * 1024 - 65536
MESH = pl.DeviceIdType.MESH


def low_half():
    return lax.broadcasted_iota(jnp.int32, (8, 128), 1) < DEPTH


def swap(values):
    return pltpu.roll(values, DEPTH, values.ndim - 1)


def inner_rows(y, p, label, width):
    return pl.ds(((y + 2) * 2 + p) * width + label, 8, stride=2 * width)


def side_rows(y, label, width):
    return pl.ds((y + 2) * width + label, 8, stride=width)


def spread(source, tiles, put):
    low = low_half()
    for tile in range(tiles):
        cols = [
            source[x, :, 128 * tile : 128 * (tile + 1)].astype(jnp.float32) for x in range(4)
        ]
        turned = [swap(col) for col in cols]
        for p in (0, 1):
            put(2 * tile, p, jnp.where(low, cols[p], turned[p + 2]))
            put(2 * tile + 1, p, jnp.where(low, turned[p], cols[p + 2]))


def gather_columns(values, tiles, put):
    low = low_half()
    for tile in range(tiles):
        for p in (0, 1):
            even, odd = values(2 * tile, p), values(2 * tile + 1, p)
            put(tile, p, jnp.where(low, even, swap(odd)))
            put(tile, p + 2, jnp.where(low, swap(even), odd))


def lay_out(inner, sides, width, label, first, second):
    low = low_half()
    inner[inner_rows(0, 0, label, width), :] = first
    inner[inner_rows(0, 1, label, width), :] = second
    sides[pl.ds(label, 8, stride=width), :] = jnp.where(low, first, swap(second))
    sides[pl.ds(8 * width + label, 8, stride=width), :] = jnp.where(low, swap(first), second)


def assemble(inner, minus, plus, width, label, y, reach):
    low = low_half()
    own = [inner[inner_rows(y, p, label, width), :] for p in (0, 1)]
    before = minus[side_rows(y, label, width), :]
    after = plus[side_rows(y, label, width), :]
    found = {0: own[0], 1: own[1]}
    found[2] = swap(jnp.where(low, after, own[0]))
    found[-1] = swap(jnp.where(low, own[1], before))
    if reach == 2:
        found[3] = jnp.where(low, swap(own[1]), after)
        found[-2] = jnp.where(low, before, swap(own[0]))
    return found


def message(weight, field, columns, y):
    sums = {p: None for p in columns}
    for step_y in (-1, 0, 1):
        for step_z in (-1, 0, 1):
            for source in range(min(columns) - 1, max(columns) + 2):
                users = [
                    (source - step_x, NUMBER[(step_x, step_y, step_z)])
                    for step_x in (-1, 0, 1)
                    if source - step_x in sums and (step_x, step_y, step_z) in NUMBER
                ]
                if not users:
                    continue
                near = field[step_z + 1, :, source + 2, pl.ds(BASE + y + step_y, 8), :]
                for p, number in users:
                    term = weight(number, p)[None] * near
                    sums[p] = term if sums[p] is None else sums[p] + term
    return sums


def mix(coef, values):
    rows = []
    for a in range(LABELS):
        total = coef(a, 0) * values[0]
        for b in range(1, LABELS):
            total = total + coef(a, b) * values[b]
        rows.append(total)
    return jnp.stack(rows)


def normalise(logits):
    powers = jnp.exp(logits - jnp.max(logits, axis=0, keepdims=True))
    return powers / jnp.sum(powers, axis=0, keepdims=True)


def softmax_back(current, grad_in):
    return current * (grad_in - jnp.sum(current * grad_in, axis=0, keepdims=True))


def put_shifts(field, p, y, values):
    field[0, :, p + 2, pl.ds(BASE + y, 8), :] = pltpu.roll(values, 1, 2)
    field[2, :, p + 2, pl.ds(BASE + y, 8), :] = pltpu.roll(values, 127, 2)


def put_field(field, p, y, values):
    field[1, :, p + 2, pl.ds(BASE + y, 8), :] = values
    put_shifts(field, p, y, values)


def rim_tiles(reach):
    return range(-reach, 2 + reach), (-2, 2) if reach == 2 else (-1, 1)


def gather_field(field, inner, minus, plus, reach):
    columns, starts = rim_tiles(reach)
    for label in range(LABELS):
        for y in starts:
            found = assemble(inner, minus, plus, LABELS, label, y, reach)
            for p in columns:
                field[1, label, p + 2, pl.ds(BASE + y, 8), :] = found[p]
    for y in starts:
        for p in columns:
            put_shifts(field, p, y, field[1, :, p + 2, pl.ds(BASE + y, 8), :])


def kernel(
    sizes,
    unary_hbm,
    affinity_hbm,
    cotangent_hbm,
    compat_hbm,
    strength_hbm,
    grad_unary_hbm,
    grad_affinity_hbm,
    grad_compat,
    grad_kernel,
    unary_in,
    affinity_in,
    cotangent_in,
    unary_out,
    affinity_out,
    compat,
    strength,
    inner_u,
    sides_u,
    minus_u,
    plus_u,
    inner_a,
    sides_a,
    minus_a,
    plus_a,
    *rest,
):
    boxes, rest = rest[:15], rest[15:]
    box_u, box_a, box_g = boxes[:5], boxes[5:10], boxes[10:]
    (
        inner_q,
        sides_q,
        minus_q,
        plus_q,
        inner_g,
        sides_g,
        minus_g,
        plus_g,
        inner_h,
        sides_h,
        minus_h,
        plus_h,
        logits,
        own_grad,
        field_0,
        field_1,
        field_2,
        field_g,
        field_h,
        field_i,
        wide_aff,
        masked_own,
        weight_own,
        weight_rim,
        weight_back,
        message_1,
        message_2,
        rim_p,
        total_u,
        total_c,
        total_r,
        gather_a,
        gather_b,
        last,
        load_sem,
        store_sem,
        halo_send,
        halo_recv,
        peer_send,
        peer_recv,
        meet_sem,
    ) = rest
    size_gx, size_gy, size_far, size_near = sizes
    me_x, me_y = lax.axis_index("gx"), lax.axis_index("gy")
    me_far, me_near = me_y // size_near, lax.rem(me_y, size_near)
    chips = size_gx // 2
    chip, core = me_x // 2, lax.rem(me_x, 2)
    low = low_half()

    def around(index, step, size):
        return lax.rem(index + (step + size), size)

    loads = [
        pltpu.make_async_copy(unary_hbm, unary_in, load_sem.at[0]),
        pltpu.make_async_copy(affinity_hbm, affinity_in, load_sem.at[1]),
        pltpu.make_async_copy(cotangent_hbm, cotangent_in, load_sem.at[2]),
        pltpu.make_async_copy(strength_hbm, strength, load_sem.at[3]),
        pltpu.make_async_copy(compat_hbm, compat, load_sem.at[4]),
    ]
    neighbours = [
        (around(me_x, step_x, size_gx), around(me_y, step_y, size_gy))
        for step_x, step_y in DIRECTIONS
    ]
    partner = (me_x + 1 - 2 * core, me_y)
    odd = [(2 * around(chip, step, chips) + 1, me_y) for step in range(chips)]
    even = [(2 * around(chip, step, chips), me_y) for step in range(chips)]

    def ring(step, size):
        return min(step, size - step)

    hops = sorted(
        [(far, near) for far in range(size_far) for near in range(size_near)][1:],
        key=lambda hop: -ring(hop[0], size_far) - ring(hop[1], size_near),
    )
    peers_b = [
        (me_x, around(me_far, far, size_far) * size_near + around(me_near, near, size_near))
        for far, near in hops
    ]
    barrier = pltpu.get_barrier_semaphore()

    def greet(devices):
        for device in devices:
            pl.semaphore_signal(barrier, inc=1, device_id=device, device_id_type=MESH)

    greet(neighbours)
    for load in loads:
        load.start()

    rounds = [doubling(size_gx), doubling(size_gy)]

    def meet(stage):
        for axis in (0, 1):
            if 0 < stage <= len(rounds[axis]):
                pl.semaphore_wait(meet_sem.at[axis, stage - 1], 2)
        for axis in (0, 1):
            if stage < len(rounds[axis]):
                step = rounds[axis][stage]
                for by in (-step, step):
                    device = (
                        (around(me_x, by, size_gx), me_y)
                        if axis == 0
                        else (me_x, around(me_y, by, size_gy))
                    )
                    pl.semaphore_signal(
                        meet_sem.at[axis, stage], inc=1, device_id=device, device_id_type=MESH
                    )

    def exchange(number, width, reach, inner, sides, minus, plus):
        copies = []
        for d, (step_x, step_y) in enumerate(DIRECTIONS):
            if step_x == 0:
                first = 2 if step_y < 0 else 10 - reach
                land = 10 if step_y < 0 else 2 - reach
                source = inner.at[pl.ds(first * 2 * width, reach * 2 * width), :]
                target = inner.at[pl.ds(land * 2 * width, reach * 2 * width), :]
            else:
                base = 0 if step_x < 0 else 8 * width
                landing = plus if step_x < 0 else minus
                if step_y == 0:
                    source = sides.at[pl.ds(base, 8 * width), :]
                    target = landing.at[pl.ds(2 * width, 8 * width), :]
                else:
                    first = 0 if step_y < 0 else 8 - reach
                    land = 10 if step_y < 0 else 2 - reach
                    source = sides.at[pl.ds(base + first * width, reach * width), :]
                    target = landing.at[pl.ds(land * width, reach * width), :]
            copies.append(remote(number, d, source, target))
        for copy in copies:
            copy.start()
        return copies

    def remote(number, d, source, target):
        return pltpu.make_async_remote_copy(
            src_ref=source,
            dst_ref=target,
            send_sem=halo_send.at[number, d],
            recv_sem=halo_recv.at[number, d],
            device_id=neighbours[d],
            device_id_type=MESH,
        )

    def arrive(copies):
        for copy in reversed(copies):
            copy.wait_recv()

    def narrow(width, reach, inner, sides, box):
        inner_send, sides_send = box[:2]
        part = reach * 2 * width
        for place, first in enumerate((2, 10 - reach)):
            rows = inner[pl.ds(first * 2 * width, part), :]
            inner_send[pl.ds(place * part, part), :] = rows.astype(jnp.bfloat16)
        sides_send[...] = sides[...].astype(jnp.bfloat16)

    def start_narrow(number, reach, box):
        inner_send, sides_send, inner_recv, minus_recv, plus_recv = box
        width = sides_send.shape[0] // 16
        part = reach * 2 * width
        copies = []
        for d, (step_x, step_y) in enumerate(DIRECTIONS):
            if step_x == 0:
                rows = pl.ds(0 if step_y < 0 else part, part)
                source, target = inner_send.at[rows, :], inner_recv.at[rows, :]
            else:
                start = 0 if step_x < 0 else 8 * width
                landing = plus_recv if step_x < 0 else minus_recv
                if step_y == 0:
                    source = sides_send.at[pl.ds(start, 8 * width), :]
                    target = landing.at[pl.ds(2 * width, 8 * width), :]
                else:
                    first = 0 if step_y < 0 else 6
                    land = 10 if step_y < 0 else 0
                    source = sides_send.at[pl.ds(start + first * width, 2 * width), :]
                    target = landing.at[pl.ds(land * width, 2 * width), :]
            copies.append(remote(number, d, source, target))
        for copy in copies:
            copy.start()
        return copies

    def arrive_narrow(copies, width, reach, inner, minus, plus, box):
        inner_recv, minus_recv, plus_recv = box[2:]
        part = reach * 2 * width
        arrive(copies)
        for place, land in enumerate((10, 2 - reach)):
            rows = inner_recv[pl.ds(place * part, part), :]
            inner[pl.ds(land * 2 * width, part), :] = rows.astype(jnp.float32)
        minus[...] = minus_recv[...].astype(jnp.float32)
        plus[...] = plus_recv[...].astype(jnp.float32)

    lane = lax.broadcasted_iota(jnp.int32, (8, 128), 1)
    depth = lax.rem(lane, DEPTH)
    half = lane // DEPTH
    sublane = lax.broadcasted_iota(jnp.int32, (8, 128), 0)

    def inside(position, size):
        return jnp.where((position >= 0) & (position < size), 1.0, 0.0)

    mask_z = {step: inside(depth + step, DEPTH) for step in (-1, 0, 1)}
    mask_x = {at: inside(me_x * 4 + at + 2 * half, 4 * size_gx) for at in range(-2, 4)}

    def mask_y(y):
        return inside(me_y * 8 + y + sublane, 8 * size_gy)

    loads[0].wait()
    held = {}

    def keep(label, p, value):
        held[(label, p)] = value
        logits[label, p + 2, pl.ds(BASE, 8), :] = value
        if p == 1:
            lay_out(inner_u, sides_u, LABELS, label, held[(label, 0)], value)

    spread(unary_in, 4, keep)

    loads[1].wait()
    loads[3].wait()
    loads[4].wait()
    mask_own_y = {step: mask_y(step) for step in (-1, 0, 1)}

    def keep_affinity(number, p, value):
        held[(number, p)] = value
        step_x, step_y, step_z = OFFSETS[number]
        mask = mask_x[p + step_x] * mask_own_y[step_y] * mask_z[step_z]
        masked_own[number, p] = value * mask
        weight_own[number, p] = value * mask * strength[number]
        if p == 1:
            lay_out(inner_a, sides_a, WIDE, number, held[(number, 0)], value)

    spread(affinity_in, NEIGH // 2, keep_affinity)
    nothing = jnp.zeros((8, 128), jnp.float32)
    for number in range(NEIGH, WIDE):
        lay_out(inner_a, sides_a, WIDE, number, nothing, nothing)
    narrow(LABELS, 1, inner_u, sides_u, box_u)
    narrow(WIDE, 2, inner_a, sides_a, box_a)
    pl.semaphore_wait(barrier, len(neighbours))
    sent_u = start_narrow(0, 1, box_u)
    sent_a = start_narrow(1, 2, box_a)
    meet(0)

    arrive_narrow(sent_u, LABELS, 1, inner_u, minus_u, plus_u, box_u)
    for label in range(LABELS):
        for y in (-1, 1):
            found = assemble(inner_u, minus_u, plus_u, LABELS, label, y, 1)
            for p in (-1, 0, 1, 2):
                logits[label, p + 2, pl.ds(BASE + y, 8), :] = found[p]
    for y in (-1, 1):
        for p in (-1, 0, 1, 2):
            value = normalise(logits[:, p + 2, pl.ds(BASE + y, 8), :])
            put_field(field_0, p, y, value)

    def own_logits(p):
        return logits[:, p + 2, pl.ds(BASE, 8), :]

    def own_weight(number, p):
        return weight_own[number, p]

    def forward(a, b):
        return compat[a, b]

    def backward(b, a):
        return compat[a, b]

    def lay_field(values, inner, sides):
        for label in range(LABELS):
            lay_out(inner, sides, LABELS, label, values[0][label], values[1][label])

    def send_field(number, reach, values, inner, sides, minus, plus):
        lay_field(values, inner, sides)
        return exchange(number, LABELS, reach, inner, sides, minus, plus)

    sums = message(own_weight, field_0, (0, 1), 0)
    values = []
    for p in (0, 1):
        message_1[:, p] = sums[p]
        values.append(normalise(own_logits(p) - mix(forward, sums[p])))
    sent_q = send_field(2, 2, values, inner_q, sides_q, minus_q, plus_q)
    meet(1)

    loads[2].wait()

    def keep_cotangent(label, p, value):
        own_grad[label, p] = value

    spread(cotangent_in, 4, keep_cotangent)
    arrive_narrow(sent_a, WIDE, 2, inner_a, minus_a, plus_a, box_a)
    for number in range(NEIGH):
        for y in (-2, 2):
            found = assemble(inner_a, minus_a, plus_a, WIDE, number, y, 2)
            for p in range(-2, 4):
                wide_aff[number, p + 2, pl.ds(BASE + y, 8), :] = found[p] * strength[number]
    rim_mask_y = {y: mask_y(y) for y in (-2, -1, 0, 1, 2)}

    def rim_weights(target, value):
        for y in (-1, 1):
            for p in (-1, 0, 1, 2):
                for number, (step_x, step_y, step_z) in enumerate(OFFSETS):
                    across = mask_x[p + step_x] * rim_mask_y[y + step_y]
                    if step_z != 0:
                        across = across * mask_z[step_z]
                    target[number, p + 1, pl.ds(BASE + y, 8), :] = across * value(number, p, y)

    def rim_value(number, p, y):
        return wide_aff[number, p + 2, pl.ds(BASE + y, 8), :]

    def back_value(number, p, y):
        step_x, step_y, step_z = OFFSETS[number]
        opposite = NUMBER[(-step_x, -step_y, -step_z)]
        value = wide_aff[opposite, p + step_x + 2, pl.ds(BASE + y + step_y, 8), :]
        if step_z != 0:
            value = pltpu.roll(value, (128 - step_z) % 128, 1)
        return value

    rim_weights(weight_rim, rim_value)

    arrive(sent_q)
    gather_field(field_1, inner_q, minus_q, plus_q, 2)
    for y in (-1, 1):

        def rim_weight(number, p, y=y):
            return weight_rim[number, p + 1, pl.ds(BASE + y, 8), :]

        sums = message(rim_weight, field_1, (-1, 0, 1, 2), y)
        for p in (-1, 0, 1, 2):
            message_2[:, p + 1, pl.ds(BASE + y, 8), :] = sums[p]
            here = logits[:, p + 2, pl.ds(BASE + y, 8), :]
            put_field(field_2, p, y, normalise(here - mix(forward, sums[p])))

    sums = message(own_weight, field_2, (0, 1), 0)
    grads = []
    values = []
    for p in (0, 1):
        current = normalise(own_logits(p) - mix(forward, sums[p]))
        step = softmax_back(current, own_grad[:, p])
        total_u[:, p] = step
        grads.append(-step)
        values.append(mix(backward, -step))
    lay_field(values, inner_g, sides_g)
    narrow(LABELS, 2, inner_g, sides_g, box_g)
    sent_g = start_narrow(3, 2, box_g)
    meet(2)

    def add_compat(grads, messages, begin):
        for b in range(LABELS):
            term = grads[0] * messages[0][b][None] + grads[1] * messages[1][b][None]
            total_c[b] = term if begin else total_c[b] + term

    def add_kernel(values, field, begin):
        for number, (step_x, step_y, step_z) in enumerate(OFFSETS):
            for p in (0, 1):
                near = field[step_z + 1, :, p + step_x + 2, pl.ds(BASE + step_y, 8), :]
                joint = jnp.sum(values[p] * near, axis=0)
                total_r[number, p] = joint if begin else total_r[number, p] + joint

    add_compat(grads, [sums[0], sums[1]], True)
    add_kernel(values, field_2, True)
    rim_weights(weight_back, back_value)

    arrive_narrow(sent_g, LABELS, 2, inner_g, minus_g, plus_g, box_g)
    meet(3)
    gather_field(field_g, inner_g, minus_g, plus_g, 2)

    def back_weight_at(y):
        def back_weight(number, p):
            return weight_back[number, p + 1, pl.ds(BASE + y, 8), :]

        return back_weight

    for y in (-1, 1):
        sums = message(back_weight_at(y), field_g, (-1, 0, 1, 2), y)
        for p in (-1, 0, 1, 2):
            current = field_2[1, :, p + 2, pl.ds(BASE + y, 8), :]
            grad_p = -softmax_back(current, sums[p])
            rim_p[:, p + 1, pl.ds(BASE + y, 8), :] = grad_p
            put_field(field_h, p, y, mix(backward, grad_p))

    sums = message(back_weight_at(0), field_h, (0, 1), 0)
    grads_1 = []
    values_1 = []
    for p in (0, 1):
        current = field_1[1, :, p + 2, pl.ds(BASE, 8), :]
        step = softmax_back(current, sums[p])
        total_u[:, p] = total_u[:, p] + step
        grads_1.append(-step)
        values_1.append(mix(backward, -step))
    grads_2 = [rim_p[:, p + 1, pl.ds(BASE, 8), :] for p in (0, 1)]
    for p in (0, 1):
        total_u[:, p] = total_u[:, p] - grads_2[p]
    add_compat(grads_2, [message_2[:, p + 1, pl.ds(BASE, 8), :] for p in (0, 1)], False)
    add_kernel([field_h[1, :, p + 2, pl.ds(BASE, 8), :] for p in (0, 1)], field_1, False)
    add_compat(grads_1, [message_1[:, p] for p in (0, 1)], False)
    add_kernel(values_1, field_0, False)

    local = jnp.zeros((8, 128), jnp.float32)
    for b in range(LABELS):
        total = jnp.sum(jnp.sum(total_c[b], axis=1), axis=1, keepdims=True)
        local = jnp.where(lane == 8 * b + sublane, total, local)
    joint_rows = []
    for number in range(NEIGH):
        row = None
        for p in (0, 1):
            term = total_r[number, p] * masked_own[number, p]
            row = term if row is None else row + term
        joint_rows.append(jnp.sum(row, axis=0, keepdims=True))
    for group in range(4):
        rows = joint_rows[8 * group : 8 * (group + 1)]
        rows = rows + [jnp.zeros((1, 128), jnp.float32)] * (8 - len(rows))
        total = jnp.sum(jnp.concatenate(rows, axis=0), axis=1, keepdims=True)
        local = jnp.where(lane == 8 * (LABELS + group) + sublane, total, local)

    gather_a[me_x] = jnp.sum(local, axis=0, keepdims=True)

    def to_peer(buffer, me, place_send, place_recv, device):
        return pltpu.make_async_remote_copy(
            src_ref=buffer.at[me],
            dst_ref=buffer.at[me],
            send_sem=peer_send.at[place_send],
            recv_sem=peer_recv.at[place_recv],
            device_id=device,
            device_id_type=MESH,
        )

    along_x = [to_peer(gather_a, me_x, step, 2 * step + core, odd[step]) for step in range(chips)]
    for step in sorted(range(1, chips), key=lambda step: -ring(step, chips)):
        along_x[step].start()

    @pl.when(core == 0)
    def _():
        along_x[0].start()

    sent_h = send_field(4, 1, values_1, inner_h, sides_h, minus_h, plus_h)

    def put_affinity(tile, x, value):
        affinity_out[x, :, 128 * tile : 128 * (tile + 1)] = value.astype(jnp.bfloat16)

    def own_affinity(number, p):
        step_x, step_y, step_z = OFFSETS[number]
        mask = mask_x[p + step_x] * mask_own_y[step_y] * mask_z[step_z]
        return total_r[number, p] * mask * strength[number]

    gather_columns(own_affinity, NEIGH // 2, put_affinity)
    store_a = pltpu.make_async_copy(affinity_out, grad_affinity_hbm, store_sem.at[0])
    store_a.start()

    meet(4)
    base = 2 * chips
    along_y = [
        to_peer(gather_b, me_y, base + place, base + place, device)
        for place, device in enumerate(peers_b)
    ]
    to_even = to_peer(last, 0, base + len(peers_b), base + len(peers_b), partner)

    @pl.when(core == 1)
    def _():
        for step in sorted(range(chips), key=lambda step: ring(step, chips)):
            for sender in (0, 1):
                if (step, sender) != (0, 1):
                    to_peer(gather_a, me_x, 0, 2 * step + sender, partner).wait_recv()
        total = gather_a[0]
        for place in range(1, size_gx):
            total = total + gather_a[place]
        gather_b[me_y] = total
        for copy in along_y:
            copy.start()

    arrive(sent_h)
    gather_field(field_i, inner_h, minus_h, plus_h, 1)
    sums = message(back_weight_at(0), field_i, (0, 1), 0)
    for p in (0, 1):
        current = field_0[1, :, p + 2, pl.ds(BASE, 8), :]
        total_u[:, p] = total_u[:, p] + softmax_back(current, sums[p])

    def put_unary(tile, x, value):
        unary_out[x, :, 128 * tile : 128 * (tile + 1)] = value.astype(jnp.bfloat16)

    gather_columns(lambda label, p: total_u[label, p], LABELS // 2, put_unary)
    store_u = pltpu.make_async_copy(unary_out, grad_unary_hbm, store_sem.at[1])
    store_u.start()

    for copy in sent_u + sent_a + sent_q + sent_g + sent_h + along_x[1:]:
        copy.wait_send()

    @pl.when(core == 0)
    def _():
        along_x[0].wait_send()

    @pl.when(core == 1)
    def _():
        for copy in along_y:
            copy.wait_send()
        arrive(along_y)
        total = gather_b[0]
        for place in range(1, size_gy):
            total = total + gather_b[place]
        last[0] = total
        to_even.start()

    @pl.when(core == 0)
    def _():
        to_even.wait_recv()

    voxels = size_gx * 4 * size_gy * 8 * DEPTH
    final = last[0] * (1.0 / math.sqrt(voxels))
    grad_kernel[...] = pltpu.roll(final, 128 - LABELS * LABELS, 1)[:, :NEIGH]
    spaced = jnp.where(lax.rem(lane, 8) == sublane, jnp.broadcast_to(final, (8, 128)), 0.0)
    table = jnp.zeros((8, 128), jnp.float32)
    for b in range(LABELS):
        column = jnp.sum(jnp.where(lane // 8 == b, spaced, 0.0), axis=1, keepdims=True)
        table = jnp.where(lane == b, column, table)
    grad_compat[...] = table[:, :LABELS]

    @pl.when(core == 1)
    def _():
        to_even.wait_send()

    store_a.wait()
    store_u.wait()


def doubling(size):
    steps, reach = [], 1
    while reach < size // 2:
        steps.append(reach)
        reach *= 2
    return steps


def hand_out(*refs):
    parts, results, held, sem = refs[:4], refs[4:8], refs[8:12], refs[12]
    inward = [
        pltpu.make_async_copy(part, hold, sem.at[0, number])
        for number, (part, hold) in enumerate(zip(parts, held))
    ]
    outward = [
        pltpu.make_async_copy(hold, result, sem.at[1, number])
        for number, (hold, result) in enumerate(zip(held, results))
    ]
    for copy in inward:
        copy.start()
    for came, copy in zip(inward, outward):
        came.wait()
        copy.start()
    for copy in outward:
        copy.wait()


def shards(sizes, unary_score, affinity, compatibility, kernel_weights, cotangent):
    size_gx, size_gy, size_far, size_near = sizes
    f32, bf16 = jnp.float32, jnp.bfloat16

    def rows(count, kind=f32):
        return pltpu.VMEM((count, 128), kind)

    def exchanged(width):
        return [
            rows(SPAN * 2 * width),
            rows(2 * 8 * width),
            rows(SPAN * width),
            rows(SPAN * width),
        ]

    def boxed(width, reach):
        return [
            rows(2 * reach * 2 * width, bf16),
            rows(2 * 8 * width, bf16),
            rows(2 * reach * 2 * width, bf16),
            rows(SPAN * width, bf16),
            rows(SPAN * width, bf16),
        ]

    field = pltpu.VMEM((3, LABELS, 6, TALL, 128), f32)
    pair = pltpu.VMEM((LABELS, 2, 8, 128), f32)
    rim = pltpu.VMEM((LABELS, 4, TALL, 128), f32)
    peers = size_gx + size_gy
    scratch = (
        [
            pltpu.VMEM(unary_score.shape, bf16),
            pltpu.VMEM(affinity.shape, bf16),
            pltpu.VMEM(cotangent.shape, bf16),
            pltpu.VMEM(unary_score.shape, bf16),
            pltpu.VMEM(affinity.shape, bf16),
            pltpu.SMEM(compatibility.shape, f32),
            pltpu.SMEM(kernel_weights.shape, f32),
        ]
        + exchanged(LABELS)
        + exchanged(WIDE)
        + boxed(LABELS, 1)
        + boxed(WIDE, 2)
        + boxed(LABELS, 2)
        + exchanged(LABELS)
        + exchanged(LABELS)
        + exchanged(LABELS)
        + [
            pltpu.VMEM((LABELS, 6, TALL, 128), f32),
            pair,
            field,
            field,
            field,
            field,
            field,
            field,
            pltpu.VMEM((NEIGH, 6, TALL, 128), f32),
            pltpu.VMEM((NEIGH, 2, 8, 128), f32),
            pltpu.VMEM((NEIGH, 2, 8, 128), f32),
            pltpu.VMEM((NEIGH, 4, TALL, 128), f32),
            pltpu.VMEM((NEIGH, 4, TALL, 128), f32),
            pair,
            rim,
            rim,
            pair,
            pltpu.VMEM((LABELS, LABELS, 8, 128), f32),
            pltpu.VMEM((NEIGH, 2, 8, 128), f32),
            pltpu.VMEM((size_gx, 1, 128), f32),
            pltpu.VMEM((size_gy, 1, 128), f32),
            pltpu.VMEM((1, 1, 128), f32),
            pltpu.SemaphoreType.DMA((5,)),
            pltpu.SemaphoreType.DMA((2,)),
            pltpu.SemaphoreType.DMA((5, 8)),
            pltpu.SemaphoreType.DMA((5, 8)),
            pltpu.SemaphoreType.DMA((peers,)),
            pltpu.SemaphoreType.DMA((peers,)),
            pltpu.SemaphoreType.REGULAR((2, 4)),
        ]
    )
    anywhere = pl.BlockSpec(memory_space=pl.ANY)
    in_hbm = pl.BlockSpec(memory_space=pltpu.HBM)
    vectors = pl.BlockSpec(memory_space=pltpu.VMEM)
    grad_unary, grad_affinity, grad_compat, grad_kernel = pl.pallas_call(
        functools.partial(kernel, sizes),
        out_shape=(
            jax.ShapeDtypeStruct(unary_score.shape, bf16),
            jax.ShapeDtypeStruct(affinity.shape, bf16),
            jax.ShapeDtypeStruct((LABELS, LABELS), f32),
            jax.ShapeDtypeStruct((1, NEIGH), f32),
        ),
        in_specs=[in_hbm] * 5,
        out_specs=(anywhere, anywhere, vectors, vectors),
        scratch_shapes=scratch,
        compiler_params=pltpu.CompilerParams(
            collective_id=0, has_side_effects=True, vmem_limit_bytes=GRANT
        ),
        name="mean_field_backward",
    )(unary_score, affinity, cotangent, compatibility, kernel_weights)
    found = (grad_unary, grad_affinity, grad_compat, grad_kernel.reshape(NEIGH))
    return pl.pallas_call(
        hand_out,
        out_shape=tuple(jax.ShapeDtypeStruct(part.shape, part.dtype) for part in found),
        in_specs=[anywhere] * 4,
        out_specs=(in_hbm,) * 4,
        scratch_shapes=[pltpu.VMEM(part.shape, part.dtype) for part in found]
        + [pltpu.SemaphoreType.DMA((2, 4))],
        compiler_params=pltpu.CompilerParams(vmem_limit_bytes=GRANT),
        name="hand_out",
    )(*found)


def solution(mesh):
    size_gx, size_gy = mesh.shape["gx"], mesh.shape["gy"]
    size_near = 4 if size_gy % 4 == 0 else 1
    sizes = (size_gx, size_gy, size_gy // size_near, size_near)
    in_specs = (P("gx", "gy", None), P("gx", "gy", None), P(), P(), P("gx", "gy", None))
    out_specs = (P("gx", "gy", None), P("gx", "gy", None), P(), P())
    return jax.shard_map(
        functools.partial(shards, sizes),
        mesh=mesh,
        in_specs=in_specs,
        out_specs=out_specs,
        check_vma=False,
    )
```
